32 devices in a mesh: dp: 4 (over z), expert: 8 (over y, x, core).
Axes of the slice: x: 2, y: 2, z: 4, core: 2. Of those that a mesh axis runs over, the one named last changes fastest.
Arguments:
- pivot_states: bfloat16 [4096, 2048], P(('dp', 'expert')), may hold values from -6 to 6
- queries: bfloat16 [4096, 2048], P(('dp', 'expert')), may hold values from -8 to 8
- keys: bfloat16 [4096, 2048], P(('dp', 'expert')), may hold values from -8 to 8
- values: bfloat16 [4096, 2048], P(('dp', 'expert')), may hold values from -6 to 6
- pack_pos: int32 [4096], P(('dp', 'expert')), may hold values from 0 to 511, as said below
- segment_ids: int32 [32, 128], P(('dp', 'expert')), may hold values from 0 to 7, never falling along the last dimension, each value on 1 to 64 neighbouring positions
- expert_ids: int32 [4096, 2], P(('dp', 'expert')), may hold values from 0 to 31, all different within a row
- gate_code: int32 [4096, 2], P(('dp', 'expert')), may hold values from 6554 to 65535
- ln_gain: float32 [2048], replicated, may hold values from 0.5 to 1.5
- ln_bias: float32 [2048], replicated, may hold values from -3 to 3
- w_in: bfloat16 [8, 2048, 4096], P('expert', None, 'dp'), may hold values from -0.125 to 0.125
- b_in: float32 [8, 4096], P('expert', 'dp'), may hold values from -3 to 3
- w_out: bfloat16 [8, 4096, 2048], P('expert', 'dp'), may hold values from -0.09375 to 0.09375
- b_out: float32 [8, 2048], replicated, may hold values from -3 to 3
Outputs:
- layer_out: bfloat16 [4096, 2048], P(('dp', 'expert'))
The draws below stay inside these ranges and needn't reach their ends.
Inputs may be any that keep to these rules, and one draw needn't show every extreme that they name: Within one index of expert, pack_pos over the devices of dp is a permutation, and each device's tokens go exactly 32 to each packed block of its column. `expert_ids`: only ids below 8 belong to the experts of this round.
All inputs are finite; a program needn't handle non-finite values.
Results may differ from the reference program's by a relative error of at most 0.0055.
Values may be sent and summed in bfloat16 or wider, within the bound.
No kernel may reach another device: no remote copies, remote signals or barrier semaphores. Data moves between devices by JAX's collectives and lax.ppermute only.
A program may use at most 64 MiB of HBM per device.

```python
import math
import jax
import jax.numpy as jnp
import numpy as np
from jax import lax

D = 2048
HEAD_DIM = 128
FF = 4096
TOK_DEV = 128
EXPERTS = 8
EXPERTS_ALL = 32
CAP = 8
BLOCKS = 32
TOKENS = 4096
N_DP = 4
N_EXPERT = 8


def drawn_rows(key, offset_tag):
    gaussian = jax.random.normal(jax.random.fold_in(key, offset_tag), (TOKENS, D), jnp.float32)
    return jnp.clip(gaussian, -6.0, 6.0)


def draw_queries(key, part):
    return drawn_rows(key, 3).astype(jnp.bfloat16)


def draw_keys(key, part):
    return drawn_rows(key, 5).astype(jnp.bfloat16)


def draw_pack_pos(key, part):
    per_target = TOK_DEV // N_DP
    first_key = jax.random.fold_in(key, 101)
    second_key = jax.random.fold_in(key, 202)
    target_keys = jax.random.split(first_key, N_EXPERT * N_DP)
    target_perm = jax.vmap(lambda subkey: jax.random.permutation(subkey, TOK_DEV))(target_keys)
    target_perm = target_perm.reshape(N_EXPERT, N_DP, TOK_DEV)
    source_keys = jax.random.split(second_key, N_DP * N_EXPERT)
    send_order = jax.vmap(lambda subkey: jax.random.permutation(subkey, TOK_DEV))(source_keys)
    send_order = send_order.reshape(N_DP, N_EXPERT, TOK_DEV)
    target_block = send_order // per_target
    within_share = send_order % per_target
    source_row = jnp.arange(N_DP, dtype=jnp.int32)[:, None, None]
    column_row = jnp.arange(N_EXPERT, dtype=jnp.int32)[None, :, None]
    offsets = target_perm[column_row, target_block, source_row * per_target + within_share]
    return (target_block * TOK_DEV + offsets).astype(jnp.int32).reshape(TOKENS)


def place_ends(values, key, smallest, largest):
    spot = [jax.random.randint(jax.random.fold_in(key, axis), (), 0, length) for axis, length in enumerate(values.shape)]
    widest = values.shape.index(max(values.shape))
    beside = spot[:widest] + [(spot[widest] + 1) % values.shape[widest]] + spot[widest + 1:]
    return values.at[tuple(spot)].set(smallest).at[tuple(beside)].set(largest)


def block_scale(own_key, shape, cuts, least, top_value):
    factor_of = 1.0
    for position, shards_of in cuts:
        steps = jax.random.uniform(jax.random.fold_in(jax.random.fold_in(own_key, 6), position), (shards_of,), jnp.float32, least / len(cuts), top_value / len(cuts))
        factor_of = factor_of * jnp.repeat(jnp.exp(steps), shape[position] // shards_of).reshape((-1,) + (1,) * (len(shape) - 1 - position))
    return factor_of


def different_ones(key, rows, amount, top, lift):
    order = jax.random.permutation(jax.random.fold_in(key, 1), amount)
    boost = order
    for power in range(3):
        boost = boost * boost // amount
    boost = boost * lift // amount
    chance = jax.random.randint(jax.random.fold_in(key, 2), (rows, amount), 0, 4096) + boost
    fixed_rows = jax.random.permutation(jax.random.fold_in(key, 3), rows)[jnp.arange(amount) % rows]
    chance = jnp.where(jnp.arange(rows)[:, None] == fixed_rows[None, :], 1 << 14, chance)
    merit = chance * amount + jnp.arange(amount)
    return lax.top_k(merit.astype(jnp.int32), top)[1].astype(jnp.int32)


def length_profile(number_of, total, bound, skew):
    loads = [(1 << 20) // math.isqrt(grade ** skew) + 1 for grade in range(2, number_of + 1)]
    surplus, holding = total - bound - (number_of - 1), [1] * (number_of - 1)
    while surplus > 0:
        candidates = [i for i in range(number_of - 1) if holding[i] < bound]
        pool, remaining = sum([loads[i] for i in candidates]), surplus
        for i in candidates:
            more = min(bound - holding[i], max(1, remaining * loads[i] // pool), surplus)
            holding[i] = holding[i] + more
            surplus = surplus - more
    return np.array([bound] + holding)


def uneven(key, count, total, most, skew):
    if count == 2:
        one = jax.random.randint(key, (), max(1, total - most), min(most, total - 1) + 1)
        return jnp.stack([one, total - one])
    tallies = jnp.asarray(length_profile(count, total, most, skew), jnp.int32)
    couples = (count - 1) // 2
    giver, receiver = tallies[1:1 + 2 * couples:2], tallies[2:2 + 2 * couples:2]
    room = jnp.minimum(giver - 1, most - receiver)
    passed = jax.random.randint(jax.random.fold_in(key, 1), (couples,), 0, 1 << 20) % (room + 1)
    tallies = tallies.at[1:1 + 2 * couples:2].set(giver - passed).at[2:2 + 2 * couples:2].set(receiver + passed)
    return tallies[jax.random.permutation(jax.random.fold_in(key, 2), count)]


def centred(stream_key, dims, spread, reach, shards=(), kind=jnp.bfloat16):
    values = spread * jax.random.normal(stream_key, dims, jnp.float32)
    if shards:
        values = values * block_scale(stream_key, dims, shards, -0.22, 0.18)
    return jnp.clip(values, -reach, reach).astype(kind)


def setup_inputs(seed: int = 0) -> dict:
    key_list = jax.random.split(jax.random.key(seed), 15)
    return {
        "pivot_states": centred(key_list[0], (TOKENS, D), 1.0, 6.0, ((0, 32),)),
        "queries": draw_queries(jax.random.fold_in(key_list[14], 71), 0),
        "keys": draw_keys(jax.random.fold_in(key_list[14], 71), 0),
        "values": centred(key_list[3], (TOKENS, D), 1.0, 6.0, ((0, 32),)),
        "pack_pos": draw_pack_pos(jax.random.fold_in(key_list[14], 71), 0),
        "segment_ids": jax.vmap(lambda own: jnp.searchsorted(jnp.cumsum(uneven(own, TOK_DEV // 16, TOK_DEV, TOK_DEV // 2, 2)), jnp.arange(TOK_DEV), side="right"))(jax.random.split(key_list[5], BLOCKS)).reshape((BLOCKS, TOK_DEV)).astype(jnp.int32),
        "expert_ids": different_ones(key_list[6], TOKENS, EXPERTS_ALL, 2, 1024),
        "gate_code": place_ends(jax.random.randint(key_list[7], (TOKENS, 2), 6554, 65536), jax.random.fold_in(key_list[7], 1), 6554, 65535).astype(jnp.int32),
        "ln_gain": jnp.clip(1.0 + 0.1 * jax.random.normal(key_list[8], (D,), jnp.float32), 0.5, 1.5),
        "ln_bias": centred(key_list[9], (D,), 0.5, 3.0, (), jnp.float32),
        "w_in": centred(key_list[10], (EXPERTS, D, FF), D ** -0.5, 0.125, ((0, 8), (2, 4))),
        "b_in": centred(key_list[11], (EXPERTS, FF), 0.5, 3.0, ((0, 8), (1, 4)), jnp.float32),
        "w_out": centred(key_list[12], (EXPERTS, FF, D), FF ** -0.5, 0.09375, ((0, 8), (1, 4))),
        "b_out": centred(key_list[13], (EXPERTS, D), 0.5, 3.0, (), jnp.float32),
    }


epsilon = 1e-05
mask_fill = -1e+30

def attend_block(block_args):
    query_rows, key_rows, value_rows, seg_row = block_args
    row_count = query_rows.shape[0]
    head_count = query_rows.shape[1] // HEAD_DIM
    query_heads = query_rows.astype(jnp.float32).reshape(row_count, head_count, HEAD_DIM)
    key_heads = key_rows.astype(jnp.float32).reshape(row_count, head_count, HEAD_DIM)
    value_heads = value_rows.astype(jnp.float32).reshape(row_count, head_count, HEAD_DIM)
    scores = jnp.einsum('qhd,khd->hqk', query_heads, key_heads) * (1.0 / math.sqrt(HEAD_DIM))
    same_doc = seg_row[:, None] == seg_row[None, :]
    scores = jnp.where(same_doc[None, :, :], scores, mask_fill)
    top_score = lax.optimization_barrier(jnp.max(scores, axis=2, keepdims=True))
    exp_terms = jnp.exp(scores - top_score)
    softmax_weights = (exp_terms / lax.optimization_barrier(jnp.sum(exp_terms, axis=2, keepdims=True))).astype(jnp.bfloat16)
    attended = jnp.einsum('hqk,khd->qhd', softmax_weights.astype(jnp.float32), value_heads)
    return attended.reshape(row_count, head_count * HEAD_DIM)

def expert_apply(expert_args):
    rows_in, first_matrix, bias_in, second_matrix, bias_out = expert_args
    hidden_units = first_matrix.shape[1] // N_DP
    running_total = jnp.zeros((rows_in.shape[0], second_matrix.shape[1]), jnp.float32)
    for slice_index in range(N_DP):
        lower_edge = slice_index * hidden_units
        hidden = jnp.dot(rows_in, first_matrix[:, lower_edge:lower_edge + hidden_units], preferred_element_type=jnp.float32)
        hidden = jnp.maximum(hidden + bias_in[lower_edge:lower_edge + hidden_units], 0.0).astype(jnp.bfloat16)
        partial_share = jnp.dot(hidden, second_matrix[lower_edge:lower_edge + hidden_units], preferred_element_type=jnp.float32).astype(jnp.bfloat16)
        partial_share = lax.optimization_barrier(partial_share)
        running_total = running_total + partial_share.astype(jnp.float32)
    return (running_total + bias_out).astype(jnp.bfloat16)

def reference(pivot_states, queries, keys, values, pack_pos, segment_ids, expert_ids, gate_code, ln_gain, ln_bias, w_in, b_in, w_out, b_out):
    tokens_all = pivot_states.shape[0]
    model_width = pivot_states.shape[1]
    blocks_all = tokens_all // TOK_DEV
    source_index = jnp.arange(tokens_all, dtype=jnp.int32)
    column_index = source_index // TOK_DEV % N_EXPERT
    destination = (pack_pos // TOK_DEV * N_EXPERT + column_index) * TOK_DEV + pack_pos % TOK_DEV

    def regroup(array):
        return jnp.zeros_like(array).at[destination].set(array)
    states_packed = regroup(pivot_states)
    attended = lax.map(attend_block, (regroup(queries).reshape(blocks_all, TOK_DEV, model_width), regroup(keys).reshape(blocks_all, TOK_DEV, model_width), regroup(values).reshape(blocks_all, TOK_DEV, model_width), segment_ids))
    hidden_state = states_packed.astype(jnp.float32) + attended.reshape(tokens_all, model_width)
    mean_value = lax.optimization_barrier(jnp.mean(hidden_state, axis=1, keepdims=True))
    centered = hidden_state - mean_value
    variance = lax.optimization_barrier(jnp.mean(centered * centered, axis=1, keepdims=True))
    normed = (centered * lax.rsqrt(variance + epsilon) * ln_gain + ln_bias).astype(jnp.bfloat16)
    experts_round = N_EXPERT
    choice_ids = expert_ids.reshape(blocks_all, TOK_DEV, 2)
    assigned = jnp.concatenate([choice_ids[:, :, 0], choice_ids[:, :, 1]], axis=1)
    expert_hot = (assigned[:, :, None] == jnp.arange(experts_round, dtype=jnp.int32)[None, None, :]).astype(jnp.int32)
    slot_rank = lax.optimization_barrier(jnp.sum(jnp.cumsum(expert_hot, axis=1) * expert_hot, axis=2)) - 1
    kept_mask = (assigned < experts_round) & (slot_rank < CAP)
    block_index = jnp.arange(blocks_all, dtype=jnp.int32)[:, None]
    overflow = experts_round * blocks_all * CAP
    slot_index = jnp.where(kept_mask, (assigned * blocks_all + block_index) * CAP + slot_rank, overflow).astype(jnp.int32)
    slot_first = slot_index[:, :TOK_DEV].reshape(tokens_all)
    slot_second = slot_index[:, TOK_DEV:].reshape(tokens_all)
    buffer = jnp.zeros((overflow, model_width), jnp.bfloat16)
    buffer = buffer.at[slot_first].set(normed, mode='drop').at[slot_second].set(normed, mode='drop')
    results = lax.map(expert_apply, (buffer.reshape(experts_round, blocks_all * CAP, model_width), w_in, b_in, w_out, b_out))
    results = results.reshape(overflow, model_width)
    gate_values = gate_code.astype(jnp.float32) / 65536.0
    weight_first = jnp.where(kept_mask[:, :TOK_DEV].reshape(tokens_all), gate_values[:, 0], 0.0)
    weight_second = jnp.where(kept_mask[:, TOK_DEV:].reshape(tokens_all), gate_values[:, 1], 0.0)
    picked_first = results[jnp.minimum(slot_first, overflow - 1)].astype(jnp.float32)
    picked_second = results[jnp.minimum(slot_second, overflow - 1)].astype(jnp.float32)
    layer_out = hidden_state + weight_first[:, None] * picked_first + weight_second[:, None] * picked_second
    return layer_out.astype(jnp.bfloat16)
```

```python
import functools
import math

import jax
import jax.numpy as jnp
from jax import lax
from jax.experimental import pallas as pl
from jax.experimental.pallas import tpu as pltpu
from jax.sharding import PartitionSpec as P

HEAD_DIM = 128
ROUNDS = 4
LANES = 128

epsilon = 1e-05
mask_fill = -1e30

F32 = jnp.float32
BF16 = jnp.bfloat16

VMEM_BYTES = 32 * 1024 * 1024


def iota(shape, axis):
    return lax.broadcasted_iota(jnp.int32, shape, axis)


def one_hot(condition):
    return jnp.where(condition, 1.0, 0.0)


def across(row, rows):
    lanes = jnp.broadcast_to(row.astype(F32), (rows, row.shape[1]))
    return lanes, lanes.T


def call(body, out_shape, *operands, flops=0):
    moved = sum(x.size * x.dtype.itemsize for x in operands)
    moved += sum(x.size * x.dtype.itemsize for x in jax.tree.leaves(out_shape))
    return pl.pallas_call(
        body,
        out_shape=out_shape,
        compiler_params=pltpu.CompilerParams(vmem_limit_bytes=VMEM_BYTES),
        cost_estimate=pl.CostEstimate(flops=flops, bytes_accessed=moved, transcendentals=0),
    )(*operands)


def pack_kernel(pos_ref, *refs):
    x_refs, out_ref = refs[:-1], refs[-1]
    tok = pos_ref.shape[1]
    lanes, subl = across(pos_ref[...], tok)
    _, offset = across(lax.rem(pos_ref[...], tok), tok)
    rank = jnp.sum(one_hot(subl < lanes), axis=0, keepdims=True)
    order = one_hot(iota((tok, tok), 0).astype(F32) == rank).astype(BF16)
    at = 0
    for x in [r[...] for r in x_refs] + [offset.astype(BF16)]:
        out_ref[:, at : at + x.shape[1]] = jnp.dot(order, x, preferred_element_type=F32).astype(BF16)
        at += x.shape[1]


def slots_of(ids_ref, cap, experts):
    tok = ids_ref.shape[1]
    first, first_t = across(ids_ref[0:1, :], tok)
    second, second_t = across(ids_ref[1:2, :], tok)
    earlier = iota((tok, tok), 0) < iota((tok, tok), 1)
    rank_first = jnp.sum(one_hot((first_t == first) & earlier), axis=0, keepdims=True)
    rank_second = jnp.sum(one_hot(first_t == second), axis=0, keepdims=True)
    rank_second += jnp.sum(one_hot((second_t == second) & earlier), axis=0, keepdims=True)

    def slot(expert, rank):
        return jnp.where((expert < experts) & (rank < cap), expert * cap + rank, -1.0)

    return slot(first[0:1, :], rank_first), slot(second[0:1, :], rank_second)


def attend_kernel(cap, experts, copies, rows_ref, seg_ref, ids_ref, gain_ref, bias_ref, hidden_ref, send_ref):
    tok, width = hidden_ref.shape
    _, seg_q = across(seg_ref[...], tok)
    offset_of_key = rows_ref[:, 4 * width :].astype(F32).T
    place = offset_of_key == iota((tok, tok), 0).astype(F32)
    seg_k = jnp.sum(jnp.where(place, seg_q, 0.0), axis=0, keepdims=True)
    same = seg_q == seg_k
    place = one_hot(place).astype(BF16)
    scale = 1.0 / math.sqrt(HEAD_DIM)
    for h in range(width // HEAD_DIM):
        lo = h * HEAD_DIM
        q = rows_ref[:, width + lo : width + lo + HEAD_DIM]
        k = rows_ref[:, 2 * width + lo : 2 * width + lo + HEAD_DIM]
        v = rows_ref[:, 3 * width + lo : 3 * width + lo + HEAD_DIM]
        s = rows_ref[:, lo : lo + HEAD_DIM]
        q = jnp.dot(place, q, preferred_element_type=F32).astype(BF16)
        scores = lax.dot_general(q, k, (((1,), (1,)), ((), ())), preferred_element_type=F32) * scale
        scores = jnp.where(same, scores, mask_fill)
        terms = jnp.exp(scores - jnp.max(scores, axis=1, keepdims=True))
        probs = (terms / jnp.sum(terms, axis=1, keepdims=True)).astype(BF16)
        mixed = jnp.dot(probs, v, preferred_element_type=F32)
        hidden_ref[:, lo : lo + HEAD_DIM] = mixed + jnp.dot(place, s, preferred_element_type=F32)
    hidden = hidden_ref[...]
    centered = hidden - jnp.mean(hidden, axis=1, keepdims=True)
    variance = jnp.mean(centered * centered, axis=1, keepdims=True)
    normed = (centered * lax.rsqrt(variance + epsilon) * gain_ref[...] + bias_ref[...]).astype(BF16)
    slot_first, slot_second = slots_of(ids_ref, cap, experts)
    slot = iota((experts * cap, tok), 0).astype(F32)
    taken = one_hot((slot == slot_first) | (slot == slot_second)).astype(BF16)
    picked = jnp.dot(taken, normed, preferred_element_type=F32).astype(BF16)
    for n in range(copies):
        send_ref[n] = picked


def combine_kernel(cap, experts, parts_ref, hidden_ref, ids_ref, code_ref, bias_ref, out_ref):
    tok = out_ref.shape[0]
    total = parts_ref[0].astype(F32)
    for n in range(1, parts_ref.shape[0]):
        total += parts_ref[n].astype(F32)
    result = (total + bias_ref[...]).astype(BF16)
    slot_first, slot_second = slots_of(ids_ref, cap, experts)
    slot = iota((experts * cap, tok), 0).astype(F32)
    high = (code_ref[...] >> 8).astype(F32)
    low = (code_ref[...] & 255).astype(F32)

    def weights(code):
        return jnp.where(slot == slot_first, code[0:1, :], 0.0) + jnp.where(
            slot == slot_second, code[1:2, :], 0.0
        )

    both = jnp.concatenate([weights(high) / 256.0, weights(low) / 65536.0], axis=0)
    result = jnp.concatenate([result, result], axis=0)
    added = jnp.dot(both.T.astype(BF16), result, preferred_element_type=F32)
    out_ref[...] = (hidden_ref[...] + added).astype(BF16)


def per_device(
    pivot_states,
    queries,
    keys,
    values,
    pack_pos,
    segment_ids,
    expert_ids,
    gate_code,
    ln_gain,
    ln_bias,
    w_in,
    b_in,
    w_out,
    b_out,
):
    tok, width = pivot_states.shape
    dp = lax.axis_size("dp")
    experts = lax.axis_size("expert")
    cap = max(2, 2 * tok // (ROUNDS * experts))
    slots = experts * cap
    ids = expert_ids.T
    codes = gate_code.T
    wide = 4 * width + LANES
    rows = call(
        pack_kernel,
        jax.ShapeDtypeStruct((tok, wide), BF16),
        pack_pos.reshape(1, tok),
        pivot_states,
        queries,
        keys,
        values,
    )
    rows = lax.all_to_all(
        rows.reshape(dp, tok // dp, wide), "dp", split_axis=0, concat_axis=0, tiled=True
    ).reshape(tok, wide)
    hidden_state, send = call(
        functools.partial(attend_kernel, cap, experts, dp),
        (
            jax.ShapeDtypeStruct((tok, width), F32),
            jax.ShapeDtypeStruct((dp, slots, width), BF16),
        ),
        rows,
        segment_ids,
        ids,
        ln_gain.reshape(1, width),
        ln_bias.reshape(1, width),
    )
    arrived = lax.all_to_all(
        send.reshape(dp * experts, cap, width), ("dp", "expert"), split_axis=0, concat_axis=0, tiled=True
    ).reshape(dp * slots, width)
    inner = jnp.dot(arrived, w_in[0], preferred_element_type=F32)
    inner = jnp.maximum(inner + b_in[0], 0.0).astype(BF16)
    share = jnp.dot(inner, w_out[0], preferred_element_type=F32).astype(BF16)
    parts = lax.all_to_all(
        share.reshape(dp * experts, cap, width), ("dp", "expert"), split_axis=0, concat_axis=0, tiled=True
    ).reshape(dp, slots, width)
    return call(
        functools.partial(combine_kernel, cap, experts),
        jax.ShapeDtypeStruct((tok, width), BF16),
        parts,
        hidden_state,
        ids,
        codes,
        jnp.repeat(b_out, cap, axis=0),
    )


def solution(mesh):
    return jax.shard_map(
        per_device,
        mesh=mesh,
        in_specs=(
            P(("dp", "expert"), None),
            P(("dp", "expert"), None),
            P(("dp", "expert"), None),
            P(("dp", "expert"), None),
            P(("dp", "expert")),
            P(("dp", "expert"), None),
            P(("dp", "expert"), None),
            P(("dp", "expert"), None),
            P(),
            P(),
            P("expert", None, "dp"),
            P("expert", "dp"),
            P("expert", "dp", None),
            P(),
        ),
        out_specs=P(("dp", "expert"), None),
        check_vma=False,
    )
```

```python
import functools
import math

import jax
import jax.numpy as jnp
from jax import lax
from jax.experimental import pallas as pl
from jax.experimental.pallas import tpu as pltpu
from jax.sharding import PartitionSpec as P

HEAD_DIM = 128
ROUNDS = 4
LANES = 128

epsilon = 1e-05
mask_fill = -1e30

F32 = jnp.float32
BF16 = jnp.bfloat16

VMEM_BYTES = 32 * 1024 * 1024


def iota(shape, axis):
    return lax.broadcasted_iota(jnp.int32, shape, axis)


def one_hot(condition):
    return jnp.where(condition, 1.0, 0.0)


def across(row, rows):
    lanes = jnp.broadcast_to(row.astype(F32), (rows, row.shape[1]))
    return lanes, lanes.T


def call(body, out_shape, *operands, flops=0):
    moved = sum(x.size * x.dtype.itemsize for x in operands)
    moved += sum(x.size * x.dtype.itemsize for x in jax.tree.leaves(out_shape))
    return pl.pallas_call(
        body,
        out_shape=out_shape,
        compiler_params=pltpu.CompilerParams(vmem_limit_bytes=VMEM_BYTES),
        cost_estimate=pl.CostEstimate(flops=flops, bytes_accessed=moved, transcendentals=0),
    )(*operands)


def pack_kernel(offsets, pos_ref, x_ref, *out_refs):
    tok, width = x_ref.shape
    share = tok // len(out_refs)
    lanes, subl = across(pos_ref[...], tok)
    rank = jnp.sum(one_hot(subl < lanes), axis=0, keepdims=True)
    order = one_hot(iota((tok, tok), 0).astype(F32) == rank).astype(BF16)
    rows = jnp.dot(order, x_ref[...], preferred_element_type=F32).astype(BF16)
    for n, out_ref in enumerate(out_refs):
        out_ref[:, :width] = rows[n * share : (n + 1) * share]
    if offsets:
        _, offset = across(lax.rem(pos_ref[...], tok), tok)
        rows = jnp.dot(order, offset.astype(BF16), preferred_element_type=F32).astype(BF16)
        for n, out_ref in enumerate(out_refs):
            out_ref[:, width:] = rows[n * share : (n + 1) * share]


def joined(refs, columns=slice(None)):
    return jnp.concatenate([r[:, columns] for r in refs], axis=0)


def slots_of(ids_ref, cap, experts):
    tok = ids_ref.shape[1]
    first, first_t = across(ids_ref[0:1, :], tok)
    second, second_t = across(ids_ref[1:2, :], tok)
    earlier = iota((tok, tok), 0) < iota((tok, tok), 1)
    rank_first = jnp.sum(one_hot((first_t == first) & earlier), axis=0, keepdims=True)
    rank_second = jnp.sum(one_hot(first_t == second), axis=0, keepdims=True)
    rank_second += jnp.sum(one_hot((second_t == second) & earlier), axis=0, keepdims=True)

    def slot(expert, rank):
        return jnp.where((expert < experts) & (rank < cap), expert * cap + rank, -1.0)

    return slot(first[0:1, :], rank_first), slot(second[0:1, :], rank_second)


def route_kernel(cap, experts, width, seg_ref, ids_ref, code_ref, *refs):
    *key_refs, place_ref, outside_ref, taken_ref, give_ref = refs
    tok = seg_ref.shape[1]
    _, seg_q = across(seg_ref[...], tok)
    place = joined(key_refs, slice(width, width + LANES)).astype(F32).T == iota((tok, tok), 0).astype(F32)
    place_ref[...] = one_hot(place).astype(BF16)
    seg_k = jnp.sum(jnp.where(place, seg_q, 0.0), axis=0, keepdims=True)
    outside_ref[...] = one_hot(seg_q != seg_k)
    slot_first, slot_second = slots_of(ids_ref, cap, experts)
    slot = iota((experts * cap, tok), 0).astype(F32)
    taken_ref[...] = one_hot((slot == slot_first) | (slot == slot_second)).astype(BF16)
    high = (code_ref[...] >> 8).astype(F32)
    low = (code_ref[...] & 255).astype(F32)

    def weights(code):
        return jnp.where(slot == slot_first, code[0:1, :], 0.0) + jnp.where(
            slot == slot_second, code[1:2, :], 0.0
        )

    both = jnp.concatenate([weights(high) / 256.0, weights(low) / 65536.0], axis=0)
    give_ref[...] = both.T.astype(BF16)


def probs_kernel(place_ref, outside_ref, *refs):
    *row_refs, out_ref = refs
    key_refs, query_refs = row_refs[: len(row_refs) // 2], row_refs[len(row_refs) // 2 :]
    scale = 1.0 / math.sqrt(HEAD_DIM)
    outside = outside_ref[...] > 0.0
    for h in range(out_ref.shape[0]):
        columns = slice(h * HEAD_DIM, (h + 1) * HEAD_DIM)
        q = jnp.dot(place_ref[...], joined(query_refs, columns), preferred_element_type=F32).astype(BF16)
        scores = lax.dot_general(
            q, joined(key_refs, columns), (((1,), (1,)), ((), ())), preferred_element_type=F32
        )
        scores = jnp.where(outside, mask_fill, scores * scale)
        terms = jnp.exp(scores - jnp.max(scores, axis=1, keepdims=True))
        out_ref[h] = (terms / jnp.sum(terms, axis=1, keepdims=True)).astype(BF16)


def mix_kernel(probs_ref, *refs):
    *value_refs, out_ref = refs
    for h in range(probs_ref.shape[0]):
        columns = slice(h * HEAD_DIM, (h + 1) * HEAD_DIM)
        out_ref[:, columns] = jnp.dot(
            probs_ref[h], joined(value_refs, columns), preferred_element_type=F32
        )


def norm_kernel(copies, place_ref, taken_ref, gain_ref, bias_ref, mixed_ref, *refs):
    *state_refs, hidden_ref, send_ref = refs
    hidden = mixed_ref[...] + jnp.dot(place_ref[...], joined(state_refs), preferred_element_type=F32)
    hidden_ref[...] = hidden
    centered = hidden - jnp.mean(hidden, axis=1, keepdims=True)
    variance = jnp.mean(centered * centered, axis=1, keepdims=True)
    normed = (centered * lax.rsqrt(variance + epsilon) * gain_ref[...] + bias_ref[...]).astype(BF16)
    picked = jnp.dot(taken_ref[...], normed, preferred_element_type=F32).astype(BF16)
    for n in range(copies):
        send_ref[n] = picked


def expert_kernel(x_ref, bias_ref, w_in_ref, w_out_ref, out_ref):
    inner = jnp.dot(x_ref[...], w_in_ref[0], preferred_element_type=F32)
    inner = jnp.maximum(inner + bias_ref[...], 0.0).astype(BF16)
    out_ref[...] = jnp.dot(inner, w_out_ref[0], preferred_element_type=F32).astype(BF16)


def combine_kernel(cap, parts_ref, hidden_ref, give_ref, bias_ref, out_ref):
    total = parts_ref[0].astype(F32)
    for n in range(1, parts_ref.shape[0]):
        total += parts_ref[n].astype(F32)
    bias = jnp.concatenate(
        [jnp.broadcast_to(bias_ref[e : e + 1, :], (cap, bias_ref.shape[1])) for e in range(bias_ref.shape[0])],
        axis=0,
    )
    result = (total + bias).astype(BF16)
    result = jnp.concatenate([result, result], axis=0)
    added = jnp.dot(give_ref[...], result, preferred_element_type=F32)
    out_ref[...] = (hidden_ref[...] + added).astype(BF16)


def per_device(
    pivot_states,
    queries,
    keys,
    values,
    pack_pos,
    segment_ids,
    expert_ids,
    gate_code,
    ln_gain,
    ln_bias,
    w_in,
    b_in,
    w_out,
    b_out,
):
    tok, width = pivot_states.shape
    dp = lax.axis_size("dp")
    experts = lax.axis_size("expert")
    cap = max(2, 2 * tok // (ROUNDS * experts))
    slots = experts * cap
    heads = width // HEAD_DIM
    position = lax.rem(pack_pos + (dp - lax.axis_index("dp")) * tok, dp * tok).reshape(1, tok)

    def exchange(rows, offsets):
        wide = width + (LANES if offsets else 0)
        parts = call(
            functools.partial(pack_kernel, offsets),
            (jax.ShapeDtypeStruct((tok // dp, wide), BF16),) * dp,
            position,
            rows,
        )
        return [
            part if n == 0 else lax.ppermute(part, "dp", [(i, (i + n) % dp) for i in range(dp)])
            for n, part in enumerate(parts)
        ]

    key_rows = exchange(keys, True)
    query_rows = exchange(queries, False)
    value_rows = exchange(values, False)
    state_rows = exchange(pivot_states, False)
    place, outside, taken, give = call(
        functools.partial(route_kernel, cap, experts, width),
        (
            jax.ShapeDtypeStruct((tok, tok), BF16),
            jax.ShapeDtypeStruct((tok, tok), F32),
            jax.ShapeDtypeStruct((slots, tok), BF16),
            jax.ShapeDtypeStruct((tok, 2 * slots), BF16),
        ),
        segment_ids,
        expert_ids.T,
        gate_code.T,
        *key_rows,
    )
    probs = call(
        probs_kernel,
        jax.ShapeDtypeStruct((heads, tok, tok), BF16),
        place,
        outside,
        *key_rows,
        *query_rows,
    )
    mixed = call(mix_kernel, jax.ShapeDtypeStruct((tok, width), F32), probs, *value_rows)
    hidden_state, send = call(
        functools.partial(norm_kernel, dp),
        (
            jax.ShapeDtypeStruct((tok, width), F32),
            jax.ShapeDtypeStruct((dp, slots, width), BF16),
        ),
        place,
        taken,
        ln_gain.reshape(1, width),
        ln_bias.reshape(1, width),
        mixed,
        *state_rows,
    )

    def over_all(x):
        x = x.reshape(dp * experts, cap, width)
        return lax.all_to_all(x, ("dp", "expert"), split_axis=0, concat_axis=0, tiled=True)

    share = call(
        expert_kernel,
        jax.ShapeDtypeStruct((dp * slots, width), BF16),
        over_all(send).reshape(dp * slots, width),
        b_in,
        w_in,
        w_out,
    )
    return call(
        functools.partial(combine_kernel, cap),
        jax.ShapeDtypeStruct((tok, width), BF16),
        over_all(share).reshape(dp, slots, width),
        hidden_state,
        give,
        b_out,
    )


def solution(mesh):
    return jax.shard_map(
        per_device,
        mesh=mesh,
        in_specs=(
            P(("dp", "expert"), None),
            P(("dp", "expert"), None),
            P(("dp", "expert"), None),
            P(("dp", "expert"), None),
            P(("dp", "expert")),
            P(("dp", "expert"), None),
            P(("dp", "expert"), None),
            P(("dp", "expert"), None),
            P(),
            P(),
            P("expert", None, "dp"),
            P("expert", "dp"),
            P("expert", "dp", None),
            P(),
        ),
        out_specs=P(("dp", "expert"), None),
        check_vma=False,
    )
```

```python
import functools
import math

import jax
import jax.numpy as jnp
from jax import lax
from jax.experimental import pallas as pl
from jax.experimental.pallas import tpu as pltpu
from jax.sharding import PartitionSpec as P

HEAD_DIM = 128
ROUNDS = 4
LANES = 128

epsilon = 1e-05
mask_fill = -1e30

F32 = jnp.float32
BF16 = jnp.bfloat16

VMEM_BYTES = 32 * 1024 * 1024


def iota(shape, axis):
    return lax.broadcasted_iota(jnp.int32, shape, axis)


def one_hot(condition):
    return jnp.where(condition, 1.0, 0.0)


def across(row, rows):
    lanes = jnp.broadcast_to(row.astype(F32), (rows, row.shape[1]))
    return lanes, lanes.T


def call(body, out_shape, *operands, flops=0):
    moved = sum(x.size * x.dtype.itemsize for x in operands)
    moved += sum(x.size * x.dtype.itemsize for x in jax.tree.leaves(out_shape))
    return pl.pallas_call(
        body,
        out_shape=out_shape,
        compiler_params=pltpu.CompilerParams(vmem_limit_bytes=VMEM_BYTES),
        cost_estimate=pl.CostEstimate(flops=flops, bytes_accessed=moved, transcendentals=0),
    )(*operands)


def pack_kernel(keyed, pos_ref, *refs):
    parts = lax.axis_size("dp")
    *x_refs, order_ref = refs[: len(refs) - parts]
    out_refs = refs[len(refs) - parts :]
    tok = order_ref.shape[0]
    share = tok // parts

    def sort(x, at):
        rows = jnp.dot(order, x, preferred_element_type=F32).astype(BF16)
        for n, out_ref in enumerate(out_refs):
            out_ref[:, at : at + x.shape[1]] = rows[n * share : (n + 1) * share]

    if keyed:
        lanes, subl = across(pos_ref[...], tok)
        rank = jnp.sum(one_hot(subl < lanes), axis=0, keepdims=True)
        order = one_hot(iota((tok, tok), 0).astype(F32) == rank).astype(BF16)
        _, offset = across(lax.rem(pos_ref[...], tok), tok)
        sort(offset.astype(BF16), sum(x.shape[1] for x in x_refs))
    else:
        order = pos_ref[...]
    order_ref[...] = order
    at = 0
    for x_ref in x_refs:
        sort(x_ref[...], at)
        at += x_ref.shape[1]


def joined(refs, columns=slice(None)):
    return jnp.concatenate([r[:, columns] for r in refs], axis=0)


def slots_of(ids_ref, cap, experts):
    tok = ids_ref.shape[1]
    first, first_t = across(ids_ref[0:1, :], tok)
    second, second_t = across(ids_ref[1:2, :], tok)
    earlier = iota((tok, tok), 0) < iota((tok, tok), 1)
    rank_first = jnp.sum(one_hot((first_t == first) & earlier), axis=0, keepdims=True)
    rank_second = jnp.sum(one_hot(first_t == second), axis=0, keepdims=True)
    rank_second += jnp.sum(one_hot((second_t == second) & earlier), axis=0, keepdims=True)

    def slot(expert, rank):
        return jnp.where((expert < experts) & (rank < cap), expert * cap + rank, -1.0)

    return slot(first[0:1, :], rank_first), slot(second[0:1, :], rank_second)


def route_kernel(cap, experts, width, seg_ref, ids_ref, code_ref, *refs):
    *key_refs, place_ref, outside_ref, taken_ref, give_ref = refs
    tok = seg_ref.shape[1]
    _, seg_q = across(seg_ref[...], tok)
    place = joined(key_refs, slice(width, width + LANES)).astype(F32).T == iota((tok, tok), 0).astype(F32)
    place_ref[...] = one_hot(place).astype(BF16)
    seg_k = jnp.sum(jnp.where(place, seg_q, 0.0), axis=0, keepdims=True)
    outside_ref[...] = one_hot(seg_q != seg_k)
    slot_first, slot_second = slots_of(ids_ref, cap, experts)
    slot = iota((experts * cap, tok), 0).astype(F32)
    taken_ref[...] = one_hot((slot == slot_first) | (slot == slot_second)).astype(BF16)
    high = (code_ref[...] >> 8).astype(F32)
    low = (code_ref[...] & 255).astype(F32)

    def weights(code):
        return jnp.where(slot == slot_first, code[0:1, :], 0.0) + jnp.where(
            slot == slot_second, code[1:2, :], 0.0
        )

    both = jnp.concatenate([weights(high) / 256.0, weights(low) / 65536.0], axis=0)
    give_ref[...] = both.T.astype(BF16)


def probs_kernel(place_ref, outside_ref, *refs):
    *row_refs, out_ref = refs
    key_refs, query_refs = row_refs[: len(row_refs) // 2], row_refs[len(row_refs) // 2 :]
    scale = 1.0 / math.sqrt(HEAD_DIM)
    outside = outside_ref[...] > 0.0
    for h in range(out_ref.shape[0]):
        columns = slice(h * HEAD_DIM, (h + 1) * HEAD_DIM)
        q = jnp.dot(place_ref[...], joined(query_refs, columns), preferred_element_type=F32).astype(BF16)
        scores = lax.dot_general(
            q, joined(key_refs, columns), (((1,), (1,)), ((), ())), preferred_element_type=F32
        )
        scores = jnp.where(outside, mask_fill, scores * scale)
        terms = jnp.exp(scores - jnp.max(scores, axis=1, keepdims=True))
        out_ref[h] = (terms / jnp.sum(terms, axis=1, keepdims=True)).astype(BF16)


def mix_kernel(probs_ref, *refs):
    *value_refs, out_ref = refs
    width = out_ref.shape[1]
    for h in range(probs_ref.shape[0]):
        lo = h * HEAD_DIM
        values = joined(value_refs, slice(width + lo, width + lo + HEAD_DIM))
        out_ref[:, lo : lo + HEAD_DIM] = jnp.dot(probs_ref[h], values, preferred_element_type=F32)


def norm_kernel(place_ref, taken_ref, gain_ref, bias_ref, mixed_ref, *refs):
    *state_refs, hidden_ref, send_ref = refs
    hidden = mixed_ref[...] + jnp.dot(place_ref[...], joined(state_refs), preferred_element_type=F32)
    hidden_ref[...] = hidden
    centered = hidden - jnp.mean(hidden, axis=1, keepdims=True)
    variance = jnp.mean(centered * centered, axis=1, keepdims=True)
    normed = (centered * lax.rsqrt(variance + epsilon) * gain_ref[...] + bias_ref[...]).astype(BF16)
    send_ref[...] = jnp.dot(taken_ref[...], normed, preferred_element_type=F32).astype(BF16)


def expert_kernel(bias_ref, w_in_ref, w_out_ref, *refs):
    x_refs, out_refs = refs[: len(refs) // 2], refs[len(refs) // 2 :]
    inner = jnp.dot(joined(x_refs), w_in_ref[0], preferred_element_type=F32)
    inner = jnp.maximum(inner + bias_ref[...], 0.0).astype(BF16)
    share = jnp.dot(inner, w_out_ref[0], preferred_element_type=F32).astype(BF16)
    at = 0
    for out_ref in out_refs:
        out_ref[...] = share[at : at + out_ref.shape[0]]
        at += out_ref.shape[0]


def add_kernel(first_ref, second_ref, out_ref):
    out_ref[...] = (first_ref[...].astype(F32) + second_ref[...].astype(F32)).astype(BF16)


def result_kernel(bias_ref, *refs):
    *share_refs, out_ref = refs
    total = share_refs[0][...].astype(F32)
    for share_ref in share_refs[1:]:
        total += share_ref[...].astype(F32)
    row = lax.axis_index("expert") == iota(bias_ref.shape, 0)
    bias = jnp.sum(jnp.where(row, bias_ref[...], 0.0), axis=0, keepdims=True)
    out_ref[...] = (total + bias).astype(BF16)


def combine_kernel(results_ref, hidden_ref, give_ref, out_ref):
    result = jnp.concatenate([results_ref[...], results_ref[...]], axis=0)
    added = jnp.dot(give_ref[...], result, preferred_element_type=F32)
    out_ref[...] = (hidden_ref[...] + added).astype(BF16)


def per_device(
    pivot_states,
    queries,
    keys,
    values,
    pack_pos,
    segment_ids,
    expert_ids,
    gate_code,
    ln_gain,
    ln_bias,
    w_in,
    b_in,
    w_out,
    b_out,
):
    tok, width = pivot_states.shape
    dp = lax.axis_size("dp")
    experts = lax.axis_size("expert")
    cap = max(2, 2 * tok // (ROUNDS * experts))
    slots = experts * cap
    heads = width // HEAD_DIM
    position = lax.rem(pack_pos + (dp - lax.axis_index("dp")) * tok, dp * tok).reshape(1, tok)

    def exchange(guide, keyed, *arrays):
        wide = width * len(arrays) + (LANES if keyed else 0)
        order, *parts = call(
            functools.partial(pack_kernel, keyed),
            (jax.ShapeDtypeStruct((tok, tok), BF16),) + (jax.ShapeDtypeStruct((tok // dp, wide), BF16),) * dp,
            guide,
            *arrays,
        )
        return order, [
            part if n == 0 else lax.ppermute(part, "dp", [(i, (i + n) % dp) for i in range(dp)])
            for n, part in enumerate(parts)
        ]

    order, key_rows = exchange(position, True, keys)
    order, pair_rows = exchange(order, False, queries, values)
    _, state_rows = exchange(order, False, pivot_states)
    place, outside, taken, give = call(
        functools.partial(route_kernel, cap, experts, width),
        (
            jax.ShapeDtypeStruct((tok, tok), BF16),
            jax.ShapeDtypeStruct((tok, tok), F32),
            jax.ShapeDtypeStruct((slots, tok), BF16),
            jax.ShapeDtypeStruct((tok, 2 * slots), BF16),
        ),
        segment_ids,
        expert_ids.T,
        gate_code.T,
        *key_rows,
    )
    probs = call(
        probs_kernel,
        jax.ShapeDtypeStruct((heads, tok, tok), BF16),
        place,
        outside,
        *key_rows,
        *pair_rows,
    )
    mixed = call(mix_kernel, jax.ShapeDtypeStruct((tok, width), F32), probs, *pair_rows)
    hidden_state, send = call(
        norm_kernel,
        (
            jax.ShapeDtypeStruct((tok, width), F32),
            jax.ShapeDtypeStruct((slots, width), BF16),
        ),
        place,
        taken,
        ln_gain.reshape(1, width),
        ln_bias.reshape(1, width),
        mixed,
        *state_rows,
    )

    def over_experts(x):
        x = x.reshape(experts, cap, width)
        return lax.all_to_all(x, "expert", split_axis=0, concat_axis=0, tiled=True).reshape(slots, width)

    def apply(*rows):
        shape = jax.ShapeDtypeStruct((slots, width), BF16)
        return call(expert_kernel, (shape,) * len(rows), b_in, w_in, w_out, *rows)

    def swap(x, distance):
        return lax.ppermute(x, "dp", [(i, i ^ distance) for i in range(dp)])

    own = over_experts(send)
    if dp == 4:
        far = swap(own, 2)
        near = swap(own, 1)
        corner = swap(far, 1)
        own_share, near_share = apply(own, near)
        corner_share, far_share = apply(corner, far)
        corner_in = swap(corner_share, 1)
        near_in = swap(near_share, 1)
        pair = call(add_kernel, jax.ShapeDtypeStruct((slots, width), BF16), corner_in, far_share)
        shares = [own_share, near_in, swap(pair, 2)]
    else:
        every = lax.all_gather(own, "dp", axis=0, tiled=True)
        (share,) = call(
            expert_kernel, (jax.ShapeDtypeStruct((dp * slots, width), BF16),), b_in, w_in, w_out, every
        )
        parts = lax.all_to_all(
            share.reshape(dp, slots, width), "dp", split_axis=0, concat_axis=0, tiled=True
        )
        shares = [parts[n] for n in range(dp)]
    results = call(result_kernel, jax.ShapeDtypeStruct((slots, width), BF16), b_out, *shares)
    return call(
        combine_kernel,
        jax.ShapeDtypeStruct((tok, width), BF16),
        over_experts(results),
        hidden_state,
        give,
    )


def solution(mesh):
    return jax.shard_map(
        per_device,
        mesh=mesh,
        in_specs=(
            P(("dp", "expert"), None),
            P(("dp", "expert"), None),
            P(("dp", "expert"), None),
            P(("dp", "expert"), None),
            P(("dp", "expert")),
            P(("dp", "expert"), None),
            P(("dp", "expert"), None),
            P(("dp", "expert"), None),
            P(),
            P(),
            P("expert", None, "dp"),
            P("expert", "dp"),
            P("expert", "dp", None),
            P(),
        ),
        out_specs=P(("dp", "expert"), None),
        check_vma=False,
    )
```

```python
import functools
import math

import jax
import jax.numpy as jnp
from jax import lax
from jax.experimental import pallas as pl
from jax.experimental.pallas import tpu as pltpu
from jax.sharding import PartitionSpec as P

HEAD_DIM = 128
ROUNDS = 4
LANES = 128

epsilon = 1e-05
mask_fill = -1e30

F32 = jnp.float32
BF16 = jnp.bfloat16

VMEM_BYTES = 32 * 1024 * 1024


def iota(shape, axis):
    return lax.broadcasted_iota(jnp.int32, shape, axis)


def one_hot(condition):
    return jnp.where(condition, 1.0, 0.0)


def across(row, rows):
    lanes = jnp.broadcast_to(row.astype(F32), (rows, row.shape[1]))
    return lanes, lanes.T


def call(body, out_shape, *operands, flops=0, vmem=VMEM_BYTES, **rest):
    moved = sum(x.size * x.dtype.itemsize for x in operands)
    moved += sum(x.size * x.dtype.itemsize for x in jax.tree.leaves(out_shape))
    return pl.pallas_call(
        body,
        out_shape=out_shape,
        compiler_params=pltpu.CompilerParams(vmem_limit_bytes=vmem),
        cost_estimate=pl.CostEstimate(flops=flops, bytes_accessed=moved, transcendentals=0),
        **rest,
    )(*operands)


def pack_kernel(pos_ref, *refs):
    parts = lax.axis_size("dp")
    count = len(refs) - parts
    x_refs, out_refs = refs[:count], refs[count:]
    tok = pos_ref.shape[1]
    share = tok // parts
    pos = lax.rem(pos_ref[...] + (parts - lax.axis_index("dp")) * tok, parts * tok)
    lanes, subl = across(pos, tok)
    rank = jnp.sum(one_hot(subl < lanes), axis=0, keepdims=True)
    order = one_hot(iota((tok, tok), 0).astype(F32) == rank).astype(BF16)

    def sort(x, at):
        rows = jnp.dot(order, x, preferred_element_type=F32).astype(BF16)
        for n, out_ref in enumerate(out_refs):
            out_ref[:, at : at + x.shape[1]] = rows[n * share : (n + 1) * share]

    at = 0
    for x_ref in x_refs:
        sort(x_ref[...], at)
        at += x_ref.shape[1]
    _, offset = across(lax.rem(pos, tok), tok)
    sort(offset.astype(BF16), at)


def joined(refs, columns=slice(None)):
    return jnp.concatenate([r[:, columns] for r in refs], axis=0)


def slots_of(ids_ref, cap, experts):
    tok = ids_ref.shape[1]
    first, first_t = across(ids_ref[0:1, :], tok)
    second, second_t = across(ids_ref[1:2, :], tok)
    earlier = iota((tok, tok), 0) < iota((tok, tok), 1)
    rank_first = jnp.sum(one_hot((first_t == first) & earlier), axis=0, keepdims=True)
    rank_second = jnp.sum(one_hot(first_t == second), axis=0, keepdims=True)
    rank_second += jnp.sum(one_hot((second_t == second) & earlier), axis=0, keepdims=True)

    def slot(expert, rank):
        return jnp.where((expert < experts) & (rank < cap), expert * cap + rank, -1.0)

    return slot(first[0:1, :], rank_first), slot(second[0:1, :], rank_second)


def slots_kernel(cap, experts, seg_ref, ids_ref, code_ref, own_ref, seg_q_ref, taken_ref, give_ref, kept_ref):
    kept_ref[...] = own_ref[...]
    tok = seg_ref.shape[1]
    _, seg_q_ref[...] = across(seg_ref[...], tok)
    slot_first, slot_second = slots_of(ids_ref, cap, experts)
    slot = iota((experts * cap, tok), 0).astype(F32)
    taken_ref[...] = one_hot((slot == slot_first) | (slot == slot_second)).astype(BF16)
    high = (code_ref[...] >> 8).astype(F32)
    low = (code_ref[...] & 255).astype(F32)

    def weights(code):
        return jnp.where(slot == slot_first, code[0:1, :], 0.0) + jnp.where(
            slot == slot_second, code[1:2, :], 0.0
        )

    both = jnp.concatenate([weights(high) / 256.0, weights(low) / 65536.0], axis=0)
    give_ref[...] = both.T.astype(BF16)


def place_kernel(first, seg_q_ref, *refs):
    *row_refs, place_ref, outside_ref = refs
    seg_q = seg_q_ref[...]
    offset = joined(row_refs, slice(first, first + LANES)).astype(F32).T
    place = offset == iota(offset.shape, 0).astype(F32)
    place_ref[...] = one_hot(place).astype(BF16)
    seg_k = jnp.sum(jnp.where(place, seg_q, 0.0), axis=0, keepdims=True)
    outside_ref[...] = one_hot(seg_q != seg_k)


def probs_kernel(place_ref, outside_ref, *refs):
    *row_refs, out_ref = refs
    width = out_ref.shape[0] * HEAD_DIM
    scale = 1.0 / math.sqrt(HEAD_DIM)
    outside = outside_ref[...] > 0.0
    for h in range(out_ref.shape[0]):
        lo = h * HEAD_DIM
        k = joined(row_refs, slice(lo, lo + HEAD_DIM))
        q = joined(row_refs, slice(width + lo, width + lo + HEAD_DIM))
        q = jnp.dot(place_ref[...], q, preferred_element_type=F32).astype(BF16)
        scores = lax.dot_general(q, k, (((1,), (1,)), ((), ())), preferred_element_type=F32)
        scores = jnp.where(outside, mask_fill, scores * scale)
        terms = jnp.exp(scores - jnp.max(scores, axis=1, keepdims=True))
        out_ref[h] = (terms / jnp.sum(terms, axis=1, keepdims=True)).astype(BF16)


def mix_kernel(probs_ref, *refs):
    *value_refs, out_ref = refs
    width = out_ref.shape[1]
    for h in range(probs_ref.shape[0]):
        lo = h * HEAD_DIM
        values = joined(value_refs, slice(2 * width + lo, 2 * width + lo + HEAD_DIM))
        out_ref[:, lo : lo + HEAD_DIM] = jnp.dot(probs_ref[h], values, preferred_element_type=F32)


def norm_kernel(place_ref, taken_ref, gain_ref, bias_ref, mixed_ref, *refs):
    *state_refs, hidden_ref, send_ref = refs
    hidden = mixed_ref[...] + jnp.dot(
        place_ref[...], joined(state_refs, slice(3 * mixed_ref.shape[1], 4 * mixed_ref.shape[1])), preferred_element_type=F32
    )
    hidden_ref[...] = hidden
    centered = hidden - jnp.mean(hidden, axis=1, keepdims=True)
    variance = jnp.mean(centered * centered, axis=1, keepdims=True)
    normed = (centered * lax.rsqrt(variance + epsilon) * gain_ref[...] + bias_ref[...]).astype(BF16)
    send_ref[...] = jnp.dot(taken_ref[...], normed, preferred_element_type=F32).astype(BF16)


def expert_kernel(count, bias_ref, w_in_ref, w_out_ref, *refs):
    x_refs, out_refs = refs[:count], refs[-count:]
    inner = jnp.dot(joined(x_refs), w_in_ref[0], preferred_element_type=F32)
    inner = jnp.maximum(inner + bias_ref[...], 0.0).astype(BF16)
    share = jnp.dot(inner, w_out_ref[0], preferred_element_type=F32).astype(BF16)
    at = 0
    for out_ref in out_refs:
        out_ref[...] = share[at : at + out_ref.shape[0]]
        at += out_ref.shape[0]


def add_kernel(first_ref, second_ref, out_ref):
    out_ref[...] = (first_ref[...].astype(F32) + second_ref[...].astype(F32)).astype(BF16)


def shares_of(refs, rows):
    shares, parts = [], []
    for ref in refs:
        parts.append(ref)
        if sum(p.shape[0] for p in parts) == rows:
            shares.append(joined(parts))
            parts = []
    return shares


def result_kernel(bias_ref, *refs):
    *share_refs, out_ref = refs
    total = 0.0
    for share in shares_of(share_refs, out_ref.shape[0]):
        total += share.astype(F32)
    row = lax.axis_index("expert") == iota(bias_ref.shape, 0)
    bias = jnp.sum(jnp.where(row, bias_ref[...], 0.0), axis=0, keepdims=True)
    out_ref[...] = (total + bias).astype(BF16)


def combine_kernel(results_ref, hidden_ref, give_ref, out_ref):
    result = jnp.concatenate([results_ref[...], results_ref[...]], axis=0)
    added = jnp.dot(give_ref[...], result, preferred_element_type=F32)
    out_ref[...] = (hidden_ref[...] + added).astype(BF16)


def per_device(
    pivot_states,
    queries,
    keys,
    values,
    pack_pos,
    segment_ids,
    expert_ids,
    gate_code,
    ln_gain,
    ln_bias,
    w_in,
    b_in,
    w_out,
    b_out,
):
    tok, width = pivot_states.shape
    dp = lax.axis_size("dp")
    experts = lax.axis_size("expert")
    cap = max(2, 2 * tok // (ROUNDS * experts))
    slots = experts * cap
    heads = width // HEAD_DIM
    packed = call(
        pack_kernel,
        (jax.ShapeDtypeStruct((tok // dp, 4 * width + LANES), BF16),) * dp,
        pack_pos.reshape(1, tok),
        keys,
        queries,
        values,
        pivot_states,
        vmem=62 * 1024 * 1024,
    )
    seg_q, taken, give, kept = call(
        functools.partial(slots_kernel, cap, experts),
        (
            jax.ShapeDtypeStruct((tok, tok), F32),
            jax.ShapeDtypeStruct((slots, tok), BF16),
            jax.ShapeDtypeStruct((tok, 2 * slots), BF16),
            jax.ShapeDtypeStruct(packed[0].shape, BF16),
        ),
        segment_ids,
        expert_ids.T,
        gate_code.T,
        packed[0],
    )
    rows = [kept]
    for n in range(1, dp):
        rows.append(lax.ppermute(packed[n], "dp", [(i, (i + n) % dp) for i in range(dp)]))
    place, outside = call(
        functools.partial(place_kernel, 4 * width),
        (jax.ShapeDtypeStruct((tok, tok), BF16), jax.ShapeDtypeStruct((tok, tok), F32)),
        seg_q,
        *rows,
    )
    probs = call(
        probs_kernel,
        jax.ShapeDtypeStruct((heads, tok, tok), BF16),
        place,
        outside,
        *rows,
    )
    mixed = call(mix_kernel, jax.ShapeDtypeStruct((tok, width), F32), probs, *rows)
    hidden_state, send = call(
        norm_kernel,
        (
            jax.ShapeDtypeStruct((tok, width), F32),
            jax.ShapeDtypeStruct((slots, width), BF16),
        ),
        place,
        taken,
        ln_gain.reshape(1, width),
        ln_bias.reshape(1, width),
        mixed,
        *rows,
    )

    def over_experts(x):
        x = x.reshape(experts, cap, width)
        return lax.all_to_all(x, "expert", split_axis=0, concat_axis=0, tiled=True).reshape(slots, width)

    def apply(rows, after=()):
        count = sum(x.shape[0] for x in rows)
        return call(
            functools.partial(expert_kernel, len(rows)),
            tuple(jax.ShapeDtypeStruct(x.shape, BF16) for x in rows),
            b_in,
            w_in,
            w_out,
            *rows,
            *after,
            flops=4 * count * width * w_in.shape[2],
        )

    def swap(x, distance):
        return lax.ppermute(x, "dp", [(i, i ^ distance) for i in range(dp)])

    own = over_experts(send)
    if dp == 4:
        half = slots // 2
        far = [swap(own[:half], 2), swap(own[half:], 2)]
        own_share, near_share = apply([own, swap(own, 1)])
        *corner_share, far_first, far_second = apply([swap(x, 1) for x in far] + far, after=[own_share])
        shares = [own_share, swap(near_share, 1)]
        for x, y in zip(corner_share, (far_first, far_second)):
            pair = call(add_kernel, jax.ShapeDtypeStruct((half, width), BF16), swap(x, 1), y)
            shares.append(swap(pair, 2))
    else:
        every = lax.all_gather(own, "dp", axis=0, tiled=True)
        (share,) = apply([every])
        parts = lax.all_to_all(
            share.reshape(dp, slots, width), "dp", split_axis=0, concat_axis=0, tiled=True
        )
        shares = [parts[n] for n in range(dp)]
    results = call(result_kernel, jax.ShapeDtypeStruct((slots, width), BF16), b_out, *shares)
    return call(
        combine_kernel,
        jax.ShapeDtypeStruct((tok, width), BF16),
        over_experts(results),
        hidden_state,
        give,
    )


def solution(mesh):
    return jax.shard_map(
        per_device,
        mesh=mesh,
        in_specs=(
            P(("dp", "expert"), None),
            P(("dp", "expert"), None),
            P(("dp", "expert"), None),
            P(("dp", "expert"), None),
            P(("dp", "expert")),
            P(("dp", "expert"), None),
            P(("dp", "expert"), None),
            P(("dp", "expert"), None),
            P(),
            P(),
            P("expert", None, "dp"),
            P("expert", "dp"),
            P("expert", "dp", None),
            P(),
        ),
        out_specs=P(("dp", "expert"), None),
        check_vma=False,
    )
```

```python
import functools
import math

import jax
import jax.numpy as jnp
from jax import lax
from jax.experimental import pallas as pl
from jax.experimental.pallas import tpu as pltpu
from jax.sharding import PartitionSpec as P

HEAD_DIM = 128
ROUNDS = 4
LANES = 128

epsilon = 1e-05
mask_fill = -1e30

F32 = jnp.float32
BF16 = jnp.bfloat16

VMEM_BYTES = 32 * 1024 * 1024
PACK_BYTES = 62 * 1024 * 1024


def iota(shape, axis):
    return lax.broadcasted_iota(jnp.int32, shape, axis)


def one_hot(condition):
    return jnp.where(condition, 1.0, 0.0)


def across(row, rows):
    lanes = jnp.broadcast_to(row.astype(F32), (rows, row.shape[1]))
    return lanes, lanes.T


def call(body, out_shape, *operands, flops=0, vmem=VMEM_BYTES, **rest):
    moved = sum(x.size * x.dtype.itemsize for x in operands)
    moved += sum(x.size * x.dtype.itemsize for x in jax.tree.leaves(out_shape))
    return pl.pallas_call(
        body,
        out_shape=out_shape,
        compiler_params=pltpu.CompilerParams(vmem_limit_bytes=vmem),
        cost_estimate=pl.CostEstimate(flops=flops, bytes_accessed=moved, transcendentals=0),
        **rest,
    )(*operands)


def pack_kernel(count, pos_ref, *refs):
    keyed = pos_ref.dtype == jnp.int32
    x_refs, order_ref, out_refs = refs[:count], refs[count], refs[count + 1 : -4]
    in_buf, out_buf, in_sem, out_sem = refs[-4:]
    parts, share, _ = out_buf.shape
    tok, width = parts * share, in_buf.shape[2]
    loads = [pltpu.make_async_copy(x, in_buf.at[i], in_sem.at[i]) for i, x in enumerate(x_refs)]
    for load in loads:
        load.start()
    stores = []

    def sort(x, i):
        columns = slice(i * width, i * width + x.shape[1])
        rows = jnp.dot(order, x, preferred_element_type=F32).astype(BF16)
        for n in range(parts):
            out_buf[n, :, columns] = rows[n * share : (n + 1) * share]
        for n in range(parts):
            store = pltpu.make_async_copy(
                out_buf.at[n, :, columns], out_refs[n].at[:, columns], out_sem.at[i, n]
            )
            store.start()
            stores.append(store)

    if keyed:
        pos = lax.rem(pos_ref[...] + (parts - lax.axis_index("dp")) * tok, parts * tok)
        lanes, subl = across(pos, tok)
        rank = jnp.sum(one_hot(subl < lanes), axis=0, keepdims=True)
        order = one_hot(iota((tok, tok), 0).astype(F32) == rank).astype(BF16)
        _, offset = across(lax.rem(pos, tok), tok)
        sort(offset.astype(BF16), count)
    else:
        order = pos_ref[...]
    order_ref[...] = order
    for i, load in enumerate(loads):
        load.wait()
        sort(in_buf[i], i)
    for store in stores:
        store.wait()


def joined(refs, columns=slice(None)):
    return jnp.concatenate([r[:, columns] for r in refs], axis=0)


def slots_of(ids_ref, cap, experts):
    tok = ids_ref.shape[1]
    first, first_t = across(ids_ref[0:1, :], tok)
    second, second_t = across(ids_ref[1:2, :], tok)
    earlier = iota((tok, tok), 0) < iota((tok, tok), 1)
    rank_first = jnp.sum(one_hot((first_t == first) & earlier), axis=0, keepdims=True)
    rank_second = jnp.sum(one_hot(first_t == second), axis=0, keepdims=True)
    rank_second += jnp.sum(one_hot((second_t == second) & earlier), axis=0, keepdims=True)

    def slot(expert, rank):
        return jnp.where((expert < experts) & (rank < cap), expert * cap + rank, -1.0)

    return slot(first[0:1, :], rank_first), slot(second[0:1, :], rank_second)


def slots_kernel(cap, experts, seg_ref, ids_ref, code_ref, own_ref, own_states_ref, *refs):
    seg_q_ref, taken_ref, give_ref, kept_ref, kept_states_ref = refs
    kept_ref[...] = own_ref[...]
    kept_states_ref[...] = own_states_ref[...]
    tok = seg_ref.shape[1]
    _, seg_q_ref[...] = across(seg_ref[...], tok)
    slot_first, slot_second = slots_of(ids_ref, cap, experts)
    slot = iota((experts * cap, tok), 0).astype(F32)
    taken_ref[...] = one_hot((slot == slot_first) | (slot == slot_second)).astype(BF16)
    high = (code_ref[...] >> 8).astype(F32)
    low = (code_ref[...] & 255).astype(F32)

    def weights(code):
        return jnp.where(slot == slot_first, code[0:1, :], 0.0) + jnp.where(
            slot == slot_second, code[1:2, :], 0.0
        )

    both = jnp.concatenate([weights(high) / 256.0, weights(low) / 65536.0], axis=0)
    give_ref[...] = both.T.astype(BF16)


def place_kernel(first, seg_q_ref, *refs):
    *row_refs, place_ref, outside_ref = refs
    seg_q = seg_q_ref[...]
    offset = joined(row_refs, slice(first, first + LANES)).astype(F32).T
    place = offset == iota(offset.shape, 0).astype(F32)
    place_ref[...] = one_hot(place).astype(BF16)
    seg_k = jnp.sum(jnp.where(place, seg_q, 0.0), axis=0, keepdims=True)
    outside_ref[...] = one_hot(seg_q != seg_k)


def probs_kernel(place_ref, outside_ref, *refs):
    *row_refs, out_ref = refs
    width = out_ref.shape[0] * HEAD_DIM
    scale = 1.0 / math.sqrt(HEAD_DIM)
    outside = outside_ref[...] > 0.0
    for h in range(out_ref.shape[0]):
        lo = h * HEAD_DIM
        k = joined(row_refs, slice(lo, lo + HEAD_DIM))
        q = joined(row_refs, slice(width + lo, width + lo + HEAD_DIM))
        q = jnp.dot(place_ref[...], q, preferred_element_type=F32).astype(BF16)
        scores = lax.dot_general(q, k, (((1,), (1,)), ((), ())), preferred_element_type=F32)
        scores = jnp.where(outside, mask_fill, scores * scale)
        terms = jnp.exp(scores - jnp.max(scores, axis=1, keepdims=True))
        out_ref[h] = (terms / jnp.sum(terms, axis=1, keepdims=True)).astype(BF16)


def mix_kernel(probs_ref, *refs):
    *value_refs, out_ref = refs
    width = out_ref.shape[1]
    for h in range(probs_ref.shape[0]):
        lo = h * HEAD_DIM
        values = joined(value_refs, slice(2 * width + lo, 2 * width + lo + HEAD_DIM))
        out_ref[:, lo : lo + HEAD_DIM] = jnp.dot(probs_ref[h], values, preferred_element_type=F32)


def norm_kernel(place_ref, taken_ref, gain_ref, bias_ref, mixed_ref, *refs):
    *state_refs, hidden_ref, send_ref = refs
    hidden = mixed_ref[...] + jnp.dot(
        place_ref[...], joined(state_refs), preferred_element_type=F32
    )
    hidden_ref[...] = hidden
    centered = hidden - jnp.mean(hidden, axis=1, keepdims=True)
    variance = jnp.mean(centered * centered, axis=1, keepdims=True)
    normed = (centered * lax.rsqrt(variance + epsilon) * gain_ref[...] + bias_ref[...]).astype(BF16)
    send_ref[...] = jnp.dot(taken_ref[...], normed, preferred_element_type=F32).astype(BF16)


def expert_kernel(count, bias_ref, w_in_ref, w_out_ref, *refs):
    x_refs, out_refs = refs[:count], refs[-count:]
    inner = jnp.dot(joined(x_refs), w_in_ref[0], preferred_element_type=F32)
    inner = jnp.maximum(inner + bias_ref[...], 0.0).astype(BF16)
    share = jnp.dot(inner, w_out_ref[0], preferred_element_type=F32).astype(BF16)
    at = 0
    for out_ref in out_refs:
        out_ref[...] = share[at : at + out_ref.shape[0]]
        at += out_ref.shape[0]


def add_kernel(first_ref, second_ref, out_ref):
    out_ref[...] = (first_ref[...].astype(F32) + second_ref[...].astype(F32)).astype(BF16)


def shares_of(refs, rows):
    shares, parts = [], []
    for ref in refs:
        parts.append(ref)
        if sum(p.shape[0] for p in parts) == rows:
            shares.append(joined(parts))
            parts = []
    return shares


def result_kernel(bias_ref, *refs):
    *share_refs, out_ref = refs
    total = 0.0
    for share in shares_of(share_refs, out_ref.shape[0]):
        total += share.astype(F32)
    row = lax.axis_index("expert") == iota(bias_ref.shape, 0)
    bias = jnp.sum(jnp.where(row, bias_ref[...], 0.0), axis=0, keepdims=True)
    out_ref[...] = (total + bias).astype(BF16)


def combine_kernel(results_ref, hidden_ref, give_ref, out_ref):
    result = jnp.concatenate([results_ref[...], results_ref[...]], axis=0)
    added = jnp.dot(give_ref[...], result, preferred_element_type=F32)
    out_ref[...] = (hidden_ref[...] + added).astype(BF16)


def per_device(
    pivot_states,
    queries,
    keys,
    values,
    pack_pos,
    segment_ids,
    expert_ids,
    gate_code,
    ln_gain,
    ln_bias,
    w_in,
    b_in,
    w_out,
    b_out,
):
    tok, width = pivot_states.shape
    dp = lax.axis_size("dp")
    experts = lax.axis_size("expert")
    cap = max(2, 2 * tok // (ROUNDS * experts))
    slots = experts * cap
    heads = width // HEAD_DIM
    def pack(guide, *arrays):
        wide = len(arrays) * width + (LANES if guide.dtype == jnp.int32 else 0)
        vmem, hbm = pl.BlockSpec(memory_space=pltpu.VMEM), pl.BlockSpec(memory_space=pl.ANY)
        return call(
            functools.partial(pack_kernel, len(arrays)),
            (jax.ShapeDtypeStruct((tok, tok), BF16),) + (jax.ShapeDtypeStruct((tok // dp, wide), BF16),) * dp,
            guide,
            *arrays,
            vmem=PACK_BYTES,
            in_specs=[vmem] + [hbm] * len(arrays),
            out_specs=(vmem,) + (hbm,) * dp,
            scratch_shapes=[
                pltpu.VMEM((len(arrays), tok, width), BF16),
                pltpu.VMEM((dp, tok // dp, wide), BF16),
                pltpu.SemaphoreType.DMA((len(arrays),)),
                pltpu.SemaphoreType.DMA((len(arrays) + 1, dp)),
            ],
        )

    def spread(parts):
        return [
            lax.ppermute(part, "dp", [(i, (i + n) % dp) for i in range(dp)]) if n else part
            for n, part in enumerate(parts)
        ]

    order, *packed = pack(pack_pos.reshape(1, tok), keys, queries, values)
    _, *packed_states = pack(order, pivot_states)
    seg_q, taken, give, kept, kept_states = call(
        functools.partial(slots_kernel, cap, experts),
        (
            jax.ShapeDtypeStruct((tok, tok), F32),
            jax.ShapeDtypeStruct((slots, tok), BF16),
            jax.ShapeDtypeStruct((tok, 2 * slots), BF16),
            jax.ShapeDtypeStruct(packed[0].shape, BF16),
            jax.ShapeDtypeStruct(packed_states[0].shape, BF16),
        ),
        segment_ids,
        expert_ids.T,
        gate_code.T,
        packed[0],
        packed_states[0],
    )
    rows = [kept] + spread(packed)[1:]
    states = [kept_states] + spread(packed_states)[1:]
    place, outside = call(
        functools.partial(place_kernel, 3 * width),
        (jax.ShapeDtypeStruct((tok, tok), BF16), jax.ShapeDtypeStruct((tok, tok), F32)),
        seg_q,
        *rows,
    )
    probs = call(
        probs_kernel,
        jax.ShapeDtypeStruct((heads, tok, tok), BF16),
        place,
        outside,
        *rows,
    )
    mixed = call(mix_kernel, jax.ShapeDtypeStruct((tok, width), F32), probs, *rows)
    hidden_state, send = call(
        norm_kernel,
        (
            jax.ShapeDtypeStruct((tok, width), F32),
            jax.ShapeDtypeStruct((slots, width), BF16),
        ),
        place,
        taken,
        ln_gain.reshape(1, width),
        ln_bias.reshape(1, width),
        mixed,
        *states,
    )

    def over_experts(x):
        x = x.reshape(experts, cap, width)
        return lax.all_to_all(x, "expert", split_axis=0, concat_axis=0, tiled=True).reshape(slots, width)

    def apply(rows, after=()):
        count = sum(x.shape[0] for x in rows)
        return call(
            functools.partial(expert_kernel, len(rows)),
            tuple(jax.ShapeDtypeStruct(x.shape, BF16) for x in rows),
            b_in,
            w_in,
            w_out,
            *rows,
            *after,
            flops=4 * count * width * w_in.shape[2],
        )

    def swap(x, distance):
        return lax.ppermute(x, "dp", [(i, i ^ distance) for i in range(dp)])

    own = over_experts(send)
    if dp == 4:
        half = slots // 2
        far = [swap(own[:half], 2), swap(own[half:], 2)]
        own_share, near_share = apply([own, swap(own, 1)])
        *corner_share, far_first, far_second = apply([swap(x, 1) for x in far] + far, after=[own_share])
        shares = [own_share, swap(near_share, 1)]
        for x, y in zip(corner_share, (far_first, far_second)):
            pair = call(add_kernel, jax.ShapeDtypeStruct((half, width), BF16), swap(x, 1), y)
            shares.append(swap(pair, 2))
    else:
        every = lax.all_gather(own, "dp", axis=0, tiled=True)
        (share,) = apply([every])
        parts = lax.all_to_all(
            share.reshape(dp, slots, width), "dp", split_axis=0, concat_axis=0, tiled=True
        )
        shares = [parts[n] for n in range(dp)]
    results = call(result_kernel, jax.ShapeDtypeStruct((slots, width), BF16), b_out, *shares)
    return call(
        combine_kernel,
        jax.ShapeDtypeStruct((tok, width), BF16),
        over_experts(results),
        hidden_state,
        give,
    )


def solution(mesh):
    return jax.shard_map(
        per_device,
        mesh=mesh,
        in_specs=(
            P(("dp", "expert"), None),
            P(("dp", "expert"), None),
            P(("dp", "expert"), None),
            P(("dp", "expert"), None),
            P(("dp", "expert")),
            P(("dp", "expert"), None),
            P(("dp", "expert"), None),
            P(("dp", "expert"), None),
            P(),
            P(),
            P("expert", None, "dp"),
            P("expert", "dp"),
            P("expert", "dp", None),
            P(),
        ),
        out_specs=P(("dp", "expert"), None),
        check_vma=False,
    )
```

```python
import functools
import math

import jax
import jax.numpy as jnp
from jax import lax
from jax.experimental import pallas as pl
from jax.experimental.pallas import tpu as pltpu
from jax.sharding import PartitionSpec as P

HEAD_DIM = 128
ROUNDS = 4
LANES = 128

epsilon = 1e-05
mask_fill = -1e30

F32 = jnp.float32
BF16 = jnp.bfloat16

VMEM_BYTES = 32 * 1024 * 1024
PACK_BYTES = 62 * 1024 * 1024


def iota(shape, axis):
    return lax.broadcasted_iota(jnp.int32, shape, axis)


def one_hot(condition):
    return jnp.where(condition, 1.0, 0.0)


def across(row, rows):
    lanes = jnp.broadcast_to(row.astype(F32), (rows, row.shape[1]))
    return lanes, lanes.T


def call(body, out_shape, *operands, flops=0, vmem=VMEM_BYTES):
    moved = sum(x.size * x.dtype.itemsize for x in operands)
    moved += sum(x.size * x.dtype.itemsize for x in jax.tree.leaves(out_shape))
    return pl.pallas_call(
        body,
        out_shape=out_shape,
        compiler_params=pltpu.CompilerParams(vmem_limit_bytes=vmem),
        cost_estimate=pl.CostEstimate(flops=flops, bytes_accessed=moved, transcendentals=0),
    )(*operands)


def pack_kernel(pos_ref, *refs):
    parts = lax.axis_size("dp")
    *x_refs, order_ref = refs[: len(refs) - parts]
    out_refs = refs[len(refs) - parts :]
    tok = order_ref.shape[0]
    share = tok // parts

    def sort(x, at):
        rows = jnp.dot(order, x, preferred_element_type=F32).astype(BF16)
        for n, out_ref in enumerate(out_refs):
            out_ref[:, at : at + x.shape[1]] = rows[n * share : (n + 1) * share]

    if pos_ref.dtype == jnp.int32:
        pos = lax.rem(pos_ref[...] + (parts - lax.axis_index("dp")) * tok, parts * tok)
        lanes, subl = across(pos, tok)
        rank = jnp.sum(one_hot(subl < lanes), axis=0, keepdims=True)
        order = one_hot(iota((tok, tok), 0).astype(F32) == rank).astype(BF16)
        _, offset = across(lax.rem(pos, tok), tok)
        sort(offset.astype(BF16), sum(x.shape[1] for x in x_refs))
    else:
        order = pos_ref[...]
    order_ref[...] = order
    at = 0
    for x_ref in x_refs:
        sort(x_ref[...], at)
        at += x_ref.shape[1]


def joined(refs, columns=slice(None)):
    return jnp.concatenate([r[:, columns] for r in refs], axis=0)


def slots_of(ids_ref, cap, experts):
    tok = ids_ref.shape[1]
    first, first_t = across(ids_ref[0:1, :], tok)
    second, second_t = across(ids_ref[1:2, :], tok)
    earlier = iota((tok, tok), 0) < iota((tok, tok), 1)
    rank_first = jnp.sum(one_hot((first_t == first) & earlier), axis=0, keepdims=True)
    rank_second = jnp.sum(one_hot(first_t == second), axis=0, keepdims=True)
    rank_second += jnp.sum(one_hot((second_t == second) & earlier), axis=0, keepdims=True)

    def slot(expert, rank):
        return jnp.where((expert < experts) & (rank < cap), expert * cap + rank, -1.0)

    return slot(first[0:1, :], rank_first), slot(second[0:1, :], rank_second)


def slots_kernel(cap, experts, seg_ref, ids_ref, code_ref, own_ref, own_later_ref, *refs):
    seg_q_ref, taken_ref, give_ref, kept_ref, kept_later_ref = refs
    kept_ref[...] = own_ref[...]
    kept_later_ref[...] = own_later_ref[...]
    tok = seg_ref.shape[1]
    _, seg_q_ref[...] = across(seg_ref[...], tok)
    slot_first, slot_second = slots_of(ids_ref, cap, experts)
    slot = iota((experts * cap, tok), 0).astype(F32)
    taken_ref[...] = one_hot((slot == slot_first) | (slot == slot_second)).astype(BF16)
    high = (code_ref[...] >> 8).astype(F32)
    low = (code_ref[...] & 255).astype(F32)

    def weights(code):
        return jnp.where(slot == slot_first, code[0:1, :], 0.0) + jnp.where(
            slot == slot_second, code[1:2, :], 0.0
        )

    both = jnp.concatenate([weights(high) / 256.0, weights(low) / 65536.0], axis=0)
    give_ref[...] = both.T.astype(BF16)


def place_kernel(first, seg_q_ref, *refs):
    *row_refs, place_ref, outside_ref = refs
    seg_q = seg_q_ref[...]
    offset = joined(row_refs, slice(first, first + LANES)).astype(F32).T
    place = offset == iota(offset.shape, 0).astype(F32)
    place_ref[...] = one_hot(place).astype(BF16)
    seg_k = jnp.sum(jnp.where(place, seg_q, 0.0), axis=0, keepdims=True)
    outside_ref[...] = one_hot(seg_q != seg_k)


def probs_kernel(place_ref, outside_ref, *refs):
    *row_refs, out_ref = refs
    width = out_ref.shape[0] * HEAD_DIM
    scale = 1.0 / math.sqrt(HEAD_DIM)
    outside = outside_ref[...] > 0.0
    for h in range(out_ref.shape[0]):
        lo = h * HEAD_DIM
        k = joined(row_refs, slice(lo, lo + HEAD_DIM))
        q = joined(row_refs, slice(width + lo, width + lo + HEAD_DIM))
        q = jnp.dot(place_ref[...], q, preferred_element_type=F32).astype(BF16)
        scores = lax.dot_general(q, k, (((1,), (1,)), ((), ())), preferred_element_type=F32)
        scores = jnp.where(outside, mask_fill, scores * scale)
        terms = jnp.exp(scores - jnp.max(scores, axis=1, keepdims=True))
        out_ref[h] = (terms / jnp.sum(terms, axis=1, keepdims=True)).astype(BF16)


def mix_kernel(probs_ref, *refs):
    *value_refs, out_ref = refs
    width = out_ref.shape[1]
    for h in range(probs_ref.shape[0]):
        lo = h * HEAD_DIM
        values = joined(value_refs, slice(lo, lo + HEAD_DIM))
        out_ref[:, lo : lo + HEAD_DIM] = jnp.dot(probs_ref[h], values, preferred_element_type=F32)


def norm_kernel(place_ref, taken_ref, gain_ref, bias_ref, mixed_ref, *refs):
    *state_refs, hidden_ref, send_ref = refs
    hidden = mixed_ref[...] + jnp.dot(
        place_ref[...], joined(state_refs, slice(mixed_ref.shape[1], None)), preferred_element_type=F32
    )
    hidden_ref[...] = hidden
    centered = hidden - jnp.mean(hidden, axis=1, keepdims=True)
    variance = jnp.mean(centered * centered, axis=1, keepdims=True)
    normed = (centered * lax.rsqrt(variance + epsilon) * gain_ref[...] + bias_ref[...]).astype(BF16)
    send_ref[...] = jnp.dot(taken_ref[...], normed, preferred_element_type=F32).astype(BF16)


def expert_kernel(count, bias_ref, w_in_ref, w_out_ref, *refs):
    x_refs, out_refs = refs[:count], refs[-count:]
    inner = jnp.dot(joined(x_refs), w_in_ref[0], preferred_element_type=F32)
    inner = jnp.maximum(inner + bias_ref[...], 0.0).astype(BF16)
    share = jnp.dot(inner, w_out_ref[0], preferred_element_type=F32).astype(BF16)
    at = 0
    for out_ref in out_refs:
        out_ref[...] = share[at : at + out_ref.shape[0]]
        at += out_ref.shape[0]


def add_kernel(first_ref, second_ref, out_ref):
    out_ref[...] = (first_ref[...].astype(F32) + second_ref[...].astype(F32)).astype(BF16)


def shares_of(refs, rows):
    shares, parts = [], []
    for ref in refs:
        parts.append(ref)
        if sum(p.shape[0] for p in parts) == rows:
            shares.append(joined(parts))
            parts = []
    return shares


def result_kernel(bias_ref, *refs):
    *share_refs, out_ref = refs
    total = 0.0
    for share in shares_of(share_refs, out_ref.shape[0]):
        total += share.astype(F32)
    row = lax.axis_index("expert") == iota(bias_ref.shape, 0)
    bias = jnp.sum(jnp.where(row, bias_ref[...], 0.0), axis=0, keepdims=True)
    out_ref[...] = (total + bias).astype(BF16)


def combine_kernel(results_ref, hidden_ref, give_ref, out_ref):
    result = jnp.concatenate([results_ref[...], results_ref[...]], axis=0)
    added = jnp.dot(give_ref[...], result, preferred_element_type=F32)
    out_ref[...] = (hidden_ref[...] + added).astype(BF16)


def per_device(
    pivot_states,
    queries,
    keys,
    values,
    pack_pos,
    segment_ids,
    expert_ids,
    gate_code,
    ln_gain,
    ln_bias,
    w_in,
    b_in,
    w_out,
    b_out,
):
    tok, width = pivot_states.shape
    dp = lax.axis_size("dp")
    experts = lax.axis_size("expert")
    cap = max(2, 2 * tok // (ROUNDS * experts))
    slots = experts * cap
    heads = width // HEAD_DIM
    def pack(guide, *arrays):
        wide = len(arrays) * width + (LANES if guide.dtype == jnp.int32 else 0)
        return call(
            pack_kernel,
            (jax.ShapeDtypeStruct((tok, tok), BF16),) + (jax.ShapeDtypeStruct((tok // dp, wide), BF16),) * dp,
            guide,
            *arrays,
            vmem=PACK_BYTES,
        )

    def spread(parts):
        return [
            lax.ppermute(part, "dp", [(i, (i + n) % dp) for i in range(dp)]) if n else part
            for n, part in enumerate(parts)
        ]

    order, *packed = pack(pack_pos.reshape(1, tok), keys, queries)
    _, *packed_later = pack(order, values, pivot_states)
    seg_q, taken, give, kept, kept_later = call(
        functools.partial(slots_kernel, cap, experts),
        (
            jax.ShapeDtypeStruct((tok, tok), F32),
            jax.ShapeDtypeStruct((slots, tok), BF16),
            jax.ShapeDtypeStruct((tok, 2 * slots), BF16),
            jax.ShapeDtypeStruct(packed[0].shape, BF16),
            jax.ShapeDtypeStruct(packed_later[0].shape, BF16),
        ),
        segment_ids,
        expert_ids.T,
        gate_code.T,
        packed[0],
        packed_later[0],
    )
    rows = [kept] + spread(packed)[1:]
    later = [kept_later] + spread(packed_later)[1:]
    place, outside = call(
        functools.partial(place_kernel, 2 * width),
        (jax.ShapeDtypeStruct((tok, tok), BF16), jax.ShapeDtypeStruct((tok, tok), F32)),
        seg_q,
        *rows,
    )
    probs = call(
        probs_kernel,
        jax.ShapeDtypeStruct((heads, tok, tok), BF16),
        place,
        outside,
        *rows,
    )
    mixed = call(mix_kernel, jax.ShapeDtypeStruct((tok, width), F32), probs, *later)
    hidden_state, send = call(
        norm_kernel,
        (
            jax.ShapeDtypeStruct((tok, width), F32),
            jax.ShapeDtypeStruct((slots, width), BF16),
        ),
        place,
        taken,
        ln_gain.reshape(1, width),
        ln_bias.reshape(1, width),
        mixed,
        *later,
    )

    def over_experts(x):
        x = x.reshape(experts, cap, width)
        return lax.all_to_all(x, "expert", split_axis=0, concat_axis=0, tiled=True).reshape(slots, width)

    def apply(rows, after=()):
        count = sum(x.shape[0] for x in rows)
        return call(
            functools.partial(expert_kernel, len(rows)),
            tuple(jax.ShapeDtypeStruct(x.shape, BF16) for x in rows),
            b_in,
            w_in,
            w_out,
            *rows,
            *after,
            flops=4 * count * width * w_in.shape[2],
        )

    def swap(x, distance):
        return lax.ppermute(x, "dp", [(i, i ^ distance) for i in range(dp)])

    own = over_experts(send)
    if dp == 4:
        half = slots // 2
        far = [swap(own[:half], 2), swap(own[half:], 2)]
        own_share, near_share = apply([own, swap(own, 1)])
        *corner_share, far_first, far_second = apply([swap(x, 1) for x in far] + far, after=[own_share])
        shares = [own_share, swap(near_share, 1)]
        for x, y in zip(corner_share, (far_first, far_second)):
            pair = call(add_kernel, jax.ShapeDtypeStruct((half, width), BF16), swap(x, 1), y)
            shares.append(swap(pair, 2))
    else:
        every = lax.all_gather(own, "dp", axis=0, tiled=True)
        (share,) = apply([every])
        parts = lax.all_to_all(
            share.reshape(dp, slots, width), "dp", split_axis=0, concat_axis=0, tiled=True
        )
        shares = [parts[n] for n in range(dp)]
    results = call(result_kernel, jax.ShapeDtypeStruct((slots, width), BF16), b_out, *shares)
    return call(
        combine_kernel,
        jax.ShapeDtypeStruct((tok, width), BF16),
        over_experts(results),
        hidden_state,
        give,
    )


def solution(mesh):
    return jax.shard_map(
        per_device,
        mesh=mesh,
        in_specs=(
            P(("dp", "expert"), None),
            P(("dp", "expert"), None),
            P(("dp", "expert"), None),
            P(("dp", "expert"), None),
            P(("dp", "expert")),
            P(("dp", "expert"), None),
            P(("dp", "expert"), None),
            P(("dp", "expert"), None),
            P(),
            P(),
            P("expert", None, "dp"),
            P("expert", "dp"),
            P("expert", "dp", None),
            P(),
        ),
        out_specs=P(("dp", "expert"), None),
        check_vma=False,
    )
```

```python
import functools
import math

import jax
import jax.numpy as jnp
from jax import lax
from jax.experimental import pallas as pl
from jax.experimental.pallas import tpu as pltpu
from jax.sharding import PartitionSpec as P

HEAD_DIM = 128
ROUNDS = 4
LANES = 128

epsilon = 1e-05
mask_fill = -1e30

F32 = jnp.float32
BF16 = jnp.bfloat16

VMEM_BYTES = 32 * 1024 * 1024
PACK_BYTES = 62 * 1024 * 1024


def iota(shape, axis):
    return lax.broadcasted_iota(jnp.int32, shape, axis)


def one_hot(condition):
    return jnp.where(condition, 1.0, 0.0)


def across(row, rows):
    lanes = jnp.broadcast_to(row.astype(F32), (rows, row.shape[1]))
    return lanes, lanes.T


def call(body, out_shape, *operands, flops=0, vmem=VMEM_BYTES):
    moved = sum(x.size * x.dtype.itemsize for x in operands)
    moved += sum(x.size * x.dtype.itemsize for x in jax.tree.leaves(out_shape))
    return pl.pallas_call(
        body,
        out_shape=out_shape,
        compiler_params=pltpu.CompilerParams(vmem_limit_bytes=vmem),
        cost_estimate=pl.CostEstimate(flops=flops, bytes_accessed=moved, transcendentals=0),
    )(*operands)


def pack_kernel(pos_ref, *refs):
    parts = lax.axis_size("dp")
    *x_refs, order_ref = refs[: len(refs) - parts]
    out_refs = refs[len(refs) - parts :]
    tok = order_ref.shape[0]
    share = tok // parts

    def sort(x, at):
        rows = jnp.dot(order, x, preferred_element_type=F32).astype(BF16)
        for n, out_ref in enumerate(out_refs):
            out_ref[:, at : at + x.shape[1]] = rows[n * share : (n + 1) * share]

    if pos_ref.dtype == jnp.int32:
        pos = lax.rem(pos_ref[...] + (parts - lax.axis_index("dp")) * tok, parts * tok)
        lanes, subl = across(pos, tok)
        rank = jnp.sum(one_hot(subl < lanes), axis=0, keepdims=True)
        order = one_hot(iota((tok, tok), 0).astype(F32) == rank).astype(BF16)
        _, offset = across(lax.rem(pos, tok), tok)
        sort(offset.astype(BF16), sum(x.shape[1] for x in x_refs))
    else:
        order = pos_ref[...]
    order_ref[...] = order
    at = 0
    for x_ref in x_refs:
        sort(x_ref[...], at)
        at += x_ref.shape[1]


def joined(refs, columns=slice(None)):
    return jnp.concatenate([r[:, columns] for r in refs], axis=0)


def slots_of(ids, cap, experts):
    tok = ids.shape[1]
    first, first_t = across(ids[0:1, :], tok)
    second, second_t = across(ids[1:2, :], tok)
    earlier = iota((tok, tok), 0) < iota((tok, tok), 1)
    rank_first = jnp.sum(one_hot((first_t == first) & earlier), axis=0, keepdims=True)
    rank_second = jnp.sum(one_hot(first_t == second), axis=0, keepdims=True)
    rank_second += jnp.sum(one_hot((second_t == second) & earlier), axis=0, keepdims=True)

    def slot(expert, rank):
        return jnp.where((expert < experts) & (rank < cap), expert * cap + rank, -1.0)

    return slot(first[0:1, :], rank_first), slot(second[0:1, :], rank_second)


def slots_kernel(cap, experts, relative, seg_ref, ids_ref, code_ref, own_ref, own_later_ref, *refs):
    seg_q_ref, taken_ref, give_ref, kept_ref, kept_later_ref = refs
    kept_ref[...] = own_ref[...]
    kept_later_ref[...] = own_later_ref[...]
    tok = seg_ref.shape[1]
    _, seg_q_ref[...] = across(seg_ref[...], tok)
    ids = ids_ref[...]
    if relative:
        other = ids ^ lax.axis_index("expert")
        ids = jnp.where(ids < experts, (other & 1) * (experts // 2) + (other >> 1), ids)
    slot_first, slot_second = slots_of(ids, cap, experts)
    slot = iota((experts * cap, tok), 0).astype(F32)
    taken_ref[...] = one_hot((slot == slot_first) | (slot == slot_second)).astype(BF16)
    high = (code_ref[...] >> 8).astype(F32)
    low = (code_ref[...] & 255).astype(F32)

    def weights(code):
        return jnp.where(slot == slot_first, code[0:1, :], 0.0) + jnp.where(
            slot == slot_second, code[1:2, :], 0.0
        )

    both = jnp.concatenate([weights(high) / 256.0, weights(low) / 65536.0], axis=0)
    give_ref[...] = both.T.astype(BF16)


def place_kernel(first, seg_q_ref, *refs):
    *row_refs, place_ref, outside_ref = refs
    seg_q = seg_q_ref[...]
    offset = joined(row_refs, slice(first, first + LANES)).astype(F32).T
    place = offset == iota(offset.shape, 0).astype(F32)
    place_ref[...] = one_hot(place).astype(BF16)
    seg_k = jnp.sum(jnp.where(place, seg_q, 0.0), axis=0, keepdims=True)
    outside_ref[...] = one_hot(seg_q != seg_k)


def probs_kernel(place_ref, outside_ref, *refs):
    *row_refs, out_ref = refs
    width = out_ref.shape[0] * HEAD_DIM
    scale = 1.0 / math.sqrt(HEAD_DIM)
    outside = outside_ref[...] > 0.0
    for h in range(out_ref.shape[0]):
        lo = h * HEAD_DIM
        k = joined(row_refs, slice(lo, lo + HEAD_DIM))
        q = joined(row_refs, slice(width + lo, width + lo + HEAD_DIM))
        q = jnp.dot(place_ref[...], q, preferred_element_type=F32).astype(BF16)
        scores = lax.dot_general(q, k, (((1,), (1,)), ((), ())), preferred_element_type=F32)
        scores = jnp.where(outside, mask_fill, scores * scale)
        terms = jnp.exp(scores - jnp.max(scores, axis=1, keepdims=True))
        out_ref[h] = (terms / jnp.sum(terms, axis=1, keepdims=True)).astype(BF16)


def mix_kernel(probs_ref, *refs):
    *value_refs, out_ref = refs
    width = out_ref.shape[1]
    for h in range(probs_ref.shape[0]):
        lo = h * HEAD_DIM
        values = joined(value_refs, slice(lo, lo + HEAD_DIM))
        out_ref[:, lo : lo + HEAD_DIM] = jnp.dot(probs_ref[h], values, preferred_element_type=F32)


def norm_kernel(parts, place_ref, taken_ref, gain_ref, bias_ref, mixed_ref, *refs):
    state_refs, hidden_ref, send_refs = refs[: -parts - 1], refs[-parts - 1], refs[-parts:]
    hidden = mixed_ref[...] + jnp.dot(
        place_ref[...], joined(state_refs, slice(mixed_ref.shape[1], None)), preferred_element_type=F32
    )
    hidden_ref[...] = hidden
    centered = hidden - jnp.mean(hidden, axis=1, keepdims=True)
    variance = jnp.mean(centered * centered, axis=1, keepdims=True)
    normed = (centered * lax.rsqrt(variance + epsilon) * gain_ref[...] + bias_ref[...]).astype(BF16)
    picked = jnp.dot(taken_ref[...], normed, preferred_element_type=F32).astype(BF16)
    at = 0
    for send_ref in send_refs:
        send_ref[...] = picked[at : at + send_ref.shape[0]]
        at += send_ref.shape[0]


def expert_kernel(count, bias_ref, w_in_ref, w_out_ref, *refs):
    x_refs, out_refs = refs[:count], refs[-count:]
    inner = jnp.dot(joined(x_refs), w_in_ref[0], preferred_element_type=F32)
    inner = jnp.maximum(inner + bias_ref[...], 0.0).astype(BF16)
    share = jnp.dot(inner, w_out_ref[0], preferred_element_type=F32).astype(BF16)
    at = 0
    for out_ref in out_refs:
        out_ref[...] = share[at : at + out_ref.shape[0]]
        at += out_ref.shape[0]


def add_kernel(first_ref, second_ref, out_ref):
    out_ref[...] = (first_ref[...].astype(F32) + second_ref[...].astype(F32)).astype(BF16)


def result_kernel(lower, bias_ref, near_ref, *refs):
    count = refs[0].shape[0]
    outs = next(n for n in range(1, len(refs)) if sum(r.shape[0] for r in refs[-n:]) == count)
    total = near_ref[lower : lower + count].astype(F32)
    for share_ref in refs[:-outs]:
        total += share_ref[...].astype(F32)
    row = lax.axis_index("expert") == iota(bias_ref.shape, 0)
    bias = jnp.sum(jnp.where(row, bias_ref[...], 0.0), axis=0, keepdims=True)
    result = (total + bias).astype(BF16)
    at = 0
    for out_ref in refs[-outs:]:
        out_ref[...] = result[at : at + out_ref.shape[0]]
        at += out_ref.shape[0]


def join_kernel(*refs):
    refs[-1][...] = joined(refs[:-1])


def pair_kernel(cap, mine_ref, other_ref, *piece_refs):
    mine, other = mine_ref[...].astype(F32), other_ref[...].astype(F32)
    for n, piece_ref in enumerate(piece_refs):
        rows = slice(n * cap, (n + 1) * cap)
        piece_ref[...] = jnp.concatenate([mine[rows], other[rows]], axis=0).astype(BF16)


def part_kernel(cap, *refs):
    *piece_refs, mine_ref, other_ref = refs
    pieces = [piece_ref[...].astype(F32) for piece_ref in piece_refs]
    mine_ref[...] = jnp.concatenate([piece[:cap] for piece in pieces], axis=0).astype(BF16)
    other_ref[...] = jnp.concatenate([piece[cap:] for piece in pieces], axis=0).astype(BF16)


def combine_kernel(hidden_ref, give_ref, *refs):
    *result_refs, out_ref = refs
    result = joined(list(result_refs) * 2)
    added = jnp.dot(give_ref[...], result, preferred_element_type=F32)
    out_ref[...] = (hidden_ref[...] + added).astype(BF16)


def per_device(
    pivot_states,
    queries,
    keys,
    values,
    pack_pos,
    segment_ids,
    expert_ids,
    gate_code,
    ln_gain,
    ln_bias,
    w_in,
    b_in,
    w_out,
    b_out,
):
    tok, width = pivot_states.shape
    dp = lax.axis_size("dp")
    experts = lax.axis_size("expert")
    cap = max(2, 2 * tok // (ROUNDS * experts))
    slots = experts * cap
    relative = dp == 4 and experts == 8
    heads = width // HEAD_DIM
    def pack(guide, *arrays):
        wide = len(arrays) * width + (LANES if guide.dtype == jnp.int32 else 0)
        return call(
            pack_kernel,
            (jax.ShapeDtypeStruct((tok, tok), BF16),) + (jax.ShapeDtypeStruct((tok // dp, wide), BF16),) * dp,
            guide,
            *arrays,
            vmem=PACK_BYTES,
        )

    def spread(parts):
        return [
            lax.ppermute(part, "dp", [(i, (i + n) % dp) for i in range(dp)]) if n else part
            for n, part in enumerate(parts)
        ]

    order, *packed = pack(pack_pos.reshape(1, tok), keys, queries)
    _, *packed_later = pack(order, values, pivot_states)
    seg_q, taken, give, kept, kept_later = call(
        functools.partial(slots_kernel, cap, experts, relative),
        (
            jax.ShapeDtypeStruct((tok, tok), F32),
            jax.ShapeDtypeStruct((slots, tok), BF16),
            jax.ShapeDtypeStruct((tok, 2 * slots), BF16),
            jax.ShapeDtypeStruct(packed[0].shape, BF16),
            jax.ShapeDtypeStruct(packed_later[0].shape, BF16),
        ),
        segment_ids,
        expert_ids.T,
        gate_code.T,
        packed[0],
        packed_later[0],
    )
    rows = [kept] + spread(packed)[1:]
    later = [kept_later] + spread(packed_later)[1:]
    place, outside = call(
        functools.partial(place_kernel, 2 * width),
        (jax.ShapeDtypeStruct((tok, tok), BF16), jax.ShapeDtypeStruct((tok, tok), F32)),
        seg_q,
        *rows,
    )
    probs = call(
        probs_kernel,
        jax.ShapeDtypeStruct((heads, tok, tok), BF16),
        place,
        outside,
        *rows,
    )
    mixed = call(mix_kernel, jax.ShapeDtypeStruct((tok, width), F32), probs, *later)
    parts = 2 if relative else 1
    hidden_state, *send = call(
        functools.partial(norm_kernel, parts),
        (jax.ShapeDtypeStruct((tok, width), F32),)
        + (jax.ShapeDtypeStruct((slots // parts, width), BF16),) * parts,
        place,
        taken,
        ln_gain.reshape(1, width),
        ln_bias.reshape(1, width),
        mixed,
        *later,
    )

    def over_experts(x):
        x = x.reshape(experts, cap, width)
        return lax.all_to_all(x, "expert", split_axis=0, concat_axis=0, tiled=True).reshape(slots, width)

    def bf16(rows):
        return jax.ShapeDtypeStruct((rows, width), BF16)

    def apply(rows, after=()):
        count = sum(x.shape[0] for x in rows)
        return call(
            functools.partial(expert_kernel, len(rows)),
            tuple(bf16(x.shape[0]) for x in rows),
            b_in,
            w_in,
            w_out,
            *rows,
            *after,
            flops=4 * count * width * w_in.shape[2],
        )

    def swap(x, distance, axis="dp"):
        return lax.ppermute(x, axis, [(i, i ^ distance) for i in range(lax.axis_size(axis))])

    if relative:
        half = slots // 2
        pieces = call(
            functools.partial(pair_kernel, cap), (bf16(2 * cap),) * 4, send[0], swap(send[1], 1, "expert")
        )
        pieces = [swap(x, 2 * n, "expert") if n else x for n, x in enumerate(pieces)]
        own = [call(join_kernel, bf16(half), *pieces[n : n + 2]) for n in (2, 0)]
        far = [swap(x, 2) for x in own]
        near = [swap(x, 1) for x in own]
        *own_share, near_first, near_second = apply(own + near)
        *corner_share, far_first, far_second = apply([swap(x, 1) for x in far] + far, after=own_share[:1])
        near_shares = [swap(near_first, 1), swap(near_second, 1)]
        far_shares = [far_first, far_second]
        pieces = ()
        for n in (1, 0):
            pair = swap(call(add_kernel, bf16(half), swap(corner_share[n], 1), far_shares[n]), 2)
            pieces += tuple(
                call(
                    functools.partial(result_kernel, 0),
                    (bf16(2 * cap),) * 2,
                    b_out,
                    near_shares[n],
                    own_share[n],
                    pair,
                )
            )
        pieces = [swap(x, 2 * n, "expert") if n else x for n, x in enumerate(pieces)]
        mine, other = call(functools.partial(part_kernel, cap), (bf16(half),) * 2, *pieces)
        returned = [mine, swap(other, 1, "expert")]
    else:
        every = lax.all_gather(over_experts(send[0]), "dp", axis=0, tiled=True)
        (share,) = apply([every])
        shares = lax.all_to_all(
            share.reshape(dp, slots, width), "dp", split_axis=0, concat_axis=0, tiled=True
        )
        (results,) = call(
            functools.partial(result_kernel, 0), (bf16(slots),), b_out, *[shares[n] for n in range(dp)]
        )
        returned = [over_experts(results)]
    return call(
        combine_kernel, jax.ShapeDtypeStruct((tok, width), BF16), hidden_state, give, *returned
    )


def solution(mesh):
    return jax.shard_map(
        per_device,
        mesh=mesh,
        in_specs=(
            P(("dp", "expert"), None),
            P(("dp", "expert"), None),
            P(("dp", "expert"), None),
            P(("dp", "expert"), None),
            P(("dp", "expert")),
            P(("dp", "expert"), None),
            P(("dp", "expert"), None),
            P(("dp", "expert"), None),
            P(),
            P(),
            P("expert", None, "dp"),
            P("expert", "dp"),
            P("expert", "dp", None),
            P(),
        ),
        out_specs=P(("dp", "expert"), None),
        check_vma=False,
    )
```

```python
import functools
import math

import jax
import jax.numpy as jnp
from jax import lax
from jax.experimental import pallas as pl
from jax.experimental.pallas import tpu as pltpu
from jax.sharding import PartitionSpec as P

HEAD_DIM = 128
ROUNDS = 4
LANES = 128

epsilon = 1e-05
mask_fill = -1e30

F32 = jnp.float32
BF16 = jnp.bfloat16

VMEM_BYTES = 32 * 1024 * 1024
PACK_BYTES = 62 * 1024 * 1024


def iota(shape, axis):
    return lax.broadcasted_iota(jnp.int32, shape, axis)


def one_hot(condition):
    return jnp.where(condition, 1.0, 0.0)


def across(row, rows):
    lanes = jnp.broadcast_to(row.astype(F32), (rows, row.shape[1]))
    return lanes, lanes.T


def call(body, out_shape, *operands, flops=0, vmem=VMEM_BYTES):
    moved = sum(x.size * x.dtype.itemsize for x in operands)
    moved += sum(x.size * x.dtype.itemsize for x in jax.tree.leaves(out_shape))
    return pl.pallas_call(
        body,
        out_shape=out_shape,
        compiler_params=pltpu.CompilerParams(vmem_limit_bytes=vmem),
        cost_estimate=pl.CostEstimate(flops=flops, bytes_accessed=moved, transcendentals=0),
    )(*operands)


def pack_kernel(pos_ref, *refs):
    parts = lax.axis_size("dp")
    *x_refs, order_ref = refs[: len(refs) - parts]
    out_refs = refs[len(refs) - parts :]
    tok = order_ref.shape[0]
    share = tok // parts

    def sort(x, at):
        rows = jnp.dot(order, x, preferred_element_type=F32).astype(BF16)
        for n, out_ref in enumerate(out_refs):
            out_ref[:, at : at + x.shape[1]] = rows[n * share : (n + 1) * share]

    if pos_ref.dtype == jnp.int32:
        pos = lax.rem(pos_ref[...] + (parts - lax.axis_index("dp")) * tok, parts * tok)
        lanes, subl = across(pos, tok)
        rank = jnp.sum(one_hot(subl < lanes), axis=0, keepdims=True)
        order = one_hot(iota((tok, tok), 0).astype(F32) == rank).astype(BF16)
        _, offset = across(lax.rem(pos, tok), tok)
        sort(offset.astype(BF16), sum(x.shape[1] for x in x_refs))
    else:
        order = pos_ref[...]
    order_ref[...] = order
    at = 0
    for x_ref in x_refs:
        sort(x_ref[...], at)
        at += x_ref.shape[1]


def joined(refs, columns=slice(None)):
    return jnp.concatenate([r[:, columns] for r in refs], axis=0)


def slots_of(ids, cap, experts):
    tok = ids.shape[1]
    first, first_t = across(ids[0:1, :], tok)
    second, second_t = across(ids[1:2, :], tok)
    earlier = iota((tok, tok), 0) < iota((tok, tok), 1)
    rank_first = jnp.sum(one_hot((first_t == first) & earlier), axis=0, keepdims=True)
    rank_second = jnp.sum(one_hot(first_t == second), axis=0, keepdims=True)
    rank_second += jnp.sum(one_hot((second_t == second) & earlier), axis=0, keepdims=True)

    def slot(expert, rank):
        return jnp.where((expert < experts) & (rank < cap), expert * cap + rank, -1.0)

    return slot(first[0:1, :], rank_first), slot(second[0:1, :], rank_second)


def slots_kernel(cap, experts, relative, seg_ref, ids_ref, code_ref, own_ref, own_later_ref, *refs):
    seg_q_ref, taken_ref, give_ref, kept_ref, kept_later_ref = refs
    kept_ref[...] = own_ref[...]
    kept_later_ref[...] = own_later_ref[...]
    tok = seg_ref.shape[1]
    _, seg_q_ref[...] = across(seg_ref[...], tok)
    ids = ids_ref[...]
    if relative:
        other = ids ^ lax.axis_index("expert")
        ids = jnp.where(ids < experts, (other & 1) * (experts // 2) + (other >> 1), ids)
    slot_first, slot_second = slots_of(ids, cap, experts)
    slot = iota((experts * cap, tok), 0).astype(F32)
    taken_ref[...] = one_hot((slot == slot_first) | (slot == slot_second)).astype(BF16)
    high = (code_ref[...] >> 8).astype(F32)
    low = (code_ref[...] & 255).astype(F32)

    def weights(code):
        return jnp.where(slot == slot_first, code[0:1, :], 0.0) + jnp.where(
            slot == slot_second, code[1:2, :], 0.0
        )

    both = jnp.concatenate([weights(high) / 256.0, weights(low) / 65536.0], axis=0)
    give_ref[...] = both.T.astype(BF16)


def place_kernel(first, seg_q_ref, *refs):
    *row_refs, place_ref, outside_ref = refs
    seg_q = seg_q_ref[...]
    offset = joined(row_refs, slice(first, first + LANES)).astype(F32).T
    place = offset == iota(offset.shape, 0).astype(F32)
    place_ref[...] = one_hot(place).astype(BF16)
    seg_k = jnp.sum(jnp.where(place, seg_q, 0.0), axis=0, keepdims=True)
    outside_ref[...] = one_hot(seg_q != seg_k)


def probs_kernel(place_ref, outside_ref, *refs):
    *row_refs, out_ref = refs
    width = out_ref.shape[0] * HEAD_DIM
    scale = 1.0 / math.sqrt(HEAD_DIM)
    outside = outside_ref[...] > 0.0
    for h in range(out_ref.shape[0]):
        lo = h * HEAD_DIM
        k = joined(row_refs, slice(lo, lo + HEAD_DIM))
        q = joined(row_refs, slice(width + lo, width + lo + HEAD_DIM))
        q = jnp.dot(place_ref[...], q, preferred_element_type=F32).astype(BF16)
        scores = lax.dot_general(q, k, (((1,), (1,)), ((), ())), preferred_element_type=F32)
        scores = jnp.where(outside, mask_fill, scores * scale)
        terms = jnp.exp(scores - jnp.max(scores, axis=1, keepdims=True))
        out_ref[h] = (terms / jnp.sum(terms, axis=1, keepdims=True)).astype(BF16)


def mix_kernel(probs_ref, *refs):
    *value_refs, out_ref = refs
    width = out_ref.shape[1]
    for h in range(probs_ref.shape[0]):
        lo = h * HEAD_DIM
        values = joined(value_refs, slice(lo, lo + HEAD_DIM))
        out_ref[:, lo : lo + HEAD_DIM] = jnp.dot(probs_ref[h], values, preferred_element_type=F32)


def norm_kernel(parts, place_ref, taken_ref, gain_ref, bias_ref, mixed_ref, *refs):
    state_refs, hidden_ref, send_refs = refs[: -parts - 1], refs[-parts - 1], refs[-parts:]
    hidden = mixed_ref[...] + jnp.dot(
        place_ref[...], joined(state_refs, slice(mixed_ref.shape[1], None)), preferred_element_type=F32
    )
    hidden_ref[...] = hidden
    centered = hidden - jnp.mean(hidden, axis=1, keepdims=True)
    variance = jnp.mean(centered * centered, axis=1, keepdims=True)
    normed = (centered * lax.rsqrt(variance + epsilon) * gain_ref[...] + bias_ref[...]).astype(BF16)
    picked = jnp.dot(taken_ref[...], normed, preferred_element_type=F32).astype(BF16)
    at = 0
    for send_ref in send_refs:
        send_ref[...] = picked[at : at + send_ref.shape[0]]
        at += send_ref.shape[0]


def expert_kernel(count, bias_ref, w_in_ref, w_out_ref, *refs):
    x_refs, out_refs = refs[:count], refs[-count:]
    inner = jnp.dot(joined(x_refs), w_in_ref[0], preferred_element_type=F32)
    inner = jnp.maximum(inner + bias_ref[...], 0.0).astype(BF16)
    share = jnp.dot(inner, w_out_ref[0], preferred_element_type=F32).astype(BF16)
    at = 0
    for out_ref in out_refs:
        out_ref[...] = share[at : at + out_ref.shape[0]]
        at += out_ref.shape[0]


def add_kernel(first_ref, second_ref, out_ref):
    out_ref[...] = (first_ref[...].astype(F32) + second_ref[...].astype(F32)).astype(BF16)


def result_kernel(lower, bias_ref, near_ref, *refs):
    count = refs[0].shape[0]
    outs = next(n for n in range(1, len(refs)) if sum(r.shape[0] for r in refs[-n:]) == count)
    total = near_ref[lower : lower + count].astype(F32)
    for share_ref in refs[:-outs]:
        total += share_ref[...].astype(F32)
    row = lax.axis_index("expert") == iota(bias_ref.shape, 0)
    bias = jnp.sum(jnp.where(row, bias_ref[...], 0.0), axis=0, keepdims=True)
    result = (total + bias).astype(BF16)
    at = 0
    for out_ref in refs[-outs:]:
        out_ref[...] = result[at : at + out_ref.shape[0]]
        at += out_ref.shape[0]


def join_kernel(*refs):
    refs[-1][...] = joined(refs[:-1])


def pair_kernel(cap, mine_ref, other_ref, *piece_refs):
    mine, other = mine_ref[...].astype(F32), other_ref[...].astype(F32)
    for n, piece_ref in enumerate(piece_refs):
        rows = slice(n * cap, (n + 1) * cap)
        piece_ref[...] = jnp.concatenate([mine[rows], other[rows]], axis=0).astype(BF16)


def part_kernel(cap, *refs):
    *piece_refs, mine_ref, other_ref = refs
    pieces = [piece_ref[...].astype(F32) for piece_ref in piece_refs]
    mine_ref[...] = jnp.concatenate([piece[:cap] for piece in pieces], axis=0).astype(BF16)
    other_ref[...] = jnp.concatenate([piece[cap:] for piece in pieces], axis=0).astype(BF16)


def combine_kernel(hidden_ref, give_ref, *refs):
    *result_refs, out_ref = refs
    result = joined(list(result_refs) * 2)
    added = jnp.dot(give_ref[...], result, preferred_element_type=F32)
    out_ref[...] = (hidden_ref[...] + added).astype(BF16)


def per_device(
    pivot_states,
    queries,
    keys,
    values,
    pack_pos,
    segment_ids,
    expert_ids,
    gate_code,
    ln_gain,
    ln_bias,
    w_in,
    b_in,
    w_out,
    b_out,
):
    tok, width = pivot_states.shape
    dp = lax.axis_size("dp")
    experts = lax.axis_size("expert")
    cap = max(2, 2 * tok // (ROUNDS * experts))
    slots = experts * cap
    relative = dp == 4 and experts == 8
    heads = width // HEAD_DIM
    def pack(guide, *arrays):
        wide = len(arrays) * width + (LANES if guide.dtype == jnp.int32 else 0)
        return call(
            pack_kernel,
            (jax.ShapeDtypeStruct((tok, tok), BF16),) + (jax.ShapeDtypeStruct((tok // dp, wide), BF16),) * dp,
            guide,
            *arrays,
            vmem=PACK_BYTES,
        )

    def spread(parts):
        return [
            lax.ppermute(part, "dp", [(i, (i + n) % dp) for i in range(dp)]) if n else part
            for n, part in enumerate(parts)
        ]

    order, *packed = pack(pack_pos.reshape(1, tok), keys, queries)
    _, *packed_later = pack(order, values, pivot_states)
    seg_q, taken, give, kept, kept_later = call(
        functools.partial(slots_kernel, cap, experts, relative),
        (
            jax.ShapeDtypeStruct((tok, tok), F32),
            jax.ShapeDtypeStruct((slots, tok), BF16),
            jax.ShapeDtypeStruct((tok, 2 * slots), BF16),
            jax.ShapeDtypeStruct(packed[0].shape, BF16),
            jax.ShapeDtypeStruct(packed_later[0].shape, BF16),
        ),
        segment_ids,
        expert_ids.T,
        gate_code.T,
        packed[0],
        packed_later[0],
    )
    rows = [kept] + spread(packed)[1:]
    later = [kept_later] + spread(packed_later)[1:]
    place, outside = call(
        functools.partial(place_kernel, 2 * width),
        (jax.ShapeDtypeStruct((tok, tok), BF16), jax.ShapeDtypeStruct((tok, tok), F32)),
        seg_q,
        *rows,
    )
    probs = call(
        probs_kernel,
        jax.ShapeDtypeStruct((heads, tok, tok), BF16),
        place,
        outside,
        *rows,
    )
    mixed = call(mix_kernel, jax.ShapeDtypeStruct((tok, width), F32), probs, *later)
    parts = 2 if relative else 1
    hidden_state, *send = call(
        functools.partial(norm_kernel, parts),
        (jax.ShapeDtypeStruct((tok, width), F32),)
        + (jax.ShapeDtypeStruct((slots // parts, width), BF16),) * parts,
        place,
        taken,
        ln_gain.reshape(1, width),
        ln_bias.reshape(1, width),
        mixed,
        *later,
    )

    def over_experts(x):
        x = x.reshape(experts, cap, width)
        return lax.all_to_all(x, "expert", split_axis=0, concat_axis=0, tiled=True).reshape(slots, width)

    def bf16(rows):
        return jax.ShapeDtypeStruct((rows, width), BF16)

    def apply(rows, after=()):
        count = sum(x.shape[0] for x in rows)
        return call(
            functools.partial(expert_kernel, len(rows)),
            tuple(bf16(x.shape[0]) for x in rows),
            b_in,
            w_in,
            w_out,
            *rows,
            *after,
            flops=4 * count * width * w_in.shape[2],
        )

    def swap(x, distance, axis="dp"):
        return lax.ppermute(x, axis, [(i, i ^ distance) for i in range(lax.axis_size(axis))])

    if relative:
        half = slots // 2
        pieces = call(
            functools.partial(pair_kernel, cap), (bf16(2 * cap),) * 4, send[0], swap(send[1], 1, "expert")
        )
        pieces = [swap(x, 2 * n, "expert") if n else x for n, x in enumerate(pieces)]
        own = [call(join_kernel, bf16(half), *pieces[n : n + 2]) for n in (2, 0)]
        far = [swap(x, 2) for x in own]
        near = [swap(x, 1) for x in own]
        early_share, near_second = apply([own[1], near[1]])
        late_share, near_first = apply([own[0], near[0]], after=[early_share])
        own_share = [late_share, early_share]
        far_first, far_second = apply(far, after=[late_share])
        corner_share = apply([swap(x, 1) for x in far], after=[far_first])
        near_shares = [swap(near_first, 1), swap(near_second, 1)]
        far_shares = [far_first, far_second]
        pieces = ()
        for n in (1, 0):
            pair = swap(call(add_kernel, bf16(half), swap(corner_share[n], 1), far_shares[n]), 2)
            pieces += tuple(
                call(
                    functools.partial(result_kernel, 0),
                    (bf16(2 * cap),) * 2,
                    b_out,
                    near_shares[n],
                    own_share[n],
                    pair,
                )
            )
        pieces = [swap(x, 2 * n, "expert") if n else x for n, x in enumerate(pieces)]
        mine, other = call(functools.partial(part_kernel, cap), (bf16(half),) * 2, *pieces)
        returned = [mine, swap(other, 1, "expert")]
    else:
        every = lax.all_gather(over_experts(send[0]), "dp", axis=0, tiled=True)
        (share,) = apply([every])
        shares = lax.all_to_all(
            share.reshape(dp, slots, width), "dp", split_axis=0, concat_axis=0, tiled=True
        )
        (results,) = call(
            functools.partial(result_kernel, 0), (bf16(slots),), b_out, *[shares[n] for n in range(dp)]
        )
        returned = [over_experts(results)]
    return call(
        combine_kernel, jax.ShapeDtypeStruct((tok, width), BF16), hidden_state, give, *returned
    )


def solution(mesh):
    return jax.shard_map(
        per_device,
        mesh=mesh,
        in_specs=(
            P(("dp", "expert"), None),
            P(("dp", "expert"), None),
            P(("dp", "expert"), None),
            P(("dp", "expert"), None),
            P(("dp", "expert")),
            P(("dp", "expert"), None),
            P(("dp", "expert"), None),
            P(("dp", "expert"), None),
            P(),
            P(),
            P("expert", None, "dp"),
            P("expert", "dp"),
            P("expert", "dp", None),
            P(),
        ),
        out_specs=P(("dp", "expert"), None),
        check_vma=False,
    )
```

```python
import functools
import math

import jax
import jax.numpy as jnp
from jax import lax
from jax.experimental import pallas as pl
from jax.experimental.pallas import tpu as pltpu
from jax.sharding import PartitionSpec as P

HEAD_DIM = 128
ROUNDS = 4
LANES = 128

epsilon = 1e-05
mask_fill = -1e30

F32 = jnp.float32
BF16 = jnp.bfloat16

VMEM_BYTES = 32 * 1024 * 1024
PACK_BYTES = 62 * 1024 * 1024


def iota(shape, axis):
    return lax.broadcasted_iota(jnp.int32, shape, axis)


def one_hot(condition):
    return jnp.where(condition, 1.0, 0.0)


def across(row, rows):
    lanes = jnp.broadcast_to(row.astype(F32), (rows, row.shape[1]))
    return lanes, lanes.T


def call(body, out_shape, *operands, flops=0, vmem=VMEM_BYTES):
    moved = sum(x.size * x.dtype.itemsize for x in operands)
    moved += sum(x.size * x.dtype.itemsize for x in jax.tree.leaves(out_shape))
    return pl.pallas_call(
        body,
        out_shape=out_shape,
        compiler_params=pltpu.CompilerParams(vmem_limit_bytes=vmem),
        cost_estimate=pl.CostEstimate(flops=flops, bytes_accessed=moved, transcendentals=0),
    )(*operands)


def pack_kernel(pos_ref, *refs):
    parts = lax.axis_size("dp")
    *x_refs, order_ref = refs[: len(refs) - parts]
    out_refs = refs[len(refs) - parts :]
    tok = order_ref.shape[0]
    share = tok // parts

    def sort(x, at):
        rows = jnp.dot(order, x, preferred_element_type=F32).astype(BF16)
        for n, out_ref in enumerate(out_refs):
            out_ref[:, at : at + x.shape[1]] = rows[n * share : (n + 1) * share]

    if pos_ref.dtype == jnp.int32:
        pos = lax.rem(pos_ref[...] + (parts - lax.axis_index("dp")) * tok, parts * tok)
        lanes, subl = across(pos, tok)
        rank = jnp.sum(one_hot(subl < lanes), axis=0, keepdims=True)
        order = one_hot(iota((tok, tok), 0).astype(F32) == rank).astype(BF16)
        _, offset = across(lax.rem(pos, tok), tok)
        sort(offset.astype(BF16), sum(x.shape[1] for x in x_refs))
    else:
        order = pos_ref[...]
    order_ref[...] = order
    at = 0
    for x_ref in x_refs:
        sort(x_ref[...], at)
        at += x_ref.shape[1]


def joined(refs, columns=slice(None)):
    return jnp.concatenate([r[:, columns] for r in refs], axis=0)


def slots_of(ids, cap, experts):
    tok = ids.shape[1]
    first, first_t = across(ids[0:1, :], tok)
    second, second_t = across(ids[1:2, :], tok)
    earlier = iota((tok, tok), 0) < iota((tok, tok), 1)
    rank_first = jnp.sum(one_hot((first_t == first) & earlier), axis=0, keepdims=True)
    rank_second = jnp.sum(one_hot(first_t == second), axis=0, keepdims=True)
    rank_second += jnp.sum(one_hot((second_t == second) & earlier), axis=0, keepdims=True)

    def slot(expert, rank):
        return jnp.where((expert < experts) & (rank < cap), expert * cap + rank, -1.0)

    return slot(first[0:1, :], rank_first), slot(second[0:1, :], rank_second)


def slots_kernel(cap, experts, relative, seg_ref, ids_ref, code_ref, own_ref, own_later_ref, *refs):
    seg_q_ref, taken_ref, give_ref, kept_ref, kept_later_ref = refs
    kept_ref[...] = own_ref[...]
    kept_later_ref[...] = own_later_ref[...]
    tok = seg_ref.shape[1]
    _, seg_q_ref[...] = across(seg_ref[...], tok)
    ids = ids_ref[...]
    if relative:
        other = ids ^ lax.axis_index("expert")
        ids = jnp.where(ids < experts, (other & 1) * (experts // 2) + (other >> 1), ids)
    slot_first, slot_second = slots_of(ids, cap, experts)
    slot = iota((experts * cap, tok), 0).astype(F32)
    taken_ref[...] = one_hot((slot == slot_first) | (slot == slot_second)).astype(BF16)
    high = (code_ref[...] >> 8).astype(F32)
    low = (code_ref[...] & 255).astype(F32)

    def weights(code):
        return jnp.where(slot == slot_first, code[0:1, :], 0.0) + jnp.where(
            slot == slot_second, code[1:2, :], 0.0
        )

    both = jnp.concatenate([weights(high) / 256.0, weights(low) / 65536.0], axis=0)
    give_ref[...] = both.T.astype(BF16)


def place_kernel(first, seg_q_ref, *refs):
    *row_refs, place_ref, outside_ref = refs
    seg_q = seg_q_ref[...]
    offset = joined(row_refs, slice(first, first + LANES)).astype(F32).T
    place = offset == iota(offset.shape, 0).astype(F32)
    place_ref[...] = one_hot(place).astype(BF16)
    seg_k = jnp.sum(jnp.where(place, seg_q, 0.0), axis=0, keepdims=True)
    outside_ref[...] = one_hot(seg_q != seg_k)


def probs_kernel(place_ref, outside_ref, *refs):
    *row_refs, out_ref = refs
    width = out_ref.shape[0] * HEAD_DIM
    scale = 1.0 / math.sqrt(HEAD_DIM)
    outside = outside_ref[...] > 0.0
    for h in range(out_ref.shape[0]):
        lo = h * HEAD_DIM
        k = joined(row_refs, slice(lo, lo + HEAD_DIM))
        q = joined(row_refs, slice(width + lo, width + lo + HEAD_DIM))
        q = jnp.dot(place_ref[...], q, preferred_element_type=F32).astype(BF16)
        scores = lax.dot_general(q, k, (((1,), (1,)), ((), ())), preferred_element_type=F32)
        scores = jnp.where(outside, mask_fill, scores * scale)
        terms = jnp.exp(scores - jnp.max(scores, axis=1, keepdims=True))
        out_ref[h] = (terms / jnp.sum(terms, axis=1, keepdims=True)).astype(BF16)


def mix_kernel(probs_ref, *refs):
    *value_refs, out_ref = refs
    width = out_ref.shape[1]
    for h in range(probs_ref.shape[0]):
        lo = h * HEAD_DIM
        values = joined(value_refs, slice(lo, lo + HEAD_DIM))
        out_ref[:, lo : lo + HEAD_DIM] = jnp.dot(probs_ref[h], values, preferred_element_type=F32)


def norm_kernel(parts, place_ref, taken_ref, gain_ref, bias_ref, mixed_ref, *refs):
    state_refs, hidden_ref, send_refs = refs[: -parts - 1], refs[-parts - 1], refs[-parts:]
    hidden = mixed_ref[...] + jnp.dot(
        place_ref[...], joined(state_refs, slice(mixed_ref.shape[1], None)), preferred_element_type=F32
    )
    hidden_ref[...] = hidden
    centered = hidden - jnp.mean(hidden, axis=1, keepdims=True)
    variance = jnp.mean(centered * centered, axis=1, keepdims=True)
    normed = (centered * lax.rsqrt(variance + epsilon) * gain_ref[...] + bias_ref[...]).astype(BF16)
    picked = jnp.dot(taken_ref[...], normed, preferred_element_type=F32).astype(BF16)
    at = 0
    for send_ref in send_refs:
        send_ref[...] = picked[at : at + send_ref.shape[0]]
        at += send_ref.shape[0]


def expert_kernel(count, outs, bias_ref, w_in_ref, w_out_ref, *refs):
    x_refs, out_refs = refs[:count], refs[-outs:]
    inner = jnp.dot(joined(x_refs), w_in_ref[0], preferred_element_type=F32)
    inner = jnp.maximum(inner + bias_ref[...], 0.0).astype(BF16)
    share = jnp.dot(inner, w_out_ref[0], preferred_element_type=F32).astype(BF16)
    at = 0
    for out_ref in out_refs:
        out_ref[...] = share[at : at + out_ref.shape[0]]
        at += out_ref.shape[0]


def add_kernel(first_ref, second_ref, out_ref):
    out_ref[...] = (first_ref[...].astype(F32) + second_ref[...].astype(F32)).astype(BF16)


def result_kernel(lower, bias_ref, near_ref, *refs):
    count = refs[0].shape[0]
    outs = next(n for n in range(1, len(refs)) if sum(r.shape[0] for r in refs[-n:]) == count)
    total = near_ref[lower : lower + count].astype(F32)
    for share_ref in refs[:-outs]:
        total += share_ref[...].astype(F32)
    row = lax.axis_index("expert") == iota(bias_ref.shape, 0)
    bias = jnp.sum(jnp.where(row, bias_ref[...], 0.0), axis=0, keepdims=True)
    result = (total + bias).astype(BF16)
    at = 0
    for out_ref in refs[-outs:]:
        out_ref[...] = result[at : at + out_ref.shape[0]]
        at += out_ref.shape[0]


def join_kernel(*refs):
    refs[-1][...] = joined(refs[:-1])


def pair_kernel(cap, mine_ref, other_ref, *piece_refs):
    mine, other = mine_ref[...].astype(F32), other_ref[...].astype(F32)
    for n, piece_ref in enumerate(piece_refs):
        rows = slice(n * cap, (n + 1) * cap)
        piece_ref[...] = jnp.concatenate([mine[rows], other[rows]], axis=0).astype(BF16)


def part_kernel(cap, *refs):
    *piece_refs, mine_ref, other_ref = refs
    pieces = [piece_ref[...].astype(F32) for piece_ref in piece_refs]
    mine_ref[...] = jnp.concatenate([piece[:cap] for piece in pieces], axis=0).astype(BF16)
    other_ref[...] = jnp.concatenate([piece[cap:] for piece in pieces], axis=0).astype(BF16)


def combine_kernel(hidden_ref, give_ref, *refs):
    *result_refs, out_ref = refs
    result = joined(list(result_refs) * 2)
    added = jnp.dot(give_ref[...], result, preferred_element_type=F32)
    out_ref[...] = (hidden_ref[...] + added).astype(BF16)


def per_device(
    pivot_states,
    queries,
    keys,
    values,
    pack_pos,
    segment_ids,
    expert_ids,
    gate_code,
    ln_gain,
    ln_bias,
    w_in,
    b_in,
    w_out,
    b_out,
):
    tok, width = pivot_states.shape
    dp = lax.axis_size("dp")
    experts = lax.axis_size("expert")
    cap = max(2, 2 * tok // (ROUNDS * experts))
    slots = experts * cap
    relative = dp == 4 and experts == 8
    heads = width // HEAD_DIM
    def pack(guide, *arrays):
        wide = len(arrays) * width + (LANES if guide.dtype == jnp.int32 else 0)
        return call(
            pack_kernel,
            (jax.ShapeDtypeStruct((tok, tok), BF16),) + (jax.ShapeDtypeStruct((tok // dp, wide), BF16),) * dp,
            guide,
            *arrays,
            vmem=PACK_BYTES,
        )

    def spread(parts):
        return [
            lax.ppermute(part, "dp", [(i, (i + n) % dp) for i in range(dp)]) if n else part
            for n, part in enumerate(parts)
        ]

    order, *packed = pack(pack_pos.reshape(1, tok), keys, queries)
    _, *packed_later = pack(order, values, pivot_states)
    seg_q, taken, give, kept, kept_later = call(
        functools.partial(slots_kernel, cap, experts, relative),
        (
            jax.ShapeDtypeStruct((tok, tok), F32),
            jax.ShapeDtypeStruct((slots, tok), BF16),
            jax.ShapeDtypeStruct((tok, 2 * slots), BF16),
            jax.ShapeDtypeStruct(packed[0].shape, BF16),
            jax.ShapeDtypeStruct(packed_later[0].shape, BF16),
        ),
        segment_ids,
        expert_ids.T,
        gate_code.T,
        packed[0],
        packed_later[0],
    )
    rows = [kept] + spread(packed)[1:]
    later = [kept_later] + spread(packed_later)[1:]
    place, outside = call(
        functools.partial(place_kernel, 2 * width),
        (jax.ShapeDtypeStruct((tok, tok), BF16), jax.ShapeDtypeStruct((tok, tok), F32)),
        seg_q,
        *rows,
    )
    probs = call(
        probs_kernel,
        jax.ShapeDtypeStruct((heads, tok, tok), BF16),
        place,
        outside,
        *rows,
    )
    mixed = call(mix_kernel, jax.ShapeDtypeStruct((tok, width), F32), probs, *later)
    parts = 2 if relative else 1
    hidden_state, *send = call(
        functools.partial(norm_kernel, parts),
        (jax.ShapeDtypeStruct((tok, width), F32),)
        + (jax.ShapeDtypeStruct((slots // parts, width), BF16),) * parts,
        place,
        taken,
        ln_gain.reshape(1, width),
        ln_bias.reshape(1, width),
        mixed,
        *later,
    )

    def over_experts(x):
        x = x.reshape(experts, cap, width)
        return lax.all_to_all(x, "expert", split_axis=0, concat_axis=0, tiled=True).reshape(slots, width)

    def bf16(rows):
        return jax.ShapeDtypeStruct((rows, width), BF16)

    def apply(rows, outs, after=()):
        count = sum(x.shape[0] for x in rows)
        return call(
            functools.partial(expert_kernel, len(rows), len(outs)),
            tuple(bf16(n) for n in outs),
            b_in,
            w_in,
            w_out,
            *rows,
            *after,
            flops=4 * count * width * w_in.shape[2],
        )

    def swap(x, distance, axis="dp"):
        return lax.ppermute(x, axis, [(i, i ^ distance) for i in range(lax.axis_size(axis))])

    if relative:
        half = slots // 2
        pieces = call(
            functools.partial(pair_kernel, cap), (bf16(2 * cap),) * 4, send[0], swap(send[1], 1, "expert")
        )
        pieces = [swap(x, 2 * n, "expert") if n else x for n, x in enumerate(pieces)]
        own = [call(join_kernel, bf16(half), *pieces[n : n + 2]) for n in (2, 0)]
        far = [swap(x, 2) for x in own]
        near = [swap(x, 1) for x in own]
        *own_share, near_share = apply(own + near, [half, half, slots])
        *corner_share, far_first, far_second = apply(
            [swap(x, 1) for x in far] + far, [half] * 4, after=own_share[:1]
        )
        far_share = [far_first, far_second]
        near_share = swap(near_share, 1)
        back = [None, None]
        for n in (0, 1):
            pair = swap(call(add_kernel, bf16(half), swap(corner_share[n], 1), far_share[n]), 2)
            back[n] = call(
                functools.partial(result_kernel, n * half),
                (bf16(2 * cap),) * 2,
                b_out,
                near_share,
                own_share[n],
                pair,
            )
        pieces = [x for n in (1, 0) for x in back[n]]
        pieces = [swap(x, 2 * n, "expert") if n else x for n, x in enumerate(pieces)]
        mine, other = call(functools.partial(part_kernel, cap), (bf16(half),) * 2, *pieces)
        returned = [mine, swap(other, 1, "expert")]
    else:
        every = lax.all_gather(over_experts(send[0]), "dp", axis=0, tiled=True)
        (share,) = apply([every], [dp * slots])
        shares = lax.all_to_all(
            share.reshape(dp, slots, width), "dp", split_axis=0, concat_axis=0, tiled=True
        )
        (results,) = call(
            functools.partial(result_kernel, 0), (bf16(slots),), b_out, *[shares[n] for n in range(dp)]
        )
        returned = [over_experts(results)]
    return call(
        combine_kernel, jax.ShapeDtypeStruct((tok, width), BF16), hidden_state, give, *returned
    )


def solution(mesh):
    return jax.shard_map(
        per_device,
        mesh=mesh,
        in_specs=(
            P(("dp", "expert"), None),
            P(("dp", "expert"), None),
            P(("dp", "expert"), None),
            P(("dp", "expert"), None),
            P(("dp", "expert")),
            P(("dp", "expert"), None),
            P(("dp", "expert"), None),
            P(("dp", "expert"), None),
            P(),
            P(),
            P("expert", None, "dp"),
            P("expert", "dp"),
            P("expert", "dp", None),
            P(),
        ),
        out_specs=P(("dp", "expert"), None),
        check_vma=False,
    )
```

```python
import functools
import math

import jax
import jax.numpy as jnp
from jax import lax
from jax.experimental import pallas as pl
from jax.experimental.pallas import tpu as pltpu
from jax.sharding import PartitionSpec as P

HEAD_DIM = 128
ROUNDS = 4
LANES = 128

epsilon = 1e-05
mask_fill = -1e30

F32 = jnp.float32
BF16 = jnp.bfloat16

VMEM_BYTES = 32 * 1024 * 1024
PACK_BYTES = 62 * 1024 * 1024


def iota(shape, axis):
    return lax.broadcasted_iota(jnp.int32, shape, axis)


def one_hot(condition):
    return jnp.where(condition, 1.0, 0.0)


def across(row, rows):
    lanes = jnp.broadcast_to(row.astype(F32), (rows, row.shape[1]))
    return lanes, lanes.T


def call(body, out_shape, *operands, flops=0, vmem=VMEM_BYTES):
    moved = sum(x.size * x.dtype.itemsize for x in operands)
    moved += sum(x.size * x.dtype.itemsize for x in jax.tree.leaves(out_shape))
    return pl.pallas_call(
        body,
        out_shape=out_shape,
        compiler_params=pltpu.CompilerParams(vmem_limit_bytes=vmem),
        cost_estimate=pl.CostEstimate(flops=flops, bytes_accessed=moved, transcendentals=0),
    )(*operands)


def pack_kernel(pos_ref, *refs):
    parts = lax.axis_size("dp")
    *x_refs, order_ref = refs[: len(refs) - parts]
    out_refs = refs[len(refs) - parts :]
    tok = order_ref.shape[0]
    share = tok // parts

    def sort(x, at):
        rows = jnp.dot(order, x, preferred_element_type=F32).astype(BF16)
        for n, out_ref in enumerate(out_refs):
            out_ref[:, at : at + x.shape[1]] = rows[n * share : (n + 1) * share]

    if pos_ref.dtype == jnp.int32:
        pos = lax.rem(pos_ref[...] + (parts - lax.axis_index("dp")) * tok, parts * tok)
        lanes, subl = across(pos, tok)
        rank = jnp.sum(one_hot(subl < lanes), axis=0, keepdims=True)
        order = one_hot(iota((tok, tok), 0).astype(F32) == rank).astype(BF16)
        _, offset = across(lax.rem(pos, tok), tok)
        sort(offset.astype(BF16), sum(x.shape[1] for x in x_refs))
    else:
        order = pos_ref[...]
    order_ref[...] = order
    at = 0
    for x_ref in x_refs:
        sort(x_ref[...], at)
        at += x_ref.shape[1]


def joined(refs, columns=slice(None)):
    return jnp.concatenate([r[:, columns] for r in refs], axis=0)


def slots_of(ids, cap, experts):
    tok = ids.shape[1]
    first, first_t = across(ids[0:1, :], tok)
    second, second_t = across(ids[1:2, :], tok)
    earlier = iota((tok, tok), 0) < iota((tok, tok), 1)
    rank_first = jnp.sum(one_hot((first_t == first) & earlier), axis=0, keepdims=True)
    rank_second = jnp.sum(one_hot(first_t == second), axis=0, keepdims=True)
    rank_second += jnp.sum(one_hot((second_t == second) & earlier), axis=0, keepdims=True)

    def slot(expert, rank):
        return jnp.where((expert < experts) & (rank < cap), expert * cap + rank, -1.0)

    return slot(first[0:1, :], rank_first), slot(second[0:1, :], rank_second)


def slots_kernel(cap, experts, relative, seg_ref, ids_ref, code_ref, own_ref, own_later_ref, *refs):
    seg_q_ref, taken_ref, give_ref, kept_ref, kept_later_ref = refs
    kept_ref[...] = own_ref[...]
    kept_later_ref[...] = own_later_ref[...]
    tok = seg_ref.shape[1]
    _, seg_q_ref[...] = across(seg_ref[...], tok)
    ids = ids_ref[...]
    if relative:
        other = ids ^ lax.axis_index("expert")
        ids = jnp.where(ids < experts, (other & 1) * (experts // 2) + (other >> 1), ids)
    slot_first, slot_second = slots_of(ids, cap, experts)
    slot = iota((experts * cap, tok), 0).astype(F32)
    taken_ref[...] = one_hot((slot == slot_first) | (slot == slot_second)).astype(BF16)
    high = (code_ref[...] >> 8).astype(F32)
    low = (code_ref[...] & 255).astype(F32)

    def weights(code):
        return jnp.where(slot == slot_first, code[0:1, :], 0.0) + jnp.where(
            slot == slot_second, code[1:2, :], 0.0
        )

    both = jnp.concatenate([weights(high) / 256.0, weights(low) / 65536.0], axis=0)
    give_ref[...] = both.T.astype(BF16)


def place_kernel(first, seg_q_ref, *refs):
    *row_refs, place_ref, outside_ref = refs
    seg_q = seg_q_ref[...]
    offset = joined(row_refs, slice(first, first + LANES)).astype(F32).T
    place = offset == iota(offset.shape, 0).astype(F32)
    place_ref[...] = one_hot(place).astype(BF16)
    seg_k = jnp.sum(jnp.where(place, seg_q, 0.0), axis=0, keepdims=True)
    outside_ref[...] = one_hot(seg_q != seg_k)


def probs_kernel(place_ref, outside_ref, *refs):
    *row_refs, out_ref = refs
    width = out_ref.shape[0] * HEAD_DIM
    scale = 1.0 / math.sqrt(HEAD_DIM)
    outside = outside_ref[...] > 0.0
    for h in range(out_ref.shape[0]):
        lo = h * HEAD_DIM
        k = joined(row_refs, slice(lo, lo + HEAD_DIM))
        q = joined(row_refs, slice(width + lo, width + lo + HEAD_DIM))
        q = jnp.dot(place_ref[...], q, preferred_element_type=F32).astype(BF16)
        scores = lax.dot_general(q, k, (((1,), (1,)), ((), ())), preferred_element_type=F32)
        scores = jnp.where(outside, mask_fill, scores * scale)
        terms = jnp.exp(scores - jnp.max(scores, axis=1, keepdims=True))
        out_ref[h] = (terms / jnp.sum(terms, axis=1, keepdims=True)).astype(BF16)


def mix_kernel(probs_ref, *refs):
    *value_refs, out_ref = refs
    width = out_ref.shape[1]
    for h in range(probs_ref.shape[0]):
        lo = h * HEAD_DIM
        values = joined(value_refs, slice(lo, lo + HEAD_DIM))
        out_ref[:, lo : lo + HEAD_DIM] = jnp.dot(probs_ref[h], values, preferred_element_type=F32)


def norm_kernel(parts, place_ref, taken_ref, gain_ref, bias_ref, mixed_ref, *refs):
    state_refs, hidden_ref, send_refs = refs[: -parts - 1], refs[-parts - 1], refs[-parts:]
    hidden = mixed_ref[...] + jnp.dot(
        place_ref[...], joined(state_refs, slice(mixed_ref.shape[1], None)), preferred_element_type=F32
    )
    hidden_ref[...] = hidden
    centered = hidden - jnp.mean(hidden, axis=1, keepdims=True)
    variance = jnp.mean(centered * centered, axis=1, keepdims=True)
    normed = (centered * lax.rsqrt(variance + epsilon) * gain_ref[...] + bias_ref[...]).astype(BF16)
    picked = jnp.dot(taken_ref[...], normed, preferred_element_type=F32).astype(BF16)
    at = 0
    for send_ref in send_refs:
        send_ref[...] = picked[at : at + send_ref.shape[0]]
        at += send_ref.shape[0]


def expert_kernel(count, bias_ref, w_in_ref, w_out_ref, *refs):
    x_refs, out_refs = refs[:count], refs[-count:]
    inner = jnp.dot(joined(x_refs), w_in_ref[0], preferred_element_type=F32)
    inner = jnp.maximum(inner + bias_ref[...], 0.0).astype(BF16)
    share = jnp.dot(inner, w_out_ref[0], preferred_element_type=F32).astype(BF16)
    at = 0
    for out_ref in out_refs:
        out_ref[...] = share[at : at + out_ref.shape[0]]
        at += out_ref.shape[0]


def add_kernel(first_ref, second_ref, out_ref):
    out_ref[...] = (first_ref[...].astype(F32) + second_ref[...].astype(F32)).astype(BF16)


def result_kernel(lower, bias_ref, near_ref, *refs):
    count = refs[0].shape[0]
    outs = next(n for n in range(1, len(refs)) if sum(r.shape[0] for r in refs[-n:]) == count)
    total = near_ref[lower : lower + count].astype(F32)
    for share_ref in refs[:-outs]:
        total += share_ref[...].astype(F32)
    row = lax.axis_index("expert") == iota(bias_ref.shape, 0)
    bias = jnp.sum(jnp.where(row, bias_ref[...], 0.0), axis=0, keepdims=True)
    result = (total + bias).astype(BF16)
    at = 0
    for out_ref in refs[-outs:]:
        out_ref[...] = result[at : at + out_ref.shape[0]]
        at += out_ref.shape[0]


def join_kernel(*refs):
    refs[-1][...] = joined(refs[:-1])


def pair_kernel(cap, mine_ref, other_ref, *piece_refs):
    mine, other = mine_ref[...].astype(F32), other_ref[...].astype(F32)
    for n, piece_ref in enumerate(piece_refs):
        rows = slice(n * cap, (n + 1) * cap)
        piece_ref[...] = jnp.concatenate([mine[rows], other[rows]], axis=0).astype(BF16)


def part_kernel(cap, *refs):
    *piece_refs, mine_ref, other_ref = refs
    pieces = [piece_ref[...].astype(F32) for piece_ref in piece_refs]
    mine_ref[...] = jnp.concatenate([piece[:cap] for piece in pieces], axis=0).astype(BF16)
    other_ref[...] = jnp.concatenate([piece[cap:] for piece in pieces], axis=0).astype(BF16)


def combine_kernel(hidden_ref, give_ref, *refs):
    *result_refs, out_ref = refs
    result = joined(list(result_refs) * 2)
    added = jnp.dot(give_ref[...], result, preferred_element_type=F32)
    out_ref[...] = (hidden_ref[...] + added).astype(BF16)


def per_device(
    pivot_states,
    queries,
    keys,
    values,
    pack_pos,
    segment_ids,
    expert_ids,
    gate_code,
    ln_gain,
    ln_bias,
    w_in,
    b_in,
    w_out,
    b_out,
):
    tok, width = pivot_states.shape
    dp = lax.axis_size("dp")
    experts = lax.axis_size("expert")
    cap = max(2, 2 * tok // (ROUNDS * experts))
    slots = experts * cap
    relative = dp == 4 and experts == 8
    heads = width // HEAD_DIM
    def pack(guide, *arrays):
        wide = len(arrays) * width + (LANES if guide.dtype == jnp.int32 else 0)
        return call(
            pack_kernel,
            (jax.ShapeDtypeStruct((tok, tok), BF16),) + (jax.ShapeDtypeStruct((tok // dp, wide), BF16),) * dp,
            guide,
            *arrays,
            vmem=PACK_BYTES,
        )

    def spread(parts):
        return [
            lax.ppermute(part, "dp", [(i, (i + n) % dp) for i in range(dp)]) if n else part
            for n, part in enumerate(parts)
        ]

    order, *packed = pack(pack_pos.reshape(1, tok), keys, queries)
    _, *packed_later = pack(order, values, pivot_states)
    seg_q, taken, give, kept, kept_later = call(
        functools.partial(slots_kernel, cap, experts, relative),
        (
            jax.ShapeDtypeStruct((tok, tok), F32),
            jax.ShapeDtypeStruct((slots, tok), BF16),
            jax.ShapeDtypeStruct((tok, 2 * slots), BF16),
            jax.ShapeDtypeStruct(packed[0].shape, BF16),
            jax.ShapeDtypeStruct(packed_later[0].shape, BF16),
        ),
        segment_ids,
        expert_ids.T,
        gate_code.T,
        packed[0],
        packed_later[0],
    )
    rows = [kept] + spread(packed)[1:]
    later = [kept_later] + spread(packed_later)[1:]
    place, outside = call(
        functools.partial(place_kernel, 2 * width),
        (jax.ShapeDtypeStruct((tok, tok), BF16), jax.ShapeDtypeStruct((tok, tok), F32)),
        seg_q,
        *rows,
    )
    probs = call(
        probs_kernel,
        jax.ShapeDtypeStruct((heads, tok, tok), BF16),
        place,
        outside,
        *rows,
    )
    mixed = call(mix_kernel, jax.ShapeDtypeStruct((tok, width), F32), probs, *later)
    parts = 2 if relative else 1
    hidden_state, *send = call(
        functools.partial(norm_kernel, parts),
        (jax.ShapeDtypeStruct((tok, width), F32),)
        + (jax.ShapeDtypeStruct((slots // parts, width), BF16),) * parts,
        place,
        taken,
        ln_gain.reshape(1, width),
        ln_bias.reshape(1, width),
        mixed,
        *later,
    )

    def over_experts(x):
        x = x.reshape(experts, cap, width)
        return lax.all_to_all(x, "expert", split_axis=0, concat_axis=0, tiled=True).reshape(slots, width)

    def bf16(rows):
        return jax.ShapeDtypeStruct((rows, width), BF16)

    def apply(rows, after=()):
        count = sum(x.shape[0] for x in rows)
        return call(
            functools.partial(expert_kernel, len(rows)),
            tuple(bf16(x.shape[0]) for x in rows),
            b_in,
            w_in,
            w_out,
            *rows,
            *after,
            flops=4 * count * width * w_in.shape[2],
        )

    def swap(x, distance, axis="dp"):
        return lax.ppermute(x, axis, [(i, i ^ distance) for i in range(lax.axis_size(axis))])

    if relative:
        half = slots // 2
        pieces = call(
            functools.partial(pair_kernel, cap), (bf16(2 * cap),) * 4, send[0], swap(send[1], 1, "expert")
        )
        pieces = [swap(x, 2 * n, "expert") if n else x for n, x in enumerate(pieces)]
        own = [call(join_kernel, bf16(half), *pieces[n : n + 2]) for n in (2, 0)]
        far = [swap(x, 2) for x in own]
        near = [swap(x, 1) for x in own]
        own_share, near_shares, last = [None, None], [None, None], ()
        for n in (1, 0):
            own_share[n], near_shares[n] = apply([own[n], near[n]], after=last)
            last = own_share[n : n + 1]
        last = last[0]
        *corner_share, far_first, far_second = apply([swap(x, 1) for x in far] + far, after=[last])
        far_shares = [far_first, far_second]
        near_shares = [swap(x, 1) for x in near_shares]
        backs = [None, None]
        for n in (1, 0):
            pair = swap(call(add_kernel, bf16(half), swap(corner_share[n], 1), far_shares[n]), 2)
            backs[n] = call(
                functools.partial(result_kernel, 0),
                (bf16(2 * cap),) * 2,
                b_out,
                near_shares[n],
                own_share[n],
                pair,
            )
        pieces = [x for n in (1, 0) for x in backs[n]]
        pieces = [swap(x, 2 * n, "expert") if n else x for n, x in enumerate(pieces)]
        mine, other = call(functools.partial(part_kernel, cap), (bf16(half),) * 2, *pieces)
        returned = [mine, swap(other, 1, "expert")]
    else:
        every = lax.all_gather(over_experts(send[0]), "dp", axis=0, tiled=True)
        (share,) = apply([every])
        shares = lax.all_to_all(
            share.reshape(dp, slots, width), "dp", split_axis=0, concat_axis=0, tiled=True
        )
        (results,) = call(
            functools.partial(result_kernel, 0), (bf16(slots),), b_out, *[shares[n] for n in range(dp)]
        )
        returned = [over_experts(results)]
    return call(
        combine_kernel, jax.ShapeDtypeStruct((tok, width), BF16), hidden_state, give, *returned
    )


def solution(mesh):
    return jax.shard_map(
        per_device,
        mesh=mesh,
        in_specs=(
            P(("dp", "expert"), None),
            P(("dp", "expert"), None),
            P(("dp", "expert"), None),
            P(("dp", "expert"), None),
            P(("dp", "expert")),
            P(("dp", "expert"), None),
            P(("dp", "expert"), None),
            P(("dp", "expert"), None),
            P(),
            P(),
            P("expert", None, "dp"),
            P("expert", "dp"),
            P("expert", "dp", None),
            P(),
        ),
        out_specs=P(("dp", "expert"), None),
        check_vma=False,
    )
```

```python
import functools
import math

import jax
import jax.numpy as jnp
from jax import lax
from jax.experimental import pallas as pl
from jax.experimental.pallas import tpu as pltpu
from jax.sharding import PartitionSpec as P

HEAD_DIM = 128
ROUNDS = 4
LANES = 128

epsilon = 1e-05
mask_fill = -1e30

F32 = jnp.float32
BF16 = jnp.bfloat16

VMEM_BYTES = 32 * 1024 * 1024
PACK_BYTES = 62 * 1024 * 1024


def iota(shape, axis):
    return lax.broadcasted_iota(jnp.int32, shape, axis)


def one_hot(condition):
    return jnp.where(condition, 1.0, 0.0)


def across(row, rows):
    lanes = jnp.broadcast_to(row.astype(F32), (rows, row.shape[1]))
    return lanes, lanes.T


def call(body, out_shape, *operands, flops=0, vmem=VMEM_BYTES):
    moved = sum(x.size * x.dtype.itemsize for x in operands)
    moved += sum(x.size * x.dtype.itemsize for x in jax.tree.leaves(out_shape))
    return pl.pallas_call(
        body,
        out_shape=out_shape,
        compiler_params=pltpu.CompilerParams(vmem_limit_bytes=vmem),
        cost_estimate=pl.CostEstimate(flops=flops, bytes_accessed=moved, transcendentals=0),
    )(*operands)


def pack_kernel(pos_ref, *refs):
    parts = lax.axis_size("dp")
    *x_refs, order_ref = refs[: len(refs) - parts]
    out_refs = refs[len(refs) - parts :]
    tok = order_ref.shape[0]
    share = tok // parts

    def sort(x, at):
        rows = jnp.dot(order, x, preferred_element_type=F32).astype(BF16)
        for n, out_ref in enumerate(out_refs):
            out_ref[:, at : at + x.shape[1]] = rows[n * share : (n + 1) * share]

    if pos_ref.dtype == jnp.int32:
        pos = lax.rem(pos_ref[...] + (parts - lax.axis_index("dp")) * tok, parts * tok)
        lanes, subl = across(pos, tok)
        rank = jnp.sum(one_hot(subl < lanes), axis=0, keepdims=True)
        order = one_hot(iota((tok, tok), 0).astype(F32) == rank).astype(BF16)
        _, offset = across(lax.rem(pos, tok), tok)
        sort(offset.astype(BF16), sum(x.shape[1] for x in x_refs))
    else:
        order = pos_ref[...]
    order_ref[...] = order
    at = 0
    for x_ref in x_refs:
        sort(x_ref[...], at)
        at += x_ref.shape[1]


def joined(refs, columns=slice(None)):
    return jnp.concatenate([r[:, columns] for r in refs], axis=0)


def slots_of(ids, cap, experts):
    tok = ids.shape[1]
    first, first_t = across(ids[0:1, :], tok)
    second, second_t = across(ids[1:2, :], tok)
    earlier = iota((tok, tok), 0) < iota((tok, tok), 1)
    rank_first = jnp.sum(one_hot((first_t == first) & earlier), axis=0, keepdims=True)
    rank_second = jnp.sum(one_hot(first_t == second), axis=0, keepdims=True)
    rank_second += jnp.sum(one_hot((second_t == second) & earlier), axis=0, keepdims=True)

    def slot(expert, rank):
        return jnp.where((expert < experts) & (rank < cap), expert * cap + rank, -1.0)

    return slot(first[0:1, :], rank_first), slot(second[0:1, :], rank_second)


def slots_kernel(cap, experts, relative, seg_ref, ids_ref, code_ref, own_ref, own_later_ref, *refs):
    seg_q_ref, taken_ref, give_ref, kept_ref, kept_later_ref = refs
    kept_ref[...] = own_ref[...]
    kept_later_ref[...] = own_later_ref[...]
    tok = seg_ref.shape[1]
    _, seg_q_ref[...] = across(seg_ref[...], tok)
    ids = ids_ref[...]
    if relative:
        other = ids ^ lax.axis_index("expert")
        ids = jnp.where(ids < experts, (other & 1) * (experts // 2) + (other >> 1), ids)
    slot_first, slot_second = slots_of(ids, cap, experts)
    slot = iota((experts * cap, tok), 0).astype(F32)
    taken_ref[...] = one_hot((slot == slot_first) | (slot == slot_second)).astype(BF16)
    high = (code_ref[...] >> 8).astype(F32)
    low = (code_ref[...] & 255).astype(F32)

    def weights(code):
        return jnp.where(slot == slot_first, code[0:1, :], 0.0) + jnp.where(
            slot == slot_second, code[1:2, :], 0.0
        )

    both = jnp.concatenate([weights(high) / 256.0, weights(low) / 65536.0], axis=0)
    give_ref[...] = both.T.astype(BF16)


def place_kernel(first, seg_q_ref, *refs):
    *row_refs, place_ref, outside_ref = refs
    seg_q = seg_q_ref[...]
    offset = joined(row_refs, slice(first, first + LANES)).astype(F32).T
    place = offset == iota(offset.shape, 0).astype(F32)
    place_ref[...] = one_hot(place).astype(BF16)
    seg_k = jnp.sum(jnp.where(place, seg_q, 0.0), axis=0, keepdims=True)
    outside_ref[...] = one_hot(seg_q != seg_k)


def probs_kernel(place_ref, outside_ref, *refs):
    *row_refs, out_ref = refs
    width = out_ref.shape[0] * HEAD_DIM
    scale = 1.0 / math.sqrt(HEAD_DIM)
    outside = outside_ref[...] > 0.0
    for h in range(out_ref.shape[0]):
        lo = h * HEAD_DIM
        k = joined(row_refs, slice(lo, lo + HEAD_DIM))
        q = joined(row_refs, slice(width + lo, width + lo + HEAD_DIM))
        q = jnp.dot(place_ref[...], q, preferred_element_type=F32).astype(BF16)
        scores = lax.dot_general(q, k, (((1,), (1,)), ((), ())), preferred_element_type=F32)
        scores = jnp.where(outside, mask_fill, scores * scale)
        terms = jnp.exp(scores - jnp.max(scores, axis=1, keepdims=True))
        out_ref[h] = (terms / jnp.sum(terms, axis=1, keepdims=True)).astype(BF16)


def mix_kernel(probs_ref, *refs):
    *value_refs, out_ref = refs
    width = out_ref.shape[1]
    for h in range(probs_ref.shape[0]):
        lo = h * HEAD_DIM
        values = joined(value_refs, slice(lo, lo + HEAD_DIM))
        out_ref[:, lo : lo + HEAD_DIM] = jnp.dot(probs_ref[h], values, preferred_element_type=F32)


def norm_kernel(parts, place_ref, taken_ref, gain_ref, bias_ref, mixed_ref, *refs):
    state_refs, hidden_ref, send_refs = refs[: -parts - 1], refs[-parts - 1], refs[-parts:]
    hidden = mixed_ref[...] + jnp.dot(
        place_ref[...], joined(state_refs, slice(mixed_ref.shape[1], None)), preferred_element_type=F32
    )
    hidden_ref[...] = hidden
    centered = hidden - jnp.mean(hidden, axis=1, keepdims=True)
    variance = jnp.mean(centered * centered, axis=1, keepdims=True)
    normed = (centered * lax.rsqrt(variance + epsilon) * gain_ref[...] + bias_ref[...]).astype(BF16)
    picked = jnp.dot(taken_ref[...], normed, preferred_element_type=F32).astype(BF16)
    at = 0
    for send_ref in send_refs:
        send_ref[...] = picked[at : at + send_ref.shape[0]]
        at += send_ref.shape[0]


def expert_kernel(count, bias_ref, w_in_ref, w_out_ref, *refs):
    x_refs, out_refs = refs[:count], refs[-count:]
    inner = jnp.dot(joined(x_refs), w_in_ref[0], preferred_element_type=F32)
    inner = jnp.maximum(inner + bias_ref[...], 0.0).astype(BF16)
    share = jnp.dot(inner, w_out_ref[0], preferred_element_type=F32).astype(BF16)
    at = 0
    for out_ref in out_refs:
        out_ref[...] = share[at : at + out_ref.shape[0]]
        at += out_ref.shape[0]


def add_kernel(first_ref, second_ref, *refs):
    count = len(refs) // 2
    refs[count][...] = (first_ref[...].astype(F32) + second_ref[...].astype(F32)).astype(BF16)
    for n in range(count):
        refs[count + 1 + n][...] = refs[n][...]


def result_kernel(lower, bias_ref, near_ref, *refs):
    count = refs[0].shape[0]
    outs = next(n for n in range(1, len(refs)) if sum(r.shape[0] for r in refs[-n:]) == count)
    total = near_ref[lower : lower + count].astype(F32)
    for share_ref in refs[:-outs]:
        total += share_ref[...].astype(F32)
    row = lax.axis_index("expert") == iota(bias_ref.shape, 0)
    bias = jnp.sum(jnp.where(row, bias_ref[...], 0.0), axis=0, keepdims=True)
    result = (total + bias).astype(BF16)
    at = 0
    for out_ref in refs[-outs:]:
        out_ref[...] = result[at : at + out_ref.shape[0]]
        at += out_ref.shape[0]


def join_kernel(*refs):
    refs[-1][...] = joined(refs[:-1])


def pair_kernel(cap, mine_ref, other_ref, *piece_refs):
    mine, other = mine_ref[...].astype(F32), other_ref[...].astype(F32)
    for n, piece_ref in enumerate(piece_refs):
        rows = slice(n * cap, (n + 1) * cap)
        piece_ref[...] = jnp.concatenate([mine[rows], other[rows]], axis=0).astype(BF16)


def part_kernel(cap, *refs):
    *piece_refs, mine_ref, other_ref = refs
    pieces = [piece_ref[...].astype(F32) for piece_ref in piece_refs]
    mine_ref[...] = jnp.concatenate([piece[:cap] for piece in pieces], axis=0).astype(BF16)
    other_ref[...] = jnp.concatenate([piece[cap:] for piece in pieces], axis=0).astype(BF16)


def combine_kernel(hidden_ref, give_ref, *refs):
    *result_refs, out_ref = refs
    result = joined(list(result_refs) * 2)
    added = jnp.dot(give_ref[...], result, preferred_element_type=F32)
    out_ref[...] = (hidden_ref[...] + added).astype(BF16)


def per_device(
    pivot_states,
    queries,
    keys,
    values,
    pack_pos,
    segment_ids,
    expert_ids,
    gate_code,
    ln_gain,
    ln_bias,
    w_in,
    b_in,
    w_out,
    b_out,
):
    tok, width = pivot_states.shape
    dp = lax.axis_size("dp")
    experts = lax.axis_size("expert")
    cap = max(2, 2 * tok // (ROUNDS * experts))
    slots = experts * cap
    relative = dp == 4 and experts == 8
    heads = width // HEAD_DIM
    def pack(guide, *arrays):
        wide = len(arrays) * width + (LANES if guide.dtype == jnp.int32 else 0)
        return call(
            pack_kernel,
            (jax.ShapeDtypeStruct((tok, tok), BF16),) + (jax.ShapeDtypeStruct((tok // dp, wide), BF16),) * dp,
            guide,
            *arrays,
            vmem=PACK_BYTES,
        )

    def spread(parts):
        return [
            lax.ppermute(part, "dp", [(i, (i + n) % dp) for i in range(dp)]) if n else part
            for n, part in enumerate(parts)
        ]

    order, *packed = pack(pack_pos.reshape(1, tok), keys, queries)
    _, *packed_later = pack(order, values, pivot_states)
    seg_q, taken, give, kept, kept_later = call(
        functools.partial(slots_kernel, cap, experts, relative),
        (
            jax.ShapeDtypeStruct((tok, tok), F32),
            jax.ShapeDtypeStruct((slots, tok), BF16),
            jax.ShapeDtypeStruct((tok, 2 * slots), BF16),
            jax.ShapeDtypeStruct(packed[0].shape, BF16),
            jax.ShapeDtypeStruct(packed_later[0].shape, BF16),
        ),
        segment_ids,
        expert_ids.T,
        gate_code.T,
        packed[0],
        packed_later[0],
    )
    rows = [kept] + spread(packed)[1:]
    later = [kept_later] + spread(packed_later)[1:]
    place, outside = call(
        functools.partial(place_kernel, 2 * width),
        (jax.ShapeDtypeStruct((tok, tok), BF16), jax.ShapeDtypeStruct((tok, tok), F32)),
        seg_q,
        *rows,
    )
    probs = call(
        probs_kernel,
        jax.ShapeDtypeStruct((heads, tok, tok), BF16),
        place,
        outside,
        *rows,
    )
    mixed = call(mix_kernel, jax.ShapeDtypeStruct((tok, width), F32), probs, *later)
    parts = 2 if relative else 1
    hidden_state, *send = call(
        functools.partial(norm_kernel, parts),
        (jax.ShapeDtypeStruct((tok, width), F32),)
        + (jax.ShapeDtypeStruct((slots // parts, width), BF16),) * parts,
        place,
        taken,
        ln_gain.reshape(1, width),
        ln_bias.reshape(1, width),
        mixed,
        *later,
    )

    def over_experts(x):
        x = x.reshape(experts, cap, width)
        return lax.all_to_all(x, "expert", split_axis=0, concat_axis=0, tiled=True).reshape(slots, width)

    def bf16(rows):
        return jax.ShapeDtypeStruct((rows, width), BF16)

    def apply(rows, after=()):
        count = sum(x.shape[0] for x in rows)
        return call(
            functools.partial(expert_kernel, len(rows)),
            tuple(bf16(x.shape[0]) for x in rows),
            b_in,
            w_in,
            w_out,
            *rows,
            *after,
            flops=4 * count * width * w_in.shape[2],
        )

    def swap(x, distance, axis="dp"):
        return lax.ppermute(x, axis, [(i, i ^ distance) for i in range(lax.axis_size(axis))])

    if relative:
        half = slots // 2
        pieces = call(
            functools.partial(pair_kernel, cap), (bf16(2 * cap),) * 4, send[0], swap(send[1], 1, "expert")
        )
        pieces = [swap(x, 2 * n, "expert") if n else x for n, x in enumerate(pieces)]
        own = [call(join_kernel, bf16(half), *pieces[n : n + 2]) for n in (2, 0)]
        far = [swap(x, 2) for x in own]
        near = [swap(x, 1) for x in own]
        own_share, near_shares, last = [None, None], [None, None], ()
        for n in (1, 0):
            own_share[n], near_shares[n] = apply([own[n], near[n]], after=last)
            last = own_share[n : n + 1]
        last = last[0]
        *corner_share, far_first, far_second = apply([swap(x, 1) for x in far] + far, after=[last])
        far_shares = [far_first, far_second]
        pairs = [None, None]
        pairs[0], *near_shares = call(
            add_kernel, (bf16(half),) * 3, swap(corner_share[0], 1), far_shares[0], *near_shares
        )
        (pairs[1],) = call(add_kernel, (bf16(half),), swap(corner_share[1], 1), far_shares[1])
        backs = [
            call(
                functools.partial(result_kernel, 0),
                (bf16(2 * cap),) * 2,
                b_out,
                swap(near_shares[n], 1),
                own_share[n],
                swap(pairs[n], 2),
            )
            for n in range(2)
        ]
        pieces = [x for n in (1, 0) for x in backs[n]]
        pieces = [swap(x, 2 * n, "expert") if n else x for n, x in enumerate(pieces)]
        mine, other = call(functools.partial(part_kernel, cap), (bf16(half),) * 2, *pieces)
        returned = [mine, swap(other, 1, "expert")]
    else:
        every = lax.all_gather(over_experts(send[0]), "dp", axis=0, tiled=True)
        (share,) = apply([every])
        shares = lax.all_to_all(
            share.reshape(dp, slots, width), "dp", split_axis=0, concat_axis=0, tiled=True
        )
        (results,) = call(
            functools.partial(result_kernel, 0), (bf16(slots),), b_out, *[shares[n] for n in range(dp)]
        )
        returned = [over_experts(results)]
    return call(
        combine_kernel, jax.ShapeDtypeStruct((tok, width), BF16), hidden_state, give, *returned
    )


def solution(mesh):
    return jax.shard_map(
        per_device,
        mesh=mesh,
        in_specs=(
            P(("dp", "expert"), None),
            P(("dp", "expert"), None),
            P(("dp", "expert"), None),
            P(("dp", "expert"), None),
            P(("dp", "expert")),
            P(("dp", "expert"), None),
            P(("dp", "expert"), None),
            P(("dp", "expert"), None),
            P(),
            P(),
            P("expert", None, "dp"),
            P("expert", "dp"),
            P("expert", "dp", None),
            P(),
        ),
        out_specs=P(("dp", "expert"), None),
        check_vma=False,
    )
```

```python
import functools
import math

import jax
import jax.numpy as jnp
from jax import lax
from jax.experimental import pallas as pl
from jax.experimental.pallas import tpu as pltpu
from jax.sharding import PartitionSpec as P

HEAD_DIM = 128
ROUNDS = 4
LANES = 128

epsilon = 1e-05
mask_fill = -1e30

F32 = jnp.float32
BF16 = jnp.bfloat16

VMEM_BYTES = 32 * 1024 * 1024
PACK_BYTES = 62 * 1024 * 1024


def iota(shape, axis):
    return lax.broadcasted_iota(jnp.int32, shape, axis)


def one_hot(condition):
    return jnp.where(condition, 1.0, 0.0)


def across(row, rows):
    lanes = jnp.broadcast_to(row.astype(F32), (rows, row.shape[1]))
    return lanes, lanes.T


def call(body, out_shape, *operands, flops=0, vmem=VMEM_BYTES):
    moved = sum(x.size * x.dtype.itemsize for x in operands)
    moved += sum(x.size * x.dtype.itemsize for x in jax.tree.leaves(out_shape))
    return pl.pallas_call(
        body,
        out_shape=out_shape,
        compiler_params=pltpu.CompilerParams(vmem_limit_bytes=vmem),
        cost_estimate=pl.CostEstimate(flops=flops, bytes_accessed=moved, transcendentals=0),
    )(*operands)


def pack_kernel(pos_ref, *refs):
    parts = lax.axis_size("dp")
    *x_refs, order_ref = refs[: len(refs) - parts]
    out_refs = refs[len(refs) - parts :]
    tok = order_ref.shape[0]
    share = tok // parts

    def sort(x, at):
        rows = jnp.dot(order, x, preferred_element_type=F32).astype(BF16)
        for n, out_ref in enumerate(out_refs):
            out_ref[:, at : at + x.shape[1]] = rows[n * share : (n + 1) * share]

    if pos_ref.dtype == jnp.int32:
        pos = lax.rem(pos_ref[...] + (parts - lax.axis_index("dp")) * tok, parts * tok)
        lanes, subl = across(pos, tok)
        rank = jnp.sum(one_hot(subl < lanes), axis=0, keepdims=True)
        order = one_hot(iota((tok, tok), 0).astype(F32) == rank).astype(BF16)
        _, offset = across(lax.rem(pos, tok), tok)
        sort(offset.astype(BF16), sum(x.shape[1] for x in x_refs))
    else:
        order = pos_ref[...]
    order_ref[...] = order
    at = 0
    for x_ref in x_refs:
        sort(x_ref[...], at)
        at += x_ref.shape[1]


def joined(refs, columns=slice(None)):
    return jnp.concatenate([r[:, columns] for r in refs], axis=0)


def slots_of(ids, cap, experts):
    tok = ids.shape[1]
    first, first_t = across(ids[0:1, :], tok)
    second, second_t = across(ids[1:2, :], tok)
    earlier = iota((tok, tok), 0) < iota((tok, tok), 1)
    rank_first = jnp.sum(one_hot((first_t == first) & earlier), axis=0, keepdims=True)
    rank_second = jnp.sum(one_hot(first_t == second), axis=0, keepdims=True)
    rank_second += jnp.sum(one_hot((second_t == second) & earlier), axis=0, keepdims=True)

    def slot(expert, rank):
        return jnp.where((expert < experts) & (rank < cap), expert * cap + rank, -1.0)

    return slot(first[0:1, :], rank_first), slot(second[0:1, :], rank_second)


def slots_kernel(cap, experts, relative, seg_ref, ids_ref, code_ref, own_ref, own_later_ref, *refs):
    seg_q_ref, taken_ref, give_ref, kept_ref, kept_later_ref = refs
    kept_ref[...] = own_ref[...]
    kept_later_ref[...] = own_later_ref[...]
    tok = seg_ref.shape[1]
    _, seg_q_ref[...] = across(seg_ref[...], tok)
    ids = ids_ref[...]
    if relative:
        other = ids ^ lax.axis_index("expert")
        ids = jnp.where(ids < experts, (other & 1) * (experts // 2) + (other >> 1), ids)
    slot_first, slot_second = slots_of(ids, cap, experts)
    slot = iota((experts * cap, tok), 0).astype(F32)
    taken_ref[...] = one_hot((slot == slot_first) | (slot == slot_second)).astype(BF16)
    high = (code_ref[...] >> 8).astype(F32)
    low = (code_ref[...] & 255).astype(F32)

    def weights(code):
        return jnp.where(slot == slot_first, code[0:1, :], 0.0) + jnp.where(
            slot == slot_second, code[1:2, :], 0.0
        )

    both = jnp.concatenate([weights(high) / 256.0, weights(low) / 65536.0], axis=0)
    give_ref[...] = both.T.astype(BF16)


def place_kernel(first, seg_q_ref, *refs):
    *row_refs, place_ref, outside_ref = refs
    seg_q = seg_q_ref[...]
    offset = joined(row_refs, slice(first, first + LANES)).astype(F32).T
    place = offset == iota(offset.shape, 0).astype(F32)
    place_ref[...] = one_hot(place).astype(BF16)
    seg_k = jnp.sum(jnp.where(place, seg_q, 0.0), axis=0, keepdims=True)
    outside_ref[...] = one_hot(seg_q != seg_k)


def probs_kernel(place_ref, outside_ref, *refs):
    *row_refs, out_ref = refs
    width = out_ref.shape[0] * HEAD_DIM
    scale = 1.0 / math.sqrt(HEAD_DIM)
    outside = outside_ref[...] > 0.0
    for h in range(out_ref.shape[0]):
        lo = h * HEAD_DIM
        k = joined(row_refs, slice(lo, lo + HEAD_DIM))
        q = joined(row_refs, slice(width + lo, width + lo + HEAD_DIM))
        q = jnp.dot(place_ref[...], q, preferred_element_type=F32).astype(BF16)
        scores = lax.dot_general(q, k, (((1,), (1,)), ((), ())), preferred_element_type=F32)
        scores = jnp.where(outside, mask_fill, scores * scale)
        terms = jnp.exp(scores - jnp.max(scores, axis=1, keepdims=True))
        out_ref[h] = (terms / jnp.sum(terms, axis=1, keepdims=True)).astype(BF16)


def mix_kernel(probs_ref, *refs):
    *value_refs, out_ref = refs
    width = out_ref.shape[1]
    for h in range(probs_ref.shape[0]):
        lo = h * HEAD_DIM
        values = joined(value_refs, slice(lo, lo + HEAD_DIM))
        out_ref[:, lo : lo + HEAD_DIM] = jnp.dot(probs_ref[h], values, preferred_element_type=F32)


def norm_kernel(parts, place_ref, taken_ref, gain_ref, bias_ref, mixed_ref, *refs):
    state_refs, hidden_ref, send_refs = refs[: -parts - 1], refs[-parts - 1], refs[-parts:]
    hidden = mixed_ref[...] + jnp.dot(
        place_ref[...], joined(state_refs, slice(mixed_ref.shape[1], None)), preferred_element_type=F32
    )
    hidden_ref[...] = hidden
    centered = hidden - jnp.mean(hidden, axis=1, keepdims=True)
    variance = jnp.mean(centered * centered, axis=1, keepdims=True)
    normed = (centered * lax.rsqrt(variance + epsilon) * gain_ref[...] + bias_ref[...]).astype(BF16)
    picked = jnp.dot(taken_ref[...], normed, preferred_element_type=F32).astype(BF16)
    at = 0
    for send_ref in send_refs:
        send_ref[...] = picked[at : at + send_ref.shape[0]]
        at += send_ref.shape[0]


def expert_kernel(count, outs, bias_ref, w_in_ref, w_out_ref, *refs):
    x_refs, out_refs = refs[:count], refs[-outs:]
    inner = jnp.dot(joined(x_refs), w_in_ref[0], preferred_element_type=F32)
    inner = jnp.maximum(inner + bias_ref[...], 0.0).astype(BF16)
    share = jnp.dot(inner, w_out_ref[0], preferred_element_type=F32).astype(BF16)
    at = 0
    for out_ref in out_refs:
        out_ref[...] = share[at : at + out_ref.shape[0]]
        at += out_ref.shape[0]


def add_kernel(first_ref, second_ref, *refs):
    count = len(refs) // 2 - 1
    total = (first_ref[...].astype(F32) + second_ref[...].astype(F32)).astype(BF16)
    half = total.shape[0] // 2
    refs[count][...] = total[:half]
    refs[count + 1][...] = total[half:]
    for n in range(count):
        refs[count + 2 + n][...] = refs[n][...]


def result_kernel(lower, bias_ref, near_ref, *refs):
    count = refs[0].shape[0]
    outs = next(n for n in range(1, len(refs)) if sum(r.shape[0] for r in refs[-n:]) == count)
    total = near_ref[lower : lower + count].astype(F32)
    for share_ref in refs[:-outs]:
        total += share_ref[...].astype(F32)
    row = lax.axis_index("expert") == iota(bias_ref.shape, 0)
    bias = jnp.sum(jnp.where(row, bias_ref[...], 0.0), axis=0, keepdims=True)
    result = (total + bias).astype(BF16)
    at = 0
    for out_ref in refs[-outs:]:
        out_ref[...] = result[at : at + out_ref.shape[0]]
        at += out_ref.shape[0]


def join_kernel(*refs):
    refs[-1][...] = joined(refs[:-1])


def pair_kernel(cap, mine_ref, other_ref, *piece_refs):
    mine, other = mine_ref[...].astype(F32), other_ref[...].astype(F32)
    for n, piece_ref in enumerate(piece_refs):
        rows = slice(n * cap, (n + 1) * cap)
        piece_ref[...] = jnp.concatenate([mine[rows], other[rows]], axis=0).astype(BF16)


def part_kernel(cap, *refs):
    *piece_refs, mine_ref, other_ref = refs
    pieces = [piece_ref[...].astype(F32) for piece_ref in piece_refs]
    mine_ref[...] = jnp.concatenate([piece[:cap] for piece in pieces], axis=0).astype(BF16)
    other_ref[...] = jnp.concatenate([piece[cap:] for piece in pieces], axis=0).astype(BF16)


def combine_kernel(hidden_ref, give_ref, *refs):
    *result_refs, out_ref = refs
    result = joined(list(result_refs) * 2)
    added = jnp.dot(give_ref[...], result, preferred_element_type=F32)
    out_ref[...] = (hidden_ref[...] + added).astype(BF16)


def per_device(
    pivot_states,
    queries,
    keys,
    values,
    pack_pos,
    segment_ids,
    expert_ids,
    gate_code,
    ln_gain,
    ln_bias,
    w_in,
    b_in,
    w_out,
    b_out,
):
    tok, width = pivot_states.shape
    dp = lax.axis_size("dp")
    experts = lax.axis_size("expert")
    cap = max(2, 2 * tok // (ROUNDS * experts))
    slots = experts * cap
    relative = dp == 4 and experts == 8
    heads = width // HEAD_DIM
    def pack(guide, *arrays):
        wide = len(arrays) * width + (LANES if guide.dtype == jnp.int32 else 0)
        return call(
            pack_kernel,
            (jax.ShapeDtypeStruct((tok, tok), BF16),) + (jax.ShapeDtypeStruct((tok // dp, wide), BF16),) * dp,
            guide,
            *arrays,
            vmem=PACK_BYTES,
        )

    def spread(parts):
        return [
            lax.ppermute(part, "dp", [(i, (i + n) % dp) for i in range(dp)]) if n else part
            for n, part in enumerate(parts)
        ]

    order, *packed = pack(pack_pos.reshape(1, tok), keys, queries)
    _, *packed_later = pack(order, values, pivot_states)
    seg_q, taken, give, kept, kept_later = call(
        functools.partial(slots_kernel, cap, experts, relative),
        (
            jax.ShapeDtypeStruct((tok, tok), F32),
            jax.ShapeDtypeStruct((slots, tok), BF16),
            jax.ShapeDtypeStruct((tok, 2 * slots), BF16),
            jax.ShapeDtypeStruct(packed[0].shape, BF16),
            jax.ShapeDtypeStruct(packed_later[0].shape, BF16),
        ),
        segment_ids,
        expert_ids.T,
        gate_code.T,
        packed[0],
        packed_later[0],
    )
    rows = [kept] + spread(packed)[1:]
    later = [kept_later] + spread(packed_later)[1:]
    place, outside = call(
        functools.partial(place_kernel, 2 * width),
        (jax.ShapeDtypeStruct((tok, tok), BF16), jax.ShapeDtypeStruct((tok, tok), F32)),
        seg_q,
        *rows,
    )
    probs = call(
        probs_kernel,
        jax.ShapeDtypeStruct((heads, tok, tok), BF16),
        place,
        outside,
        *rows,
    )
    mixed = call(mix_kernel, jax.ShapeDtypeStruct((tok, width), F32), probs, *later)
    parts = 2 if relative else 1
    hidden_state, *send = call(
        functools.partial(norm_kernel, parts),
        (jax.ShapeDtypeStruct((tok, width), F32),)
        + (jax.ShapeDtypeStruct((slots // parts, width), BF16),) * parts,
        place,
        taken,
        ln_gain.reshape(1, width),
        ln_bias.reshape(1, width),
        mixed,
        *later,
    )

    def over_experts(x):
        x = x.reshape(experts, cap, width)
        return lax.all_to_all(x, "expert", split_axis=0, concat_axis=0, tiled=True).reshape(slots, width)

    def bf16(rows):
        return jax.ShapeDtypeStruct((rows, width), BF16)

    def apply(rows, outs, after=()):
        count = sum(x.shape[0] for x in rows)
        return call(
            functools.partial(expert_kernel, len(rows), outs),
            (bf16(count // outs),) * outs,
            b_in,
            w_in,
            w_out,
            *rows,
            *after,
            flops=4 * count * width * w_in.shape[2],
        )

    def swap(x, distance, axis="dp"):
        return lax.ppermute(x, axis, [(i, i ^ distance) for i in range(lax.axis_size(axis))])

    if relative:
        half = slots // 2
        pieces = call(
            functools.partial(pair_kernel, cap), (bf16(2 * cap),) * 4, send[0], swap(send[1], 1, "expert")
        )
        pieces = [swap(x, 2 * n, "expert") if n else x for n, x in enumerate(pieces)]
        own = [call(join_kernel, bf16(half), *pieces[n : n + 2]) for n in (2, 0)]
        far = [swap(x, 2) for x in own]
        near = [swap(x, 1) for x in own]
        own_share, near_shares, last = [None, None], [None, None], ()
        for n in (1, 0):
            own_share[n], near_shares[n] = apply([own[n], near[n]], 2, after=last)
            last = own_share[n : n + 1]
        last = last[0]
        corner_share, far_share = apply([swap(x, 1) for x in far] + far, 2, after=[last])
        *pairs, near_shares[0], near_shares[1] = call(
            add_kernel, (bf16(half),) * 4, swap(corner_share, 1), far_share, *near_shares
        )
        backs = [
            call(
                functools.partial(result_kernel, 0),
                (bf16(2 * cap),) * 2,
                b_out,
                swap(near_shares[n], 1),
                own_share[n],
                swap(pairs[n], 2),
            )
            for n in range(2)
        ]
        pieces = [x for n in (1, 0) for x in backs[n]]
        pieces = [swap(x, 2 * n, "expert") if n else x for n, x in enumerate(pieces)]
        mine, other = call(functools.partial(part_kernel, cap), (bf16(half),) * 2, *pieces)
        returned = [mine, swap(other, 1, "expert")]
    else:
        every = lax.all_gather(over_experts(send[0]), "dp", axis=0, tiled=True)
        (share,) = apply([every], 1)
        shares = lax.all_to_all(
            share.reshape(dp, slots, width), "dp", split_axis=0, concat_axis=0, tiled=True
        )
        (results,) = call(
            functools.partial(result_kernel, 0), (bf16(slots),), b_out, *[shares[n] for n in range(dp)]
        )
        returned = [over_experts(results)]
    return call(
        combine_kernel, jax.ShapeDtypeStruct((tok, width), BF16), hidden_state, give, *returned
    )


def solution(mesh):
    return jax.shard_map(
        per_device,
        mesh=mesh,
        in_specs=(
            P(("dp", "expert"), None),
            P(("dp", "expert"), None),
            P(("dp", "expert"), None),
            P(("dp", "expert"), None),
            P(("dp", "expert")),
            P(("dp", "expert"), None),
            P(("dp", "expert"), None),
            P(("dp", "expert"), None),
            P(),
            P(),
            P("expert", None, "dp"),
            P("expert", "dp"),
            P("expert", "dp", None),
            P(),
        ),
        out_specs=P(("dp", "expert"), None),
        check_vma=False,
    )
```

```python
import functools
import math

import jax
import jax.numpy as jnp
from jax import lax
from jax.experimental import pallas as pl
from jax.experimental.pallas import tpu as pltpu
from jax.sharding import PartitionSpec as P

HEAD_DIM = 128
ROUNDS = 4
LANES = 128

epsilon = 1e-05
mask_fill = -1e30

F32 = jnp.float32
BF16 = jnp.bfloat16

VMEM_BYTES = 32 * 1024 * 1024
PACK_BYTES = 62 * 1024 * 1024


def iota(shape, axis):
    return lax.broadcasted_iota(jnp.int32, shape, axis)


def one_hot(condition):
    return jnp.where(condition, 1.0, 0.0)


def across(row, rows):
    lanes = jnp.broadcast_to(row.astype(F32), (rows, row.shape[1]))
    return lanes, lanes.T


def call(body, out_shape, *operands, flops=0, vmem=VMEM_BYTES):
    moved = sum(x.size * x.dtype.itemsize for x in operands)
    moved += sum(x.size * x.dtype.itemsize for x in jax.tree.leaves(out_shape))
    return pl.pallas_call(
        body,
        out_shape=out_shape,
        compiler_params=pltpu.CompilerParams(vmem_limit_bytes=vmem),
        cost_estimate=pl.CostEstimate(flops=flops, bytes_accessed=moved, transcendentals=0),
    )(*operands)


def pack_kernel(pos_ref, *refs):
    parts = lax.axis_size("dp")
    *x_refs, order_ref = refs[: len(refs) - parts]
    out_refs = refs[len(refs) - parts :]
    tok = order_ref.shape[0]
    share = tok // parts

    def sort(x, at):
        rows = jnp.dot(order, x, preferred_element_type=F32).astype(BF16)
        for n, out_ref in enumerate(out_refs):
            out_ref[:, at : at + x.shape[1]] = rows[n * share : (n + 1) * share]

    if pos_ref.dtype == jnp.int32:
        pos = lax.rem(pos_ref[...] + (parts - lax.axis_index("dp")) * tok, parts * tok)
        lanes, subl = across(pos, tok)
        rank = jnp.sum(one_hot(subl < lanes), axis=0, keepdims=True)
        order = one_hot(iota((tok, tok), 0).astype(F32) == rank).astype(BF16)
        _, offset = across(lax.rem(pos, tok), tok)
        sort(offset.astype(BF16), sum(x.shape[1] for x in x_refs))
    else:
        order = pos_ref[...]
    order_ref[...] = order
    at = 0
    for x_ref in x_refs:
        sort(x_ref[...], at)
        at += x_ref.shape[1]


def joined(refs, columns=slice(None)):
    return jnp.concatenate([r[:, columns] for r in refs], axis=0)


def slots_of(ids, cap, experts):
    tok = ids.shape[1]
    first, first_t = across(ids[0:1, :], tok)
    second, second_t = across(ids[1:2, :], tok)
    earlier = iota((tok, tok), 0) < iota((tok, tok), 1)
    rank_first = jnp.sum(one_hot((first_t == first) & earlier), axis=0, keepdims=True)
    rank_second = jnp.sum(one_hot(first_t == second), axis=0, keepdims=True)
    rank_second += jnp.sum(one_hot((second_t == second) & earlier), axis=0, keepdims=True)

    def slot(expert, rank):
        return jnp.where((expert < experts) & (rank < cap), expert * cap + rank, -1.0)

    return slot(first[0:1, :], rank_first), slot(second[0:1, :], rank_second)


def slots_kernel(cap, experts, relative, seg_ref, ids_ref, code_ref, own_ref, own_later_ref, *refs):
    seg_q_ref, taken_ref, give_ref, kept_ref, kept_later_ref = refs
    kept_ref[...] = own_ref[...]
    kept_later_ref[...] = own_later_ref[...]
    tok = seg_ref.shape[1]
    _, seg_q_ref[...] = across(seg_ref[...], tok)
    ids = ids_ref[...]
    if relative:
        other = ids ^ lax.axis_index("expert")
        ids = jnp.where(ids < experts, (other & 1) * (experts // 2) + (other >> 1), ids)
    slot_first, slot_second = slots_of(ids, cap, experts)
    slot = iota((experts * cap, tok), 0).astype(F32)
    taken_ref[...] = one_hot((slot == slot_first) | (slot == slot_second)).astype(BF16)
    high = (code_ref[...] >> 8).astype(F32)
    low = (code_ref[...] & 255).astype(F32)

    def weights(code):
        return jnp.where(slot == slot_first, code[0:1, :], 0.0) + jnp.where(
            slot == slot_second, code[1:2, :], 0.0
        )

    both = jnp.concatenate([weights(high) / 256.0, weights(low) / 65536.0], axis=0)
    give_ref[...] = both.T.astype(BF16)


def place_kernel(first, seg_q_ref, *refs):
    *row_refs, place_ref, outside_ref = refs
    seg_q = seg_q_ref[...]
    offset = joined(row_refs, slice(first, first + LANES)).astype(F32).T
    place = offset == iota(offset.shape, 0).astype(F32)
    place_ref[...] = one_hot(place).astype(BF16)
    seg_k = jnp.sum(jnp.where(place, seg_q, 0.0), axis=0, keepdims=True)
    outside_ref[...] = one_hot(seg_q != seg_k)


def probs_kernel(place_ref, outside_ref, *refs):
    *row_refs, out_ref = refs
    width = out_ref.shape[0] * HEAD_DIM
    scale = 1.0 / math.sqrt(HEAD_DIM)
    outside = outside_ref[...] > 0.0
    for h in range(out_ref.shape[0]):
        lo = h * HEAD_DIM
        k = joined(row_refs, slice(lo, lo + HEAD_DIM))
        q = joined(row_refs, slice(width + lo, width + lo + HEAD_DIM))
        q = jnp.dot(place_ref[...], q, preferred_element_type=F32).astype(BF16)
        scores = lax.dot_general(q, k, (((1,), (1,)), ((), ())), preferred_element_type=F32)
        scores = jnp.where(outside, mask_fill, scores * scale)
        terms = jnp.exp(scores - jnp.max(scores, axis=1, keepdims=True))
        out_ref[h] = (terms / jnp.sum(terms, axis=1, keepdims=True)).astype(BF16)


def norm_kernel(parts, place_ref, taken_ref, gain_ref, bias_ref, probs_ref, *refs):
    row_refs, hidden_ref, send_refs = refs[: -parts - 1], refs[-parts - 1], refs[-parts:]
    width = hidden_ref.shape[1]
    for h in range(probs_ref.shape[0]):
        lo = h * HEAD_DIM
        values = joined(row_refs, slice(lo, lo + HEAD_DIM))
        states = joined(row_refs, slice(width + lo, width + lo + HEAD_DIM))
        hidden_ref[:, lo : lo + HEAD_DIM] = jnp.dot(
            probs_ref[h], values, preferred_element_type=F32
        ) + jnp.dot(place_ref[...], states, preferred_element_type=F32)
    hidden = hidden_ref[...]
    centered = hidden - jnp.mean(hidden, axis=1, keepdims=True)
    variance = jnp.mean(centered * centered, axis=1, keepdims=True)
    normed = (centered * lax.rsqrt(variance + epsilon) * gain_ref[...] + bias_ref[...]).astype(BF16)
    picked = jnp.dot(taken_ref[...], normed, preferred_element_type=F32).astype(BF16)
    at = 0
    for send_ref in send_refs:
        send_ref[...] = picked[at : at + send_ref.shape[0]]
        at += send_ref.shape[0]


def expert_kernel(count, bias_ref, w_in_ref, w_out_ref, *refs):
    x_refs, out_refs = refs[:count], refs[-count:]
    inner = jnp.dot(joined(x_refs), w_in_ref[0], preferred_element_type=F32)
    inner = jnp.maximum(inner + bias_ref[...], 0.0).astype(BF16)
    share = jnp.dot(inner, w_out_ref[0], preferred_element_type=F32).astype(BF16)
    at = 0
    for out_ref in out_refs:
        out_ref[...] = share[at : at + out_ref.shape[0]]
        at += out_ref.shape[0]


def add_kernel(first_ref, second_ref, out_ref):
    out_ref[...] = (first_ref[...].astype(F32) + second_ref[...].astype(F32)).astype(BF16)


def hand_kernel(first_ref, second_ref, _, *out_refs):
    rows = out_refs[0].shape[0]
    for n, out_ref in enumerate(out_refs):
        source_ref = (first_ref, second_ref)[n // 2]
        out_ref[...] = source_ref[n % 2 * rows : (n % 2 + 1) * rows]


def result_kernel(lower, bias_ref, near_ref, *refs):
    count = refs[0].shape[0]
    outs = next(n for n in range(1, len(refs)) if sum(r.shape[0] for r in refs[-n:]) == count)
    total = near_ref[lower : lower + count].astype(F32)
    for share_ref in refs[:-outs]:
        total += share_ref[...].astype(F32)
    row = lax.axis_index("expert") == iota(bias_ref.shape, 0)
    bias = jnp.sum(jnp.where(row, bias_ref[...], 0.0), axis=0, keepdims=True)
    result = (total + bias).astype(BF16)
    at = 0
    for out_ref in refs[-outs:]:
        out_ref[...] = result[at : at + out_ref.shape[0]]
        at += out_ref.shape[0]


def join_kernel(*refs):
    refs[-1][...] = joined(refs[:-1])


def pair_kernel(cap, mine_ref, other_ref, *piece_refs):
    mine, other = mine_ref[...].astype(F32), other_ref[...].astype(F32)
    for n, piece_ref in enumerate(piece_refs):
        rows = slice(n * cap, (n + 1) * cap)
        piece_ref[...] = jnp.concatenate([mine[rows], other[rows]], axis=0).astype(BF16)


def part_kernel(cap, *refs):
    *piece_refs, mine_ref, other_ref = refs
    pieces = [piece_ref[...].astype(F32) for piece_ref in piece_refs]
    mine_ref[...] = jnp.concatenate([piece[:cap] for piece in pieces], axis=0).astype(BF16)
    other_ref[...] = jnp.concatenate([piece[cap:] for piece in pieces], axis=0).astype(BF16)


def combine_kernel(hidden_ref, give_ref, *refs):
    *result_refs, out_ref = refs
    result = joined(list(result_refs) * 2)
    added = jnp.dot(give_ref[...], result, preferred_element_type=F32)
    out_ref[...] = (hidden_ref[...] + added).astype(BF16)


def per_device(
    pivot_states,
    queries,
    keys,
    values,
    pack_pos,
    segment_ids,
    expert_ids,
    gate_code,
    ln_gain,
    ln_bias,
    w_in,
    b_in,
    w_out,
    b_out,
):
    tok, width = pivot_states.shape
    dp = lax.axis_size("dp")
    experts = lax.axis_size("expert")
    cap = max(2, 2 * tok // (ROUNDS * experts))
    slots = experts * cap
    relative = dp == 4 and experts == 8
    heads = width // HEAD_DIM
    def pack(guide, *arrays):
        wide = len(arrays) * width + (LANES if guide.dtype == jnp.int32 else 0)
        return call(
            pack_kernel,
            (jax.ShapeDtypeStruct((tok, tok), BF16),) + (jax.ShapeDtypeStruct((tok // dp, wide), BF16),) * dp,
            guide,
            *arrays,
            vmem=PACK_BYTES,
        )

    def spread(parts):
        return [
            lax.ppermute(part, "dp", [(i, (i + n) % dp) for i in range(dp)]) if n else part
            for n, part in enumerate(parts)
        ]

    order, *packed = pack(pack_pos.reshape(1, tok), keys, queries)
    _, *packed_later = pack(order, values, pivot_states)
    seg_q, taken, give, kept, kept_later = call(
        functools.partial(slots_kernel, cap, experts, relative),
        (
            jax.ShapeDtypeStruct((tok, tok), F32),
            jax.ShapeDtypeStruct((slots, tok), BF16),
            jax.ShapeDtypeStruct((tok, 2 * slots), BF16),
            jax.ShapeDtypeStruct(packed[0].shape, BF16),
            jax.ShapeDtypeStruct(packed_later[0].shape, BF16),
        ),
        segment_ids,
        expert_ids.T,
        gate_code.T,
        packed[0],
        packed_later[0],
    )
    rows = [kept] + spread(packed)[1:]
    later = [kept_later] + spread(packed_later)[1:]
    place, outside = call(
        functools.partial(place_kernel, 2 * width),
        (jax.ShapeDtypeStruct((tok, tok), BF16), jax.ShapeDtypeStruct((tok, tok), F32)),
        seg_q,
        *rows,
    )
    probs = call(
        probs_kernel,
        jax.ShapeDtypeStruct((heads, tok, tok), BF16),
        place,
        outside,
        *rows,
    )
    parts = 2 if relative else 1
    hidden_state, *send = call(
        functools.partial(norm_kernel, parts),
        (jax.ShapeDtypeStruct((tok, width), F32),)
        + (jax.ShapeDtypeStruct((slots // parts, width), BF16),) * parts,
        place,
        taken,
        ln_gain.reshape(1, width),
        ln_bias.reshape(1, width),
        probs,
        *later,
    )

    def over_experts(x):
        x = x.reshape(experts, cap, width)
        return lax.all_to_all(x, "expert", split_axis=0, concat_axis=0, tiled=True).reshape(slots, width)

    def bf16(rows):
        return jax.ShapeDtypeStruct((rows, width), BF16)

    def apply(rows, after=()):
        count = sum(x.shape[0] for x in rows)
        return call(
            functools.partial(expert_kernel, len(rows)),
            tuple(bf16(x.shape[0]) for x in rows),
            b_in,
            w_in,
            w_out,
            *rows,
            *after,
            flops=4 * count * width * w_in.shape[2],
        )

    def swap(x, distance, axis="dp"):
        return lax.ppermute(x, axis, [(i, i ^ distance) for i in range(lax.axis_size(axis))])

    if relative:
        half = slots // 2
        pieces = call(
            functools.partial(pair_kernel, cap), (bf16(2 * cap),) * 4, send[0], swap(send[1], 1, "expert")
        )
        pieces = [swap(x, 2 * n, "expert") if n else x for n, x in enumerate(pieces)]
        own = [call(join_kernel, bf16(half), *pieces[n : n + 2]) for n in (2, 0)]
        far = [swap(x, 2) for x in own]
        near = [swap(x, 1) for x in own]
        own_share, near_shares, last = [None, None], [None, None], ()
        for n in (1, 0):
            own_share[n], near_shares[n] = apply([own[n], near[n]], after=last)
            last = own_share[n : n + 1]
        last = last[0]
        *corner_share, far_first, far_second = apply([swap(x, 1) for x in far] + far, after=[last])
        far_shares = [far_first, far_second]
        first_pair = call(add_kernel, bf16(half), swap(corner_share[0], 1), far_shares[0])
        second_pair = call(add_kernel, bf16(half), swap(corner_share[1], 1), far_shares[1])
        near_parts = call(hand_kernel, (bf16(half // 2),) * 4, *near_shares, first_pair)
        near_parts = [swap(x, 1) for x in near_parts]
        near_shares = [call(join_kernel, bf16(half), *near_parts[n : n + 2]) for n in (0, 2)]
        pairs = [first_pair, second_pair]
        backs = [
            call(
                functools.partial(result_kernel, 0),
                (bf16(2 * cap),) * 2,
                b_out,
                near_shares[n],
                own_share[n],
                swap(pairs[n], 2),
            )
            for n in range(2)
        ]
        pieces = [x for n in (1, 0) for x in backs[n]]
        pieces = [swap(x, 2 * n, "expert") if n else x for n, x in enumerate(pieces)]
        mine, other = call(functools.partial(part_kernel, cap), (bf16(half),) * 2, *pieces)
        returned = [mine, swap(other, 1, "expert")]
    else:
        every = lax.all_gather(over_experts(send[0]), "dp", axis=0, tiled=True)
        (share,) = apply([every])
        shares = lax.all_to_all(
            share.reshape(dp, slots, width), "dp", split_axis=0, concat_axis=0, tiled=True
        )
        (results,) = call(
            functools.partial(result_kernel, 0), (bf16(slots),), b_out, *[shares[n] for n in range(dp)]
        )
        returned = [over_experts(results)]
    return call(
        combine_kernel, jax.ShapeDtypeStruct((tok, width), BF16), hidden_state, give, *returned
    )


def solution(mesh):
    return jax.shard_map(
        per_device,
        mesh=mesh,
        in_specs=(
            P(("dp", "expert"), None),
            P(("dp", "expert"), None),
            P(("dp", "expert"), None),
            P(("dp", "expert"), None),
            P(("dp", "expert")),
            P(("dp", "expert"), None),
            P(("dp", "expert"), None),
            P(("dp", "expert"), None),
            P(),
            P(),
            P("expert", None, "dp"),
            P("expert", "dp"),
            P("expert", "dp", None),
            P(),
        ),
        out_specs=P(("dp", "expert"), None),
        check_vma=False,
    )
```

```python
import functools
import math

import jax
import jax.numpy as jnp
from jax import lax
from jax.experimental import pallas as pl
from jax.experimental.pallas import tpu as pltpu
from jax.sharding import PartitionSpec as P

HEAD_DIM = 128
ROUNDS = 4
LANES = 128
OUT_PARTS = 4

epsilon = 1e-05
mask_fill = -1e30

F32 = jnp.float32
BF16 = jnp.bfloat16

VMEM_BYTES = 32 * 1024 * 1024
PACK_BYTES = 62 * 1024 * 1024


def iota(shape, axis):
    return lax.broadcasted_iota(jnp.int32, shape, axis)


def one_hot(condition):
    return jnp.where(condition, 1.0, 0.0)


def across(row, rows):
    lanes = jnp.broadcast_to(row.astype(F32), (rows, row.shape[1]))
    return lanes, lanes.T


def call(body, out_shape, *operands, flops=0, vmem=VMEM_BYTES):
    moved = sum(x.size * x.dtype.itemsize for x in operands)
    moved += sum(x.size * x.dtype.itemsize for x in jax.tree.leaves(out_shape))
    return pl.pallas_call(
        body,
        out_shape=out_shape,
        compiler_params=pltpu.CompilerParams(vmem_limit_bytes=vmem),
        cost_estimate=pl.CostEstimate(flops=flops, bytes_accessed=moved, transcendentals=0),
    )(*operands)


def pack_kernel(pos_ref, *refs):
    parts = lax.axis_size("dp")
    *x_refs, order_ref = refs[: len(refs) - parts]
    out_refs = refs[len(refs) - parts :]
    tok = order_ref.shape[0]
    share = tok // parts

    def sort(x, at):
        rows = jnp.dot(order, x, preferred_element_type=F32).astype(BF16)
        for n, out_ref in enumerate(out_refs):
            out_ref[:, at : at + x.shape[1]] = rows[n * share : (n + 1) * share]

    if pos_ref.dtype == jnp.int32:
        pos = lax.rem(pos_ref[...] + (parts - lax.axis_index("dp")) * tok, parts * tok)
        lanes, subl = across(pos, tok)
        rank = jnp.sum(one_hot(subl < lanes), axis=0, keepdims=True)
        order = one_hot(iota((tok, tok), 0).astype(F32) == rank).astype(BF16)
        _, offset = across(lax.rem(pos, tok), tok)
        sort(offset.astype(BF16), sum(x.shape[1] for x in x_refs))
    else:
        order = pos_ref[...]
    order_ref[...] = order
    at = 0
    for x_ref in x_refs:
        sort(x_ref[...], at)
        at += x_ref.shape[1]


def joined(refs, columns=slice(None)):
    return jnp.concatenate([r[:, columns] for r in refs], axis=0)


def slots_of(ids, cap, experts):
    tok = ids.shape[1]
    first, first_t = across(ids[0:1, :], tok)
    second, second_t = across(ids[1:2, :], tok)
    earlier = iota((tok, tok), 0) < iota((tok, tok), 1)
    rank_first = jnp.sum(one_hot((first_t == first) & earlier), axis=0, keepdims=True)
    rank_second = jnp.sum(one_hot(first_t == second), axis=0, keepdims=True)
    rank_second += jnp.sum(one_hot((second_t == second) & earlier), axis=0, keepdims=True)

    def slot(expert, rank):
        return jnp.where((expert < experts) & (rank < cap), expert * cap + rank, -1.0)

    return slot(first[0:1, :], rank_first), slot(second[0:1, :], rank_second)


def slots_kernel(cap, experts, relative, seg_ref, ids_ref, code_ref, own_ref, own_later_ref, *refs):
    seg_q_ref, taken_ref, give_ref, kept_ref, kept_later_ref = refs
    kept_ref[...] = own_ref[...]
    kept_later_ref[...] = own_later_ref[...]
    tok = seg_ref.shape[1]
    _, seg_q_ref[...] = across(seg_ref[...], tok)
    ids = ids_ref[...]
    if relative:
        other = ids ^ lax.axis_index("expert")
        ids = jnp.where(ids < experts, (other & 1) * (experts // 2) + (other >> 1), ids)
    slot_first, slot_second = slots_of(ids, cap, experts)
    slot = iota((experts * cap, tok), 0).astype(F32)
    taken_ref[...] = one_hot((slot == slot_first) | (slot == slot_second)).astype(BF16)
    high = (code_ref[...] >> 8).astype(F32)
    low = (code_ref[...] & 255).astype(F32)

    def weights(code):
        return jnp.where(slot == slot_first, code[0:1, :], 0.0) + jnp.where(
            slot == slot_second, code[1:2, :], 0.0
        )

    both = jnp.concatenate([weights(high) / 256.0, weights(low) / 65536.0], axis=0)
    give_ref[...] = both.T.astype(BF16)


def place_kernel(first, seg_q_ref, *refs):
    *row_refs, place_ref, outside_ref = refs
    seg_q = seg_q_ref[...]
    offset = joined(row_refs, slice(first, first + LANES)).astype(F32).T
    place = offset == iota(offset.shape, 0).astype(F32)
    place_ref[...] = one_hot(place).astype(BF16)
    seg_k = jnp.sum(jnp.where(place, seg_q, 0.0), axis=0, keepdims=True)
    outside_ref[...] = one_hot(seg_q != seg_k)


def probs_kernel(place_ref, outside_ref, *refs):
    *row_refs, out_ref = refs
    width = out_ref.shape[0] * HEAD_DIM
    scale = 1.0 / math.sqrt(HEAD_DIM)
    outside = outside_ref[...] > 0.0
    for h in range(out_ref.shape[0]):
        lo = h * HEAD_DIM
        k = joined(row_refs, slice(lo, lo + HEAD_DIM))
        q = joined(row_refs, slice(width + lo, width + lo + HEAD_DIM))
        q = jnp.dot(place_ref[...], q, preferred_element_type=F32).astype(BF16)
        scores = lax.dot_general(q, k, (((1,), (1,)), ((), ())), preferred_element_type=F32)
        scores = jnp.where(outside, mask_fill, scores * scale)
        terms = jnp.exp(scores - jnp.max(scores, axis=1, keepdims=True))
        out_ref[h] = (terms / jnp.sum(terms, axis=1, keepdims=True)).astype(BF16)


def norm_kernel(parts, place_ref, taken_ref, gain_ref, bias_ref, probs_ref, *refs):
    row_refs, hidden_ref, send_refs = refs[: -parts - 1], refs[-parts - 1], refs[-parts:]
    width = hidden_ref.shape[1]
    for h in range(probs_ref.shape[0]):
        lo = h * HEAD_DIM
        values = joined(row_refs, slice(lo, lo + HEAD_DIM))
        states = joined(row_refs, slice(width + lo, width + lo + HEAD_DIM))
        hidden_ref[:, lo : lo + HEAD_DIM] = jnp.dot(
            probs_ref[h], values, preferred_element_type=F32
        ) + jnp.dot(place_ref[...], states, preferred_element_type=F32)
    hidden = hidden_ref[...]
    centered = hidden - jnp.mean(hidden, axis=1, keepdims=True)
    variance = jnp.mean(centered * centered, axis=1, keepdims=True)
    normed = (centered * lax.rsqrt(variance + epsilon) * gain_ref[...] + bias_ref[...]).astype(BF16)
    picked = jnp.dot(taken_ref[...], normed, preferred_element_type=F32).astype(BF16)
    at = 0
    for send_ref in send_refs:
        send_ref[...] = picked[at : at + send_ref.shape[0]]
        at += send_ref.shape[0]


def expert_kernel(count, bias_ref, w_in_ref, w_out_ref, *refs):
    x_refs, out_refs = refs[:count], refs[-count:]
    inner = jnp.dot(joined(x_refs), w_in_ref[0], preferred_element_type=F32)
    inner = jnp.maximum(inner + bias_ref[...], 0.0).astype(BF16)
    share = jnp.dot(inner, w_out_ref[0], preferred_element_type=F32).astype(BF16)
    at = 0
    for out_ref in out_refs:
        out_ref[...] = share[at : at + out_ref.shape[0]]
        at += out_ref.shape[0]


def add_kernel(first_ref, second_ref, out_ref):
    out_ref[...] = (first_ref[...].astype(F32) + second_ref[...].astype(F32)).astype(BF16)


def result_kernel(lower, bias_ref, near_ref, *refs):
    count = refs[0].shape[0]
    outs = next(n for n in range(1, len(refs)) if sum(r.shape[0] for r in refs[-n:]) == count)
    total = near_ref[lower : lower + count].astype(F32)
    for share_ref in refs[:-outs]:
        total += share_ref[...].astype(F32)
    row = lax.axis_index("expert") == iota(bias_ref.shape, 0)
    bias = jnp.sum(jnp.where(row, bias_ref[...], 0.0), axis=0, keepdims=True)
    result = (total + bias).astype(BF16)
    at = 0
    for out_ref in refs[-outs:]:
        out_ref[...] = result[at : at + out_ref.shape[0]]
        at += out_ref.shape[0]


def join_kernel(*refs):
    refs[-1][...] = joined(refs[:-1])


def pair_kernel(cap, mine_ref, other_ref, *piece_refs):
    mine, other = mine_ref[...].astype(F32), other_ref[...].astype(F32)
    for n, piece_ref in enumerate(piece_refs):
        rows = slice(n * cap, (n + 1) * cap)
        piece_ref[...] = jnp.concatenate([mine[rows], other[rows]], axis=0).astype(BF16)


def part_kernel(cap, *refs):
    *piece_refs, mine_ref, other_ref = refs
    pieces = [piece_ref[...].astype(F32) for piece_ref in piece_refs]
    mine_ref[...] = jnp.concatenate([piece[:cap] for piece in pieces], axis=0).astype(BF16)
    other_ref[...] = jnp.concatenate([piece[cap:] for piece in pieces], axis=0).astype(BF16)


def combine_kernel(count, hidden_ref, give_ref, *refs):
    result_refs, out_ref, buf, sem = refs[:count], refs[count], refs[count + 1], refs[count + 2]
    result = joined(list(result_refs) * 2)
    rows = buf.shape[0] // OUT_PARTS
    copies = []
    for n in range(OUT_PARTS):
        part = slice(n * rows, (n + 1) * rows)
        added = jnp.dot(give_ref[part, :], result, preferred_element_type=F32)
        buf[part, :] = (hidden_ref[part, :] + added).astype(BF16)
        copies.append(pltpu.make_async_copy(buf.at[part, :], out_ref.at[part, :], sem.at[n]))
        copies[n].start()
    for copy in copies:
        copy.wait()


def per_device(
    pivot_states,
    queries,
    keys,
    values,
    pack_pos,
    segment_ids,
    expert_ids,
    gate_code,
    ln_gain,
    ln_bias,
    w_in,
    b_in,
    w_out,
    b_out,
):
    tok, width = pivot_states.shape
    dp = lax.axis_size("dp")
    experts = lax.axis_size("expert")
    cap = max(2, 2 * tok // (ROUNDS * experts))
    slots = experts * cap
    relative = dp == 4 and experts == 8
    heads = width // HEAD_DIM
    def pack(guide, *arrays):
        wide = len(arrays) * width + (LANES if guide.dtype == jnp.int32 else 0)
        return call(
            pack_kernel,
            (jax.ShapeDtypeStruct((tok, tok), BF16),) + (jax.ShapeDtypeStruct((tok // dp, wide), BF16),) * dp,
            guide,
            *arrays,
            vmem=PACK_BYTES,
        )

    def spread(parts):
        return [
            lax.ppermute(part, "dp", [(i, (i + n) % dp) for i in range(dp)]) if n else part
            for n, part in enumerate(parts)
        ]

    order, *packed = pack(pack_pos.reshape(1, tok), keys, queries)
    _, *packed_later = pack(order, values, pivot_states)
    seg_q, taken, give, kept, kept_later = call(
        functools.partial(slots_kernel, cap, experts, relative),
        (
            jax.ShapeDtypeStruct((tok, tok), F32),
            jax.ShapeDtypeStruct((slots, tok), BF16),
            jax.ShapeDtypeStruct((tok, 2 * slots), BF16),
            jax.ShapeDtypeStruct(packed[0].shape, BF16),
            jax.ShapeDtypeStruct(packed_later[0].shape, BF16),
        ),
        segment_ids,
        expert_ids.T,
        gate_code.T,
        packed[0],
        packed_later[0],
    )
    rows = [kept] + spread(packed)[1:]
    later = [kept_later] + spread(packed_later)[1:]
    place, outside = call(
        functools.partial(place_kernel, 2 * width),
        (jax.ShapeDtypeStruct((tok, tok), BF16), jax.ShapeDtypeStruct((tok, tok), F32)),
        seg_q,
        *rows,
    )
    probs = call(
        probs_kernel,
        jax.ShapeDtypeStruct((heads, tok, tok), BF16),
        place,
        outside,
        *rows,
    )
    parts = 2 if relative else 1
    hidden_state, *send = call(
        functools.partial(norm_kernel, parts),
        (jax.ShapeDtypeStruct((tok, width), F32),)
        + (jax.ShapeDtypeStruct((slots // parts, width), BF16),) * parts,
        place,
        taken,
        ln_gain.reshape(1, width),
        ln_bias.reshape(1, width),
        probs,
        *later,
    )

    def over_experts(x):
        x = x.reshape(experts, cap, width)
        return lax.all_to_all(x, "expert", split_axis=0, concat_axis=0, tiled=True).reshape(slots, width)

    def bf16(rows):
        return jax.ShapeDtypeStruct((rows, width), BF16)

    def apply(rows, after=()):
        count = sum(x.shape[0] for x in rows)
        return call(
            functools.partial(expert_kernel, len(rows)),
            tuple(bf16(x.shape[0]) for x in rows),
            b_in,
            w_in,
            w_out,
            *rows,
            *after,
            flops=4 * count * width * w_in.shape[2],
        )

    def swap(x, distance, axis="dp"):
        return lax.ppermute(x, axis, [(i, i ^ distance) for i in range(lax.axis_size(axis))])

    if relative:
        half = slots // 2
        pieces = call(
            functools.partial(pair_kernel, cap), (bf16(2 * cap),) * 4, send[0], swap(send[1], 1, "expert")
        )
        pieces = [swap(x, 2 * n, "expert") if n else x for n, x in enumerate(pieces)]
        own = [call(join_kernel, bf16(half), *pieces[n : n + 2]) for n in (2, 0)]
        far = [swap(x, 2) for x in own]
        near = [swap(x, 1) for x in own]
        own_share, near_shares, last = [None, None], [None, None], ()
        for n in (1, 0):
            own_share[n], near_shares[n] = apply([own[n], near[n]], after=last)
            last = own_share[n : n + 1]
        last = last[0]
        *corner_share, far_first, far_second = apply([swap(x, 1) for x in far] + far, after=[last])
        far_shares = [far_first, far_second]
        near_shares = [swap(x, 1) for x in near_shares]
        backs = [None, None]
        for n in (1, 0):
            pair = swap(call(add_kernel, bf16(half), swap(corner_share[n], 1), far_shares[n]), 2)
            backs[n] = call(
                functools.partial(result_kernel, 0),
                (bf16(2 * cap),) * 2,
                b_out,
                near_shares[n],
                own_share[n],
                pair,
            )
        pieces = [x for n in (1, 0) for x in backs[n]]
        pieces = [swap(x, 2 * n, "expert") if n else x for n, x in enumerate(pieces)]
        mine, other = call(functools.partial(part_kernel, cap), (bf16(half),) * 2, *pieces)
        returned = [mine, swap(other, 1, "expert")]
    else:
        every = lax.all_gather(over_experts(send[0]), "dp", axis=0, tiled=True)
        (share,) = apply([every])
        shares = lax.all_to_all(
            share.reshape(dp, slots, width), "dp", split_axis=0, concat_axis=0, tiled=True
        )
        (results,) = call(
            functools.partial(result_kernel, 0), (bf16(slots),), b_out, *[shares[n] for n in range(dp)]
        )
        returned = [over_experts(results)]
    return pl.pallas_call(
        functools.partial(combine_kernel, len(returned)),
        out_shape=jax.ShapeDtypeStruct((tok, width), BF16),
        in_specs=[pl.BlockSpec(memory_space=pltpu.VMEM)] * (2 + len(returned)),
        out_specs=pl.BlockSpec(memory_space=pl.ANY),
        scratch_shapes=[pltpu.VMEM((tok, width), BF16), pltpu.SemaphoreType.DMA((OUT_PARTS,))],
        compiler_params=pltpu.CompilerParams(vmem_limit_bytes=VMEM_BYTES),
    )(hidden_state, give, *returned)


def solution(mesh):
    return jax.shard_map(
        per_device,
        mesh=mesh,
        in_specs=(
            P(("dp", "expert"), None),
            P(("dp", "expert"), None),
            P(("dp", "expert"), None),
            P(("dp", "expert"), None),
            P(("dp", "expert")),
            P(("dp", "expert"), None),
            P(("dp", "expert"), None),
            P(("dp", "expert"), None),
            P(),
            P(),
            P("expert", None, "dp"),
            P("expert", "dp"),
            P("expert", "dp", None),
            P(),
        ),
        out_specs=P(("dp", "expert"), None),
        check_vma=False,
    )
```

```python
import functools
import math

import jax
import jax.numpy as jnp
from jax import lax
from jax.experimental import pallas as pl
from jax.experimental.pallas import tpu as pltpu
from jax.sharding import PartitionSpec as P

HEAD_DIM = 128
ROUNDS = 4
LANES = 128

epsilon = 1e-05
mask_fill = -1e30

F32 = jnp.float32
BF16 = jnp.bfloat16

VMEM_BYTES = 32 * 1024 * 1024
PACK_BYTES = 62 * 1024 * 1024


def iota(shape, axis):
    return lax.broadcasted_iota(jnp.int32, shape, axis)


def one_hot(condition):
    return jnp.where(condition, 1.0, 0.0)


def across(row, rows):
    lanes = jnp.broadcast_to(row.astype(F32), (rows, row.shape[1]))
    return lanes, lanes.T


def call(body, out_shape, *operands, flops=0, vmem=VMEM_BYTES):
    moved = sum(x.size * x.dtype.itemsize for x in operands)
    moved += sum(x.size * x.dtype.itemsize for x in jax.tree.leaves(out_shape))
    return pl.pallas_call(
        body,
        out_shape=out_shape,
        compiler_params=pltpu.CompilerParams(vmem_limit_bytes=vmem),
        cost_estimate=pl.CostEstimate(flops=flops, bytes_accessed=moved, transcendentals=0),
    )(*operands)


def pack_kernel(pos_ref, *refs):
    parts = lax.axis_size("dp")
    *x_refs, order_ref = refs[: len(refs) - parts]
    out_refs = refs[len(refs) - parts :]
    tok = order_ref.shape[0]
    share = tok // parts

    def sort(x, at):
        rows = jnp.dot(order, x, preferred_element_type=F32).astype(BF16)
        for n, out_ref in enumerate(out_refs):
            out_ref[:, at : at + x.shape[1]] = rows[n * share : (n + 1) * share]

    if pos_ref.dtype == jnp.int32:
        pos = lax.rem(pos_ref[...] + (parts - lax.axis_index("dp")) * tok, parts * tok)
        lanes, subl = across(pos, tok)
        rank = jnp.sum(one_hot(subl < lanes), axis=0, keepdims=True)
        order = one_hot(iota((tok, tok), 0).astype(F32) == rank).astype(BF16)
        _, offset = across(lax.rem(pos, tok), tok)
        sort(offset.astype(BF16), sum(x.shape[1] for x in x_refs))
    else:
        order = pos_ref[...]
    order_ref[...] = order
    at = 0
    for x_ref in x_refs:
        sort(x_ref[...], at)
        at += x_ref.shape[1]


def joined(refs, columns=slice(None)):
    return jnp.concatenate([r[:, columns] for r in refs], axis=0)


def slots_of(ids, cap, experts):
    tok = ids.shape[1]
    first, first_t = across(ids[0:1, :], tok)
    second, second_t = across(ids[1:2, :], tok)
    earlier = iota((tok, tok), 0) < iota((tok, tok), 1)
    rank_first = jnp.sum(one_hot((first_t == first) & earlier), axis=0, keepdims=True)
    rank_second = jnp.sum(one_hot(first_t == second), axis=0, keepdims=True)
    rank_second += jnp.sum(one_hot((second_t == second) & earlier), axis=0, keepdims=True)

    def slot(expert, rank):
        return jnp.where((expert < experts) & (rank < cap), expert * cap + rank, -1.0)

    return slot(first[0:1, :], rank_first), slot(second[0:1, :], rank_second)


def slots_kernel(cap, experts, relative, seg_ref, ids_ref, code_ref, own_ref, own_later_ref, *refs):
    seg_q_ref, taken_ref, give_ref, kept_ref, kept_later_ref = refs
    kept_ref[...] = own_ref[...]
    kept_later_ref[...] = own_later_ref[...]
    tok = seg_ref.shape[1]
    _, seg_q_ref[...] = across(seg_ref[...], tok)
    ids = ids_ref[...]
    if relative:
        other = ids ^ lax.axis_index("expert")
        ids = jnp.where(ids < experts, (other & 1) * (experts // 2) + (other >> 1), ids)
    slot_first, slot_second = slots_of(ids, cap, experts)
    slot = iota((experts * cap, tok), 0).astype(F32)
    taken_ref[...] = one_hot((slot == slot_first) | (slot == slot_second)).astype(BF16)
    high = (code_ref[...] >> 8).astype(F32)
    low = (code_ref[...] & 255).astype(F32)

    def weights(code):
        return jnp.where(slot == slot_first, code[0:1, :], 0.0) + jnp.where(
            slot == slot_second, code[1:2, :], 0.0
        )

    both = jnp.concatenate([weights(high) / 256.0, weights(low) / 65536.0], axis=0)
    give_ref[...] = both.T.astype(BF16)


def place_kernel(first, seg_q_ref, *refs):
    *row_refs, place_ref, outside_ref = refs
    seg_q = seg_q_ref[...]
    offset = joined(row_refs, slice(first, first + LANES)).astype(F32).T
    place = offset == iota(offset.shape, 0).astype(F32)
    place_ref[...] = one_hot(place).astype(BF16)
    seg_k = jnp.sum(jnp.where(place, seg_q, 0.0), axis=0, keepdims=True)
    outside_ref[...] = one_hot(seg_q != seg_k)


def probs_kernel(place_ref, outside_ref, *refs):
    *row_refs, out_ref = refs
    width = out_ref.shape[0] * HEAD_DIM
    scale = 1.0 / math.sqrt(HEAD_DIM)
    outside = outside_ref[...] > 0.0
    for h in range(out_ref.shape[0]):
        lo = h * HEAD_DIM
        k = joined(row_refs, slice(lo, lo + HEAD_DIM))
        q = joined(row_refs, slice(width + lo, width + lo + HEAD_DIM))
        q = jnp.dot(place_ref[...], q, preferred_element_type=F32).astype(BF16)
        scores = lax.dot_general(q, k, (((1,), (1,)), ((), ())), preferred_element_type=F32)
        scores = jnp.where(outside, mask_fill, scores * scale)
        terms = jnp.exp(scores - jnp.max(scores, axis=1, keepdims=True))
        out_ref[h] = (terms / jnp.sum(terms, axis=1, keepdims=True)).astype(BF16)


def norm_kernel(parts, place_ref, taken_ref, gain_ref, bias_ref, probs_ref, *refs):
    row_refs, hidden_ref, send_refs = refs[: -parts - 1], refs[-parts - 1], refs[-parts:]
    width = hidden_ref.shape[1]
    for h in range(probs_ref.shape[0]):
        lo = h * HEAD_DIM
        values = joined(row_refs, slice(lo, lo + HEAD_DIM))
        states = joined(row_refs, slice(width + lo, width + lo + HEAD_DIM))
        hidden_ref[:, lo : lo + HEAD_DIM] = jnp.dot(
            probs_ref[h], values, preferred_element_type=F32
        ) + jnp.dot(place_ref[...], states, preferred_element_type=F32)
    hidden = hidden_ref[...]
    centered = hidden - jnp.mean(hidden, axis=1, keepdims=True)
    variance = jnp.mean(centered * centered, axis=1, keepdims=True)
    normed = (centered * lax.rsqrt(variance + epsilon) * gain_ref[...] + bias_ref[...]).astype(BF16)
    picked = jnp.dot(taken_ref[...], normed, preferred_element_type=F32).astype(BF16)
    at = 0
    for send_ref in send_refs:
        send_ref[...] = picked[at : at + send_ref.shape[0]]
        at += send_ref.shape[0]


def expert_kernel(count, bias_ref, w_in_ref, w_out_ref, *refs):
    x_refs, out_refs = refs[:count], refs[-count:]
    inner = jnp.dot(joined(x_refs), w_in_ref[0], preferred_element_type=F32)
    inner = jnp.maximum(inner + bias_ref[...], 0.0).astype(BF16)
    share = jnp.dot(inner, w_out_ref[0], preferred_element_type=F32).astype(BF16)
    at = 0
    for out_ref in out_refs:
        out_ref[...] = share[at : at + out_ref.shape[0]]
        at += out_ref.shape[0]


def add_kernel(first_ref, second_ref, out_ref):
    out_ref[...] = (first_ref[...].astype(F32) + second_ref[...].astype(F32)).astype(BF16)


def result_kernel(lower, bias_ref, near_ref, *refs):
    count = refs[0].shape[0]
    outs = next(n for n in range(1, len(refs)) if sum(r.shape[0] for r in refs[-n:]) == count)
    total = near_ref[lower : lower + count].astype(F32)
    for share_ref in refs[:-outs]:
        total += share_ref[...].astype(F32)
    row = lax.axis_index("expert") == iota(bias_ref.shape, 0)
    bias = jnp.sum(jnp.where(row, bias_ref[...], 0.0), axis=0, keepdims=True)
    result = (total + bias).astype(BF16)
    at = 0
    for out_ref in refs[-outs:]:
        out_ref[...] = result[at : at + out_ref.shape[0]]
        at += out_ref.shape[0]


def join_kernel(*refs):
    refs[-1][...] = joined(refs[:-1])


def pair_kernel(cap, mine_ref, other_ref, *piece_refs):
    mine, other = mine_ref[...].astype(F32), other_ref[...].astype(F32)
    for n, piece_ref in enumerate(piece_refs):
        rows = slice(n * cap, (n + 1) * cap)
        piece_ref[...] = jnp.concatenate([mine[rows], other[rows]], axis=0).astype(BF16)


def part_kernel(cap, *refs):
    *piece_refs, mine_ref, other_ref = refs
    pieces = [piece_ref[...].astype(F32) for piece_ref in piece_refs]
    mine_ref[...] = jnp.concatenate([piece[:cap] for piece in pieces], axis=0).astype(BF16)
    other_ref[...] = jnp.concatenate([piece[cap:] for piece in pieces], axis=0).astype(BF16)


def combine_kernel(hidden_ref, give_ref, *refs):
    *result_refs, out_ref = refs
    result = joined(list(result_refs) * 2)
    added = jnp.dot(give_ref[...], result, preferred_element_type=F32)
    out_ref[...] = (hidden_ref[...] + added).astype(BF16)


def per_device(
    pivot_states,
    queries,
    keys,
    values,
    pack_pos,
    segment_ids,
    expert_ids,
    gate_code,
    ln_gain,
    ln_bias,
    w_in,
    b_in,
    w_out,
    b_out,
):
    tok, width = pivot_states.shape
    dp = lax.axis_size("dp")
    experts = lax.axis_size("expert")
    cap = max(2, 2 * tok // (ROUNDS * experts))
    slots = experts * cap
    relative = dp == 4 and experts == 8
    heads = width // HEAD_DIM
    def pack(guide, *arrays):
        wide = len(arrays) * width + (LANES if guide.dtype == jnp.int32 else 0)
        return call(
            pack_kernel,
            (jax.ShapeDtypeStruct((tok, tok), BF16),) + (jax.ShapeDtypeStruct((tok // dp, wide), BF16),) * dp,
            guide,
            *arrays,
            vmem=PACK_BYTES,
        )

    def spread(parts):
        return [
            lax.ppermute(part, "dp", [(i, (i + n) % dp) for i in range(dp)]) if n else part
            for n, part in enumerate(parts)
        ]

    order, *packed = pack(pack_pos.reshape(1, tok), keys, queries)
    _, *packed_later = pack(order, values, pivot_states)
    seg_q, taken, give, kept, kept_later = call(
        functools.partial(slots_kernel, cap, experts, relative),
        (
            jax.ShapeDtypeStruct((tok, tok), F32),
            jax.ShapeDtypeStruct((slots, tok), BF16),
            jax.ShapeDtypeStruct((tok, 2 * slots), BF16),
            jax.ShapeDtypeStruct(packed[0].shape, BF16),
            jax.ShapeDtypeStruct(packed_later[0].shape, BF16),
        ),
        segment_ids,
        expert_ids.T,
        gate_code.T,
        packed[0],
        packed_later[0],
    )
    rows = [kept] + spread(packed)[1:]
    later = [kept_later] + spread(packed_later)[1:]
    place, outside = call(
        functools.partial(place_kernel, 2 * width),
        (jax.ShapeDtypeStruct((tok, tok), BF16), jax.ShapeDtypeStruct((tok, tok), F32)),
        seg_q,
        *rows,
    )
    probs = call(
        probs_kernel,
        jax.ShapeDtypeStruct((heads, tok, tok), BF16),
        place,
        outside,
        *rows,
    )
    parts = 2 if relative else 1
    hidden_state, *send = call(
        functools.partial(norm_kernel, parts),
        (jax.ShapeDtypeStruct((tok, width), F32),)
        + (jax.ShapeDtypeStruct((slots // parts, width), BF16),) * parts,
        place,
        taken,
        ln_gain.reshape(1, width),
        ln_bias.reshape(1, width),
        probs,
        *later,
    )

    def over_experts(x):
        x = x.reshape(experts, cap, width)
        return lax.all_to_all(x, "expert", split_axis=0, concat_axis=0, tiled=True).reshape(slots, width)

    def bf16(rows):
        return jax.ShapeDtypeStruct((rows, width), BF16)

    def apply(rows, after=()):
        count = sum(x.shape[0] for x in rows)
        return call(
            functools.partial(expert_kernel, len(rows)),
            tuple(bf16(x.shape[0]) for x in rows),
            b_in,
            w_in,
            w_out,
            *rows,
            *after,
            flops=4 * count * width * w_in.shape[2],
        )

    def swap(x, distance, axis="dp"):
        return lax.ppermute(x, axis, [(i, i ^ distance) for i in range(lax.axis_size(axis))])

    if relative:
        half = slots // 2
        pieces = call(
            functools.partial(pair_kernel, cap), (bf16(2 * cap),) * 4, send[0], swap(send[1], 1, "expert")
        )
        pieces = [swap(x, 2 * n, "expert") if n else x for n, x in enumerate(pieces)]
        own = [call(join_kernel, bf16(half), *pieces[n : n + 2]) for n in (2, 0)]
        far = [swap(x, 2) for x in own]
        near = [swap(x, 1) for x in own]
        own_share, near_shares, last = [None, None], [None, None], ()
        for n in (1, 0):
            own_share[n], near_shares[n] = apply([own[n], near[n]], after=last)
            last = own_share[n : n + 1]
        last = last[0]
        *corner_share, far_first, far_second = apply([swap(x, 1) for x in far] + far, after=[last])
        far_shares = [far_first, far_second]
        near_shares = [swap(x, 1) for x in near_shares]
        backs = [None, None]
        for n in (1, 0):
            pair = swap(call(add_kernel, bf16(half), swap(corner_share[n], 1), far_shares[n]), 2)
            backs[n] = call(
                functools.partial(result_kernel, 0),
                (bf16(2 * cap),) * 2,
                b_out,
                near_shares[n],
                own_share[n],
                pair,
            )
        pieces = [x for n in (1, 0) for x in backs[n]]
        pieces = [swap(x, 2 * n, "expert") if n else x for n, x in enumerate(pieces)]
        mine, other = call(functools.partial(part_kernel, cap), (bf16(half),) * 2, *pieces)
        returned = [mine, swap(other, 1, "expert")]
    else:
        every = lax.all_gather(over_experts(send[0]), "dp", axis=0, tiled=True)
        (share,) = apply([every])
        shares = lax.all_to_all(
            share.reshape(dp, slots, width), "dp", split_axis=0, concat_axis=0, tiled=True
        )
        (results,) = call(
            functools.partial(result_kernel, 0), (bf16(slots),), b_out, *[shares[n] for n in range(dp)]
        )
        returned = [over_experts(results)]
    return call(
        combine_kernel, jax.ShapeDtypeStruct((tok, width), BF16), hidden_state, give, *returned
    )


def solution(mesh):
    return jax.shard_map(
        per_device,
        mesh=mesh,
        in_specs=(
            P(("dp", "expert"), None),
            P(("dp", "expert"), None),
            P(("dp", "expert"), None),
            P(("dp", "expert"), None),
            P(("dp", "expert")),
            P(("dp", "expert"), None),
            P(("dp", "expert"), None),
            P(("dp", "expert"), None),
            P(),
            P(),
            P("expert", None, "dp"),
            P("expert", "dp"),
            P("expert", "dp", None),
            P(),
        ),
        out_specs=P(("dp", "expert"), None),
        check_vma=False,
    )
```
